32 devices in a mesh: head: 4 (over y, x), tok: 8 (over z, core).
Axes of the slice: x: 2, y: 2, z: 4, core: 2. Of those that a mesh axis runs over, the one named last changes fastest.
Arguments:
- tokens: bfloat16 [4096, 8192], P('tok', 'head'), may hold values from -20 to 20
- qkv_maps: bfloat16 [16, 512, 1536], P('head'), may hold values from -0.26516504 to 0.26516504
- rate_map: bfloat16 [8192, 16], P('head'), may hold values from -0.09375 to 0.09375
- fast_init: bfloat16 [16, 3, 512, 512], P('head'), may hold values from -0.25 to 0.25
Outputs:
- layer_out: bfloat16 [4096, 8192], P('tok', 'head')
The draws below stay inside these ranges and needn't reach their ends.
All inputs are finite; a program needn't handle non-finite values.
Results may differ from the reference program's by a relative error of at most 0.04.
Values may be sent and summed in bfloat16 or wider, within the bound.
No kernel may reach another device: no remote copies, remote signals or barrier semaphores. Data moves between devices by JAX's collectives and lax.ppermute only.
A program may use at most 128 MiB of HBM per device.

```python
import jax
import jax.numpy as jnp
from jax import lax

H = 16
HD = 512
WINDOW = 512
TOK_DEV = 512
D = 8192
TOKENS = 4096
STRETCH = 2048
PIECE = 64
N_TOK = 8


def draw_tokens(key, part):
    keys = jax.random.split(jax.random.fold_in(key, 17), 1)
    return jnp.clip(jax.random.normal(keys[0], (TOKENS, D), jnp.float32), -6.0, 6.0).astype(jnp.bfloat16)


def draw_qkv_maps(key, part):
    keys = jax.random.split(jax.random.fold_in(key, 29), 3)
    shape = (H, HD, HD)
    factor = HD ** (-0.5)
    query_map = jnp.clip(jax.random.normal(keys[0], shape, jnp.float32), -5.0, 5.0) * factor
    own_key = jnp.clip(jax.random.normal(keys[1], shape, jnp.float32), -5.0, 5.0) * factor
    value_map = jnp.clip(jax.random.normal(keys[2], shape, jnp.float32), -5.0, 5.0) * factor
    key_map = own_key
    return jnp.concatenate([query_map, key_map, value_map], 2).astype(jnp.bfloat16)


def spiked(drawn, key, source, target, blocks, factor):
    def block_of(dim):
        return (jnp.arange(drawn.shape[dim]) // (drawn.shape[dim] // blocks)).reshape((-1,) + (1,) * (drawn.ndim - 1 - dim))

    near = jax.random.permutation(key, blocks)[block_of(target)]
    second = (block_of(target) + blocks // 2) % blocks
    return jnp.where((block_of(source) == near) | (block_of(source) == second), factor * drawn, drawn)


def levels(key, extent, cuts, smallest, largest):
    def one(axis_at, shards_of):
        heights = jax.random.uniform(jax.random.fold_in(jax.random.fold_in(key, 6), axis_at), (shards_of,), jnp.float32, smallest / len(cuts), largest / len(cuts))
        return jnp.repeat(jnp.exp(heights), extent[axis_at] // shards_of).reshape((-1,) + (1,) * (len(extent) - axis_at - 1))

    factor_of = one(*cuts[0])
    for cut in cuts[1:]:
        factor_of = factor_of * one(*cut)
    return factor_of


def scatter_about(key, extent, deviation, limit, shards=(), kind=jnp.bfloat16):
    entries = jax.random.normal(key, extent, jnp.float32) * deviation
    if len(shards) > 0:
        entries = levels(key, extent, shards, -0.22, 0.18) * entries
    return jnp.clip(entries, min=-limit, max=limit).astype(kind)


def gaussian_with(rng, extent, width, bound, shards, heavy, held_as=jnp.bfloat16):
    values = width * jax.random.normal(rng, extent, jnp.float32)
    if shards:
        values = values * levels(rng, extent, shards, -0.22, 0.18)
    return jnp.clip(spiked(values, jax.random.fold_in(rng, 3), *heavy), -bound, bound).astype(held_as)


def setup_inputs(seed: int = 0) -> dict:
    splits = jax.random.split(jax.random.key(seed), 5)
    tokens = draw_tokens(jax.random.fold_in(splits[4], 71), 0)
    qkv_maps = draw_qkv_maps(jax.random.fold_in(splits[4], 71), 0)
    rate_map = gaussian_with(splits[2], (D, H), D ** -0.5, 0.09375, ((0, 4),), (0, 1, 4, 2.0))
    fast_init = scatter_about(splits[3], (H, 3, HD, HD), HD ** -0.5, 0.25, ((0, 4),))
    return dict(tokens=tokens, qkv_maps=qkv_maps, rate_map=rate_map, fast_init=fast_init)


rate_base = 0.003
epsilon = 1e-06

def rms_rows(matrix):
    matrix = matrix.astype(jnp.float32)
    return matrix / jnp.sqrt(lax.optimization_barrier(jnp.mean(matrix * matrix, axis=-1, keepdims=True)) + epsilon)

def renorm(updated, initial):
    target = jnp.sqrt(lax.optimization_barrier(jnp.mean(initial * initial, axis=-1, keepdims=True)) + epsilon)
    current = jnp.sqrt(lax.optimization_barrier(jnp.mean(updated * updated, axis=-1, keepdims=True)) + epsilon)
    return (updated * (target / current)).astype(jnp.bfloat16)

def settle(array):
    return lax.optimization_barrier(array.astype(jnp.bfloat16)).astype(jnp.float32)

def band_attention(queries, key_rows, value_rows):
    zeros = jnp.zeros((WINDOW, HD), jnp.bfloat16)
    padded_keys = jnp.concatenate([zeros, key_rows], 0)
    padded_values = jnp.concatenate([zeros, value_rows], 0)
    score_scale = HD ** (-0.5)

    def one_span(span_index):
        start = span_index * TOK_DEV
        query_span = lax.dynamic_slice_in_dim(queries, start, TOK_DEV, 0)
        key_span = lax.dynamic_slice_in_dim(padded_keys, start, TOK_DEV + WINDOW, 0)
        value_span = lax.dynamic_slice_in_dim(padded_values, start, TOK_DEV + WINDOW, 0)
        scores = jnp.dot(query_span, key_span.T, preferred_element_type=jnp.float32) * score_scale
        query_pos = start + jnp.arange(TOK_DEV, dtype=jnp.int32)
        key_pos = start - WINDOW + jnp.arange(TOK_DEV + WINDOW, dtype=jnp.int32)
        key_mask = (key_pos[None, :] <= query_pos[:, None]) & (key_pos[None, :] > query_pos[:, None] - WINDOW) & (key_pos[None, :] >= 0)
        row_max = lax.optimization_barrier(jnp.max(jnp.where(key_mask, scores, -1e+30), axis=1, keepdims=True))
        raised = jnp.where(key_mask, jnp.exp(scores - row_max), 0.0)
        probs = (raised / lax.optimization_barrier(jnp.sum(raised, axis=1, keepdims=True))).astype(jnp.bfloat16)
        return jnp.dot(probs, value_span, preferred_element_type=jnp.float32)
    spans = lax.map(one_span, jnp.arange(TOKENS // TOK_DEV, dtype=jnp.int32))
    return spans.reshape(TOKENS, HD)

def regroup(array):
    shaped = array.reshape((N_TOK // 2, N_TOK, PIECE) + array.shape[1:])
    shaped = jnp.swapaxes(shaped, 0, 1)
    return shaped.reshape((N_TOK, N_TOK // 2 * PIECE) + array.shape[1:])

def fast_head(q_norm, k_norm, value_rows, rate_row, fast_weights):
    initial = fast_weights.astype(jnp.float32)
    weights = fast_weights
    outputs = []
    for half_index in range(2):
        first = half_index * STRETCH
        key_groups = regroup(k_norm[first:first + STRETCH]).astype(jnp.float32)
        value_groups = regroup(value_rows[first:first + STRETCH]).astype(jnp.float32)
        rate_groups = regroup(rate_row[first:first + STRETCH]).astype(jnp.float32)
        current = weights.astype(jnp.float32)
        pre_gate = jnp.einsum('jrd,de->jre', key_groups, current[0])
        pre_up = jnp.einsum('jrd,de->jre', key_groups, current[1])
        sigma = jax.nn.sigmoid(pre_gate)
        gated = pre_gate * sigma
        hidden = settle(gated * pre_up)
        target = settle(rate_groups[:, :, None] * value_groups)
        grad_down = jnp.einsum('jre,jrd->jed', hidden, target)
        back_hidden = jnp.einsum('jrd,ed->jre', target, current[2])
        gate_delta = settle(back_hidden * pre_up * sigma * (1.0 + pre_gate * (1.0 - sigma)))
        up_delta = settle(back_hidden * gated)
        grad_gate = jnp.einsum('jrd,jre->jde', key_groups, gate_delta)
        grad_up = jnp.einsum('jrd,jre->jde', key_groups, up_delta)
        partials = settle(jnp.stack([grad_gate, grad_up, grad_down], 1))
        weights = renorm(current + lax.optimization_barrier(jnp.sum(partials, 0)), initial)
        query_rows = q_norm[first:first + STRETCH]
        app_gate = jnp.dot(query_rows, weights[0], preferred_element_type=jnp.float32)
        app_up = jnp.dot(query_rows, weights[1], preferred_element_type=jnp.float32)
        app_hidden = (app_gate * jax.nn.sigmoid(app_gate) * app_up).astype(jnp.bfloat16)
        outputs.append(jnp.dot(app_hidden, weights[2], preferred_element_type=jnp.float32).astype(jnp.bfloat16))
    return jnp.concatenate(outputs, 0)

def reference(tokens, qkv_maps, rate_map, fast_init):
    logits = jnp.dot(tokens, rate_map, preferred_element_type=jnp.float32)
    rate = (rate_base * jax.nn.softplus(logits)).astype(jnp.bfloat16)
    head_inputs = jnp.swapaxes(tokens.reshape(TOKENS, H, HD), 0, 1)

    def per_head(items):
        inputs, maps, rate_row, fast_weights = items
        projected = jnp.dot(inputs, maps, preferred_element_type=jnp.float32)
        queries = projected[:, :HD].astype(jnp.bfloat16)
        key_rows = projected[:, HD:2 * HD].astype(jnp.bfloat16)
        value_rows = projected[:, 2 * HD:].astype(jnp.bfloat16)
        attended = band_attention(queries, key_rows, value_rows)
        q_norm = rms_rows(queries).astype(jnp.bfloat16)
        k_norm = rms_rows(key_rows).astype(jnp.bfloat16)
        fast = fast_head(q_norm, k_norm, value_rows, rate_row, fast_weights)
        return (attended + fast.astype(jnp.float32)).astype(jnp.bfloat16)
    result = lax.map(per_head, (head_inputs, qkv_maps, rate.T, fast_init))
    return jnp.swapaxes(result, 0, 1).reshape(TOKENS, D)
```

```python
import functools

import jax
import jax.numpy as jnp
from jax import lax
from jax.experimental import pallas as pl
from jax.experimental.pallas import tpu as pltpu
from jax.sharding import PartitionSpec as P

WINDOW = 512


rate_base = 0.003
epsilon = 1e-06
VMEM_LIMIT = 48 * 1024 * 1024


def from_behind(block, axis, distance):
    devices = range(lax.axis_size(axis))
    route = [(i - distance, i) for i in devices if i - distance in devices]
    return lax.ppermute(block, axis, route)


def rms_rows(matrix):
    matrix = matrix.astype(jnp.float32)
    return matrix / jnp.sqrt(jnp.mean(matrix * matrix, axis=-1, keepdims=True) + epsilon)


def renorm(updated, initial):
    target = jnp.sqrt(jnp.mean(initial * initial, axis=-1, keepdims=True) + epsilon)
    current = jnp.sqrt(jnp.mean(updated * updated, axis=-1, keepdims=True) + epsilon)
    return (updated * (target / current)).astype(jnp.bfloat16)


def band_attention(queries, key_rows, value_rows, query_pos, key_pos, score_scale):
    scores = (
        jnp.einsum("qhd,khd->hqk", queries, key_rows, preferred_element_type=jnp.float32)
        * score_scale
    )
    key_mask = (
        (key_pos[None, :] <= query_pos[:, None])
        & (key_pos[None, :] > query_pos[:, None] - WINDOW)
        & (key_pos[None, :] >= 0)
    )
    key_mask = key_mask[None]
    row_max = jnp.max(jnp.where(key_mask, scores, -1e30), axis=2, keepdims=True)
    raised = jnp.where(key_mask, jnp.exp(scores - row_max), 0.0)
    probs = (raised / jnp.sum(raised, axis=2, keepdims=True)).astype(jnp.bfloat16)
    return jnp.einsum("hqk,khd->qhd", probs, value_rows, preferred_element_type=jnp.float32)


def fast_gradient(weights, key_part, value_part, rate_part):
    pre_gate = jnp.einsum(
        "rhd,hde->rhe", key_part, weights[:, 0], preferred_element_type=jnp.float32
    )
    pre_up = jnp.einsum("rhd,hde->rhe", key_part, weights[:, 1], preferred_element_type=jnp.float32)
    sigma = jax.nn.sigmoid(pre_gate)
    gated = pre_gate * sigma
    hidden = (gated * pre_up).astype(jnp.bfloat16)
    target = (rate_part.astype(jnp.float32)[:, :, None] * value_part.astype(jnp.float32)).astype(
        jnp.bfloat16
    )
    grad_down = jnp.einsum("rhe,rhd->hed", hidden, target, preferred_element_type=jnp.float32)
    back_hidden = jnp.einsum(
        "rhd,hed->rhe", target, weights[:, 2], preferred_element_type=jnp.float32
    )
    gate_delta = (back_hidden * pre_up * sigma * (1.0 + pre_gate * (1.0 - sigma))).astype(
        jnp.bfloat16
    )
    up_delta = (back_hidden * gated).astype(jnp.bfloat16)
    grad_gate = jnp.einsum("rhd,rhe->hde", key_part, gate_delta, preferred_element_type=jnp.float32)
    grad_up = jnp.einsum("rhd,rhe->hde", key_part, up_delta, preferred_element_type=jnp.float32)
    return jnp.stack([grad_gate, grad_up, grad_down], 1)


def fast_apply(weights, query_part):
    app_gate = jnp.einsum(
        "rhd,hde->rhe", query_part, weights[:, 0], preferred_element_type=jnp.float32
    )
    app_up = jnp.einsum(
        "rhd,hde->rhe", query_part, weights[:, 1], preferred_element_type=jnp.float32
    )
    app_hidden = (app_gate * jax.nn.sigmoid(app_gate) * app_up).astype(jnp.bfloat16)
    result = jnp.einsum(
        "rhe,hed->rhd", app_hidden, weights[:, 2], preferred_element_type=jnp.float32
    )
    return result.astype(jnp.bfloat16)


def update_weights(weights, partial_value, initial):
    total = lax.psum(partial_value.astype(jnp.bfloat16), "tok").astype(jnp.float32)
    return renorm(weights.astype(jnp.float32) + total, initial)


def general_body(tokens, qkv_maps, rate_map, fast_init):
    tok_rows = tokens.shape[0]
    head_count = qkv_maps.shape[0]
    head_width = qkv_maps.shape[1]
    groups = lax.axis_size("tok")
    logit_terms = jnp.dot(tokens, rate_map, preferred_element_type=jnp.float32)
    logits = lax.psum_scatter(
        logit_terms.astype(jnp.bfloat16), "head", scatter_dimension=1, tiled=True
    ).astype(jnp.float32)
    rate = (rate_base * jax.nn.softplus(logits)).astype(jnp.bfloat16)
    inputs = tokens.reshape(tok_rows, head_count, head_width)
    projected = jnp.einsum("rhd,hde->rhe", inputs, qkv_maps, preferred_element_type=jnp.float32)
    queries = projected[:, :, :head_width].astype(jnp.bfloat16)
    key_rows = projected[:, :, head_width : 2 * head_width].astype(jnp.bfloat16)
    value_rows = projected[:, :, 2 * head_width :].astype(jnp.bfloat16)
    tail_rows = min(WINDOW, tok_rows)
    edge = jnp.stack([key_rows, value_rows], 0)
    distance = 0
    received = [from_behind(edge, "tok", distance + 1)]
    anchor = lax.axis_index("tok") * tok_rows
    offsets = jnp.arange(tail_rows, dtype=jnp.int32)
    distance = 1
    arrived = received[distance - 1]
    key_parts = [arrived[0]]
    value_parts = [arrived[1]]
    position_parts = [anchor - distance * tok_rows + tok_rows - tail_rows + offsets]
    local_pos = anchor + jnp.arange(tok_rows, dtype=jnp.int32)
    all_keys = jnp.concatenate(key_parts + [key_rows], 0)
    all_values = jnp.concatenate(value_parts + [value_rows], 0)
    all_pos = jnp.concatenate(position_parts + [local_pos], 0)
    attended = band_attention(
        queries, all_keys, all_values, local_pos, all_pos, head_width ** (-0.5)
    )
    q_norm = rms_rows(queries).astype(jnp.bfloat16)
    k_norm = rms_rows(key_rows).astype(jnp.bfloat16)
    initial = fast_init.astype(jnp.float32)
    weights = fast_init
    own_block = lax.axis_index("tok") // (groups // 2)
    fast_out = jnp.zeros_like(q_norm)
    for half_index in range(2):
        partial_value = fast_gradient(weights, k_norm, value_rows, rate)
        partial_value = jnp.where(own_block == half_index, partial_value, 0.0)
        weights = update_weights(weights, partial_value, initial)
        applied = fast_apply(weights, q_norm)
        fast_out = jnp.where(own_block == half_index, applied, fast_out)
    combined = (attended + fast_out.astype(jnp.float32)).astype(jnp.bfloat16)
    return combined.reshape(tok_rows, head_count * head_width)


def matmul(left, right):
    return jnp.dot(left, right, preferred_element_type=jnp.float32)


def matmul_nt(left, right):
    return lax.dot_general(left, right, (((1,), (1,)), ((), ())), preferred_element_type=jnp.float32)


def matmul_tn(left, right):
    return lax.dot_general(left, right, (((0,), (0,)), ((), ())), preferred_element_type=jnp.float32)


def unit_rows(rows):
    rows = rows.astype(jnp.float32)
    scale = lax.rsqrt(jnp.mean(rows * rows, axis=-1, keepdims=True) + epsilon)
    return (rows * scale).astype(jnp.bfloat16)


def logistic(a):
    return 0.5 * jnp.tanh(0.5 * a) + 0.5


def project_kernel(width, table, x0, x1, x2, x3, maps, q_out, k_out, v_out):
    step = pl.program_id(0)

    def block(x_ref, own):
        x = x_ref[...]
        if own:
            q_out[0] = matmul(x, maps[0, :, :width]).astype(jnp.bfloat16)
        k_out[0] = matmul(x, maps[0, :, width : 2 * width]).astype(jnp.bfloat16)
        v_out[0] = matmul(x, maps[0, :, 2 * width :]).astype(jnp.bfloat16)

    for at, x_ref in enumerate((x0, x1, x2, x3)):
        pl.when(step == at)(functools.partial(block, x_ref, at % 2 == 0))


def project(table, blocks, maps):
    rows, width = blocks[0].shape
    count = len(blocks)
    whole = pl.BlockSpec((rows, width), lambda i, t: (0, 0))
    out = functools.partial(pl.BlockSpec, (1, rows, width))
    return pl.pallas_call(
        functools.partial(project_kernel, width),
        grid_spec=pltpu.PrefetchScalarGridSpec(
            num_scalar_prefetch=1,
            grid=(count,),
            in_specs=[whole] * count + [pl.BlockSpec((1, width, 3 * width), lambda i, t: (t[0], 0, 0))],
            out_specs=[
                out(lambda i, t: (i // 2, 0, 0)),
                out(lambda i, t: (i, 0, 0)),
                out(lambda i, t: (i, 0, 0)),
            ],
        ),
        out_shape=[
            jax.ShapeDtypeStruct((count // 2, rows, width), jnp.bfloat16),
            jax.ShapeDtypeStruct((count, rows, width), jnp.bfloat16),
            jax.ShapeDtypeStruct((count, rows, width), jnp.bfloat16),
        ],
        compiler_params=pltpu.CompilerParams(vmem_limit_bytes=VMEM_LIMIT),
        name="project",
    )(table, *blocks, maps)


def attend_kernel(slots, table, q, k_now, v_now, k_near, v_near, k_far, v_far, out):
    step = pl.program_id(0)
    rows, width = q.shape[1:]
    part = rows // 2
    place = table[1 + step]
    is_far = place >= slots
    bound = jnp.where(table[1 + slots + step] > 0, 0, rows)
    row = lax.broadcasted_iota(jnp.int32, (part, rows + part), 0)
    column = lax.broadcasted_iota(jnp.int32, (part, rows + part), 1)

    def block(k_before, v_before):
        for at in range(2):
            first = at * part
            queries = q[0, first : first + part]
            keys = jnp.concatenate([k_before[0, first:], k_now[0, : first + part]], 0)
            values = jnp.concatenate([v_before[0, first:], v_now[0, : first + part]], 0)
            scores = matmul_nt(queries, keys) * (width ** -0.5)
            mask = (column > row) & (column <= row + rows) & (column >= bound - first)
            scores = jnp.where(mask, scores, -1e30)
            raised = jnp.exp(scores - jnp.max(scores, axis=1, keepdims=True))
            total = jnp.sum(raised, axis=1, keepdims=True)
            out[0, first : first + part] = matmul(raised.astype(jnp.bfloat16), values) / total

    pl.when(jnp.logical_not(is_far))(lambda: block(k_near, v_near))
    pl.when(is_far)(lambda: block(k_far, v_far))


def attend(table, q, k_now, v_now, k_near, v_near, k_far, v_far):
    slots, rows, width = q.shape
    block = functools.partial(pl.BlockSpec, (1, rows, width))
    now = block(lambda i, t: (2 * i, 0, 0))
    near = block(lambda i, t: (2 * jnp.minimum(t[1 + i], slots - 1) + 1, 0, 0))
    far = block(lambda i, t: (2 * jnp.maximum(t[1 + i] - slots, 0) + 1, 0, 0))
    each = block(lambda i, t: (i, 0, 0))
    return pl.pallas_call(
        functools.partial(attend_kernel, slots),
        grid_spec=pltpu.PrefetchScalarGridSpec(
            num_scalar_prefetch=1,
            grid=(slots,),
            in_specs=[each, now, now, near, near, far, far],
            out_specs=each,
        ),
        out_shape=jax.ShapeDtypeStruct((slots, rows, width), jnp.float32),
        compiler_params=pltpu.CompilerParams(vmem_limit_bytes=VMEM_LIMIT),
        name="attend",
    )(table, q, k_now, v_now, k_near, v_near, k_far, v_far)


def fast_kernel(count, table, k, v, rate, weights, initial, q, attended, out, new, grads):
    step = pl.program_id(0)
    active = table[1] > 0
    width = k.shape[2]

    @pl.when(active & (step == 0))
    def _():
        grads[...] = jnp.zeros_like(grads)

    @pl.when(active & (step < count))
    def _():
        keys = unit_rows(k[0])
        spread = jnp.concatenate([rate[0]] * (width // rate.shape[2]), 1).astype(jnp.float32)
        target = (spread * v[0].astype(jnp.float32)).astype(jnp.bfloat16)
        gate = matmul(keys, weights[0, 0])
        up = matmul(keys, weights[0, 1])
        back = matmul_nt(target, weights[0, 2])
        sigma = logistic(gate)
        gated = gate * sigma
        hidden = (gated * up).astype(jnp.bfloat16)
        gate_delta = (back * up * sigma * (1.0 + gate * (1.0 - sigma))).astype(jnp.bfloat16)
        up_delta = (back * gated).astype(jnp.bfloat16)
        grads[0] += matmul_tn(keys, gate_delta)
        grads[1] += matmul_tn(keys, up_delta)
        grads[2] += matmul_tn(hidden, target)

    @pl.when(active & (step == count - 1))
    def _():
        for at in range(3):
            start = initial[0, at].astype(jnp.float32)
            updated = weights[0, at].astype(jnp.float32) + grads[at]
            wanted = jnp.mean(start * start, axis=-1, keepdims=True) + epsilon
            held = jnp.mean(updated * updated, axis=-1, keepdims=True) + epsilon
            new[0, at] = (updated * (jnp.sqrt(wanted) / jnp.sqrt(held))).astype(jnp.bfloat16)

    @pl.when(jnp.logical_not(active) & (step == 0))
    def _():
        new[...] = weights[...]

    @pl.when(active & (step >= count))
    def _():
        queries = unit_rows(q[0])
        gate = matmul(queries, new[0, 0])
        hidden = (gate * logistic(gate) * matmul(queries, new[0, 1])).astype(jnp.bfloat16)
        fast = matmul(hidden, new[0, 2]).astype(jnp.bfloat16).astype(jnp.float32)
        out[0] = (attended[0] + fast).astype(jnp.bfloat16)


def fast_stretch(table, k, v, rate, weights, initial, q, attended):
    count, rows, width = k.shape
    own = q.shape[0]
    held = weights.shape[0] - 1
    block = functools.partial(pl.BlockSpec, (1, rows, width))
    token = block(lambda i, t: (jnp.minimum(i, count - 1), 0, 0))
    query = block(lambda i, t: (jnp.maximum(i - count, 0), 0, 0))
    matrices = functools.partial(pl.BlockSpec, (1,) + weights.shape[1:])
    return pl.pallas_call(
        functools.partial(fast_kernel, count),
        grid_spec=pltpu.PrefetchScalarGridSpec(
            num_scalar_prefetch=1,
            grid=(count + own,),
            in_specs=[
                token,
                token,
                pl.BlockSpec((1,) + rate.shape[1:], lambda i, t: (t[2 + jnp.minimum(i, count - 1)], 0, 0)),
                matrices(lambda i, t: (jnp.minimum(t[0], held), 0, 0, 0)),
                matrices(lambda i, t: (t[0], 0, 0, 0)),
                query,
                query,
            ],
            out_specs=[query, matrices(lambda i, t: (0, 0, 0, 0))],
            scratch_shapes=[pltpu.VMEM(weights.shape[1:], jnp.float32)],
        ),
        out_shape=[
            jax.ShapeDtypeStruct((own, rows, width), jnp.bfloat16),
            jax.ShapeDtypeStruct((1,) + weights.shape[1:], jnp.bfloat16),
        ],
        compiler_params=pltpu.CompilerParams(vmem_limit_bytes=VMEM_LIMIT),
        name="fast_stretch",
    )(table, k, v, rate, weights, initial, q, attended)


def head_body(tokens, qkv_maps, rate_map, fast_init):
    rows = tokens.shape[0]
    heads, width = qkv_maps.shape[:2]
    groups = lax.axis_size("tok")
    chips = groups // 2
    slots = chips // 2
    me = lax.axis_index("tok")
    chip, core = me // 2, me % 2

    def swap(block, bits):
        return lax.ppermute(block, "tok", [(i, i ^ bits) for i in range(groups)])

    def piece(slot):
        return lax.dynamic_slice_in_dim(tokens, (chip ^ slot) * width, width, 1)

    pieces = [piece(slot) for slot in range(chips)]
    same = [pieces[0]] + [swap(pieces[slot], 2 * slot) for slot in range(1, chips)]
    other = [swap(block, 1) for block in same]

    terms = lax.dot_general(
        rate_map, tokens, (((0,), (1,)), ((), ())), preferred_element_type=jnp.float32
    )
    terms = lax.all_to_all(terms.reshape(-1, heads, rows), "head", 0, 0)
    rate = (rate_base * jax.nn.softplus(jnp.sum(terms, 0))).astype(jnp.bfloat16)
    rate = lax.all_to_all(jnp.repeat(rate, 2, axis=0), "tok", 0, 0, tiled=True)
    rate = jnp.broadcast_to(rate[:, :, None], (groups, rows, 128))

    def mixed(first):
        return [part for slot in range(first, first + slots) for part in (same[slot], other[slot])]

    head = jnp.asarray(chip, jnp.int32)
    q_near, k_near, v_near = project(head[None], mixed(0), qkv_maps)
    q_far, k_far, v_far = project(head[None], mixed(slots), qkv_maps)

    def attend_table(first):
        at = chip ^ jnp.arange(first, first + slots, dtype=jnp.int32)
        before = jnp.where(core == 1, at, at - 1)
        there = (before >= 0).astype(jnp.int32)
        return jnp.concatenate([head[None], chip ^ jnp.maximum(before, 0), there])

    attended_near = attend(
        attend_table(0), q_near, k_near, v_near, k_near, v_near, k_far, v_far
    )
    attended_far = attend(
        attend_table(slots), q_far, k_far, v_far, k_near, v_near, k_far, v_far
    )

    def fast_table(first, active):
        at = chip ^ jnp.arange(first, first + slots, dtype=jnp.int32)
        blocks = (2 * at[:, None] + (core ^ jnp.arange(2, dtype=jnp.int32))[None]).reshape(-1)
        return jnp.concatenate([head[None], jnp.asarray(active, jnp.int32)[None], blocks])

    is_first = chip < slots
    initial = lax.dynamic_slice_in_dim(fast_init, chip, 1, 0)
    out_early, weights = fast_stretch(
        fast_table(0, is_first), k_near, v_near, rate, initial, fast_init, q_near, attended_near
    )
    out_far, weights = fast_stretch(
        fast_table(slots, True), k_far, v_far, rate, weights, fast_init, q_far, attended_far
    )
    out_late, weights = fast_stretch(
        fast_table(0, ~is_first), k_near, v_near, rate, weights, fast_init, q_near, attended_near
    )
    out_near = jnp.where(is_first, out_early, out_late)
    results = [out_near[slot] for slot in range(slots)] + [out_far[slot] for slot in range(slots)]
    results = [results[0]] + [swap(results[slot], 2 * slot) for slot in range(1, chips)]
    combined = jnp.zeros_like(tokens)
    for slot in range(chips):
        combined = lax.dynamic_update_slice_in_dim(combined, results[slot], (chip ^ slot) * width, 1)
    return combined


def body(tokens, qkv_maps, rate_map, fast_init):
    groups = lax.axis_size("tok")
    heads = qkv_maps.shape[0]
    powers = groups & (groups - 1) == 0
    if powers and groups == 2 * heads and tokens.shape[0] == WINDOW:
        return head_body(tokens, qkv_maps, rate_map, fast_init)
    return general_body(tokens, qkv_maps, rate_map, fast_init)


def solution(mesh):
    in_specs = (
        P("tok", "head"),
        P("head", None, None),
        P("head", None),
        P("head", None, None, None),
    )
    out_specs = P("tok", "head")
    return jax.shard_map(body, mesh=mesh, in_specs=in_specs, out_specs=out_specs, check_vma=False)
```

```python
import functools

import jax
import jax.numpy as jnp
from jax import lax
from jax.experimental import pallas as pl
from jax.experimental.pallas import tpu as pltpu
from jax.sharding import PartitionSpec as P

WINDOW = 512


rate_base = 0.003
epsilon = 1e-06
VMEM_LIMIT = 48 * 1024 * 1024


def from_behind(block, axis, distance):
    devices = range(lax.axis_size(axis))
    route = [(i - distance, i) for i in devices if i - distance in devices]
    return lax.ppermute(block, axis, route)


def rms_rows(matrix):
    matrix = matrix.astype(jnp.float32)
    return matrix / jnp.sqrt(jnp.mean(matrix * matrix, axis=-1, keepdims=True) + epsilon)


def renorm(updated, initial):
    target = jnp.sqrt(jnp.mean(initial * initial, axis=-1, keepdims=True) + epsilon)
    current = jnp.sqrt(jnp.mean(updated * updated, axis=-1, keepdims=True) + epsilon)
    return (updated * (target / current)).astype(jnp.bfloat16)


def band_attention(queries, key_rows, value_rows, query_pos, key_pos, score_scale):
    scores = (
        jnp.einsum("qhd,khd->hqk", queries, key_rows, preferred_element_type=jnp.float32)
        * score_scale
    )
    key_mask = (
        (key_pos[None, :] <= query_pos[:, None])
        & (key_pos[None, :] > query_pos[:, None] - WINDOW)
        & (key_pos[None, :] >= 0)
    )
    key_mask = key_mask[None]
    row_max = jnp.max(jnp.where(key_mask, scores, -1e30), axis=2, keepdims=True)
    raised = jnp.where(key_mask, jnp.exp(scores - row_max), 0.0)
    probs = (raised / jnp.sum(raised, axis=2, keepdims=True)).astype(jnp.bfloat16)
    return jnp.einsum("hqk,khd->qhd", probs, value_rows, preferred_element_type=jnp.float32)


def fast_gradient(weights, key_part, value_part, rate_part):
    pre_gate = jnp.einsum(
        "rhd,hde->rhe", key_part, weights[:, 0], preferred_element_type=jnp.float32
    )
    pre_up = jnp.einsum("rhd,hde->rhe", key_part, weights[:, 1], preferred_element_type=jnp.float32)
    sigma = jax.nn.sigmoid(pre_gate)
    gated = pre_gate * sigma
    hidden = (gated * pre_up).astype(jnp.bfloat16)
    target = (rate_part.astype(jnp.float32)[:, :, None] * value_part.astype(jnp.float32)).astype(
        jnp.bfloat16
    )
    grad_down = jnp.einsum("rhe,rhd->hed", hidden, target, preferred_element_type=jnp.float32)
    back_hidden = jnp.einsum(
        "rhd,hed->rhe", target, weights[:, 2], preferred_element_type=jnp.float32
    )
    gate_delta = (back_hidden * pre_up * sigma * (1.0 + pre_gate * (1.0 - sigma))).astype(
        jnp.bfloat16
    )
    up_delta = (back_hidden * gated).astype(jnp.bfloat16)
    grad_gate = jnp.einsum("rhd,rhe->hde", key_part, gate_delta, preferred_element_type=jnp.float32)
    grad_up = jnp.einsum("rhd,rhe->hde", key_part, up_delta, preferred_element_type=jnp.float32)
    return jnp.stack([grad_gate, grad_up, grad_down], 1)


def fast_apply(weights, query_part):
    app_gate = jnp.einsum(
        "rhd,hde->rhe", query_part, weights[:, 0], preferred_element_type=jnp.float32
    )
    app_up = jnp.einsum(
        "rhd,hde->rhe", query_part, weights[:, 1], preferred_element_type=jnp.float32
    )
    app_hidden = (app_gate * jax.nn.sigmoid(app_gate) * app_up).astype(jnp.bfloat16)
    result = jnp.einsum(
        "rhe,hed->rhd", app_hidden, weights[:, 2], preferred_element_type=jnp.float32
    )
    return result.astype(jnp.bfloat16)


def update_weights(weights, partial_value, initial):
    total = lax.psum(partial_value.astype(jnp.bfloat16), "tok").astype(jnp.float32)
    return renorm(weights.astype(jnp.float32) + total, initial)


def general_body(tokens, qkv_maps, rate_map, fast_init):
    tok_rows = tokens.shape[0]
    head_count = qkv_maps.shape[0]
    head_width = qkv_maps.shape[1]
    groups = lax.axis_size("tok")
    logit_terms = jnp.dot(tokens, rate_map, preferred_element_type=jnp.float32)
    logits = lax.psum_scatter(
        logit_terms.astype(jnp.bfloat16), "head", scatter_dimension=1, tiled=True
    ).astype(jnp.float32)
    rate = (rate_base * jax.nn.softplus(logits)).astype(jnp.bfloat16)
    inputs = tokens.reshape(tok_rows, head_count, head_width)
    projected = jnp.einsum("rhd,hde->rhe", inputs, qkv_maps, preferred_element_type=jnp.float32)
    queries = projected[:, :, :head_width].astype(jnp.bfloat16)
    key_rows = projected[:, :, head_width : 2 * head_width].astype(jnp.bfloat16)
    value_rows = projected[:, :, 2 * head_width :].astype(jnp.bfloat16)
    tail_rows = min(WINDOW, tok_rows)
    edge = jnp.stack([key_rows, value_rows], 0)
    distance = 0
    received = [from_behind(edge, "tok", distance + 1)]
    anchor = lax.axis_index("tok") * tok_rows
    offsets = jnp.arange(tail_rows, dtype=jnp.int32)
    distance = 1
    arrived = received[distance - 1]
    key_parts = [arrived[0]]
    value_parts = [arrived[1]]
    position_parts = [anchor - distance * tok_rows + tok_rows - tail_rows + offsets]
    local_pos = anchor + jnp.arange(tok_rows, dtype=jnp.int32)
    all_keys = jnp.concatenate(key_parts + [key_rows], 0)
    all_values = jnp.concatenate(value_parts + [value_rows], 0)
    all_pos = jnp.concatenate(position_parts + [local_pos], 0)
    attended = band_attention(
        queries, all_keys, all_values, local_pos, all_pos, head_width ** (-0.5)
    )
    q_norm = rms_rows(queries).astype(jnp.bfloat16)
    k_norm = rms_rows(key_rows).astype(jnp.bfloat16)
    initial = fast_init.astype(jnp.float32)
    weights = fast_init
    own_block = lax.axis_index("tok") // (groups // 2)
    fast_out = jnp.zeros_like(q_norm)
    for half_index in range(2):
        partial_value = fast_gradient(weights, k_norm, value_rows, rate)
        partial_value = jnp.where(own_block == half_index, partial_value, 0.0)
        weights = update_weights(weights, partial_value, initial)
        applied = fast_apply(weights, q_norm)
        fast_out = jnp.where(own_block == half_index, applied, fast_out)
    combined = (attended + fast_out.astype(jnp.float32)).astype(jnp.bfloat16)
    return combined.reshape(tok_rows, head_count * head_width)


def matmul(left, right):
    return jnp.dot(left, right, preferred_element_type=jnp.float32)


def matmul_nt(left, right):
    return lax.dot_general(left, right, (((1,), (1,)), ((), ())), preferred_element_type=jnp.float32)


def matmul_tn(left, right):
    return lax.dot_general(left, right, (((0,), (0,)), ((), ())), preferred_element_type=jnp.float32)


def unit_rows(rows):
    rows = rows.astype(jnp.float32)
    scale = lax.rsqrt(jnp.mean(rows * rows, axis=-1, keepdims=True) + epsilon)
    return (rows * scale).astype(jnp.bfloat16)


def logistic(a):
    return 0.5 * jnp.tanh(0.5 * a) + 0.5


def stage_kernel(count, kept, table, *refs):
    slots = count // 2
    blocks, before, refs = refs[:count], refs[count : count + slots], refs[count + slots :]
    (maps, rate, earlier, initial), refs = refs[:4], refs[4 + kept :]
    results, new, refs = refs[:slots], refs[slots], refs[slots + 1 :]
    x, m, w, start, fresh, k, v, q, attended, kn, target, hidden, gate_delta, up_delta, out, sems = refs
    rows, width = x.shape[1:]
    part = rows // 2
    head, first, there, later = table[0], table[2], table[3] > 0, table[4] > 0
    place = [table[6 + at] for at in range(count)]
    copies = [pltpu.make_async_copy(blocks[at], x.at[at], sems.at[at]) for at in range(count)]
    copy_before = [pltpu.make_async_copy(ref, x.at[count], sems.at[count]) for ref in before]
    copy_maps = pltpu.make_async_copy(maps.at[head], m, sems.at[count + 1])
    copy_initial = pltpu.make_async_copy(initial.at[head], start, sems.at[count + 2])
    copy_weights = pltpu.make_async_copy(earlier.at[0], w, sems.at[count + 3])
    copy_same = pltpu.make_async_copy(initial.at[head], w, sems.at[count + 3])
    send_new = pltpu.make_async_copy(fresh, new.at[0], sems.at[count + 4])
    send = [
        pltpu.make_async_copy(out.at[at], results[at], sems.at[count + 5 + at]) for at in range(slots)
    ]

    def span(at, size=rows):
        return pl.ds(pl.multiple_of(at, part), size)

    def keys_values(at, to):
        key_rows = matmul(x[at], m[:, width : 2 * width]).astype(jnp.bfloat16)
        value_rows = matmul(x[at], m[:, 2 * width :]).astype(jnp.bfloat16)
        k[span(to)] = key_rows
        v[span(to)] = value_rows
        return key_rows, value_rows

    @pl.when(table[1] > 0)
    def _():
        copy_maps.start()
        for copy in copies:
            copy.start()
        for at in range(slots):
            pl.when(there & (table[5] == at))(copy_before[at].start)
        pl.when(later)(copy_weights.start)
        pl.when(jnp.logical_not(later))(copy_same.start)
        copy_initial.start()
        copy_maps.wait()
        for at in range(count):
            copies[at].wait()
            key_rows, value_rows = keys_values(at, rows * (place[at] + 1))
            kn[span(rows * place[at])] = unit_rows(key_rows)
            spread = jnp.broadcast_to(rate[pl.ds(first + place[at], 1)], (128, rows)).T
            spread = jnp.concatenate([spread] * (width // 128), 1)
            target[span(rows * place[at])] = (spread * value_rows.astype(jnp.float32)).astype(jnp.bfloat16)
            if at % 2 == 0:
                q[at // 2] = matmul(x[at], m[:, :width]).astype(jnp.bfloat16)

        @pl.when(there)
        def _():
            copy_before[0].wait()
            keys_values(count, 0)

        @pl.when(jnp.logical_not(there))
        def _():
            k[:rows] = jnp.zeros((rows, width), jnp.bfloat16)
            v[:rows] = jnp.zeros((rows, width), jnp.bfloat16)

        copy_weights.wait()
        for at in range(count):
            here = slice(rows * at, rows * (at + 1))
            gate = matmul(kn[here], w[0])
            up = matmul(kn[here], w[1])
            back = matmul_nt(target[here], w[2])
            sigma = logistic(gate)
            gated = gate * sigma
            hidden[here] = (gated * up).astype(jnp.bfloat16)
            gate_delta[here] = (back * up * sigma * (1.0 + gate * (1.0 - sigma))).astype(jnp.bfloat16)
            up_delta[here] = (back * gated).astype(jnp.bfloat16)
        copy_initial.wait()
        for at, (left, right) in enumerate(((kn, gate_delta), (kn, up_delta), (hidden, target))):
            updated = w[at].astype(jnp.float32) + matmul_tn(left[...], right[...])
            origin = start[at].astype(jnp.float32)
            wanted = jnp.mean(origin * origin, axis=-1, keepdims=True) + epsilon
            held = jnp.mean(updated * updated, axis=-1, keepdims=True) + epsilon
            fresh[at] = (updated * (jnp.sqrt(wanted) * lax.rsqrt(held))).astype(jnp.bfloat16)
        send_new.start()
        row = lax.broadcasted_iota(jnp.int32, (part, rows + part), 0)
        column = lax.broadcasted_iota(jnp.int32, (part, rows + part), 1)
        band = (column > row) & (column <= row + rows)
        for at in range(slots):
            for half in range(2):
                base = rows * place[2 * at] + part * half
                queries = q[at, part * half : part * (half + 1)]
                scores = matmul_nt(queries, k[span(base, rows + part)]) * (width ** -0.5)
                floor = jnp.where(first > 0, 0, rows - base)
                scores = jnp.where(band & (column >= floor), scores, -1e30)
                raised = jnp.exp(scores - jnp.max(scores, axis=1, keepdims=True))
                total = jnp.sum(raised, axis=1, keepdims=True)
                values = v[span(base, rows + part)]
                attended[part * half : part * (half + 1)] = (
                    matmul(raised.astype(jnp.bfloat16), values) / total
                )
            queries = unit_rows(q[at])
            gate = matmul(queries, fresh[0])
            up = matmul(queries, fresh[1])
            inner = (gate * logistic(gate) * up).astype(jnp.bfloat16)
            fast = matmul(inner, fresh[2]).astype(jnp.bfloat16).astype(jnp.float32)
            out[at] = (attended[...] + fast).astype(jnp.bfloat16)
            send[at].start()
        send_new.wait()
        for copy in send:
            copy.wait()


def stage(table, blocks, before, maps, rate, earlier, initial, kept):
    count = len(blocks)
    rows, width = blocks[0].shape
    matrices = initial.shape[1:]
    bfloat = functools.partial(pltpu.VMEM, dtype=jnp.bfloat16)
    anywhere = pl.BlockSpec(memory_space=pl.ANY)
    tokens = rows * count
    work = tokens * width * width
    return pl.pallas_call(
        functools.partial(stage_kernel, count, len(kept)),
        grid_spec=pltpu.PrefetchScalarGridSpec(
            num_scalar_prefetch=1,
            grid=(),
            in_specs=[anywhere] * (count + len(before) + 1)
            + [pl.BlockSpec(memory_space=pltpu.VMEM)]
            + [anywhere] * (2 + len(kept)),
            out_specs=[anywhere] * (count // 2 + 1),
            scratch_shapes=[
                bfloat((count + 1, rows, width)),
                bfloat(maps.shape[1:]),
                bfloat(matrices),
                bfloat(matrices),
                bfloat(matrices),
                bfloat((tokens + rows, width)),
                bfloat((tokens + rows, width)),
                bfloat((count // 2, rows, width)),
                pltpu.VMEM((rows, width), jnp.float32),
                bfloat((tokens, width)),
                bfloat((tokens, width)),
                bfloat((tokens, width)),
                bfloat((tokens, width)),
                bfloat((tokens, width)),
                bfloat((count // 2, rows, width)),
                pltpu.SemaphoreType.DMA((count + 5 + count // 2,)),
            ],
        ),
        out_shape=[jax.ShapeDtypeStruct((rows, width), jnp.bfloat16)] * (count // 2)
        + [jax.ShapeDtypeStruct((1,) + matrices, jnp.bfloat16)],
        input_output_aliases={1 + count + len(before) + 4 + at: at for at in range(len(kept))},
        compiler_params=pltpu.CompilerParams(vmem_limit_bytes=VMEM_LIMIT),
        cost_estimate=pl.CostEstimate(flops=24 * work, bytes_accessed=20 * tokens * width, transcendentals=0),
        name="stage",
    )(table, *blocks, *before, maps, rate, earlier, initial, *kept)


def head_body(tokens, qkv_maps, rate_map, fast_init):
    rows = tokens.shape[0]
    heads, width = qkv_maps.shape[:2]
    groups = lax.axis_size("tok")
    chips = groups // 2
    slots = chips // 2
    me = lax.axis_index("tok")
    chip, core = me // 2, me % 2

    def swap(block, bits):
        return lax.ppermute(block, "tok", [(i, i ^ bits) for i in range(groups)])

    def piece(slot):
        return lax.dynamic_slice_in_dim(tokens, (chip ^ slot) * width, width, 1)

    pieces = [piece(slot) for slot in range(chips)]
    same = [pieces[0]] + [swap(pieces[slot], 2 * slot) for slot in range(1, chips)]
    other = [swap(block, 1) for block in same]

    terms = lax.dot_general(
        rate_map, tokens, (((0,), (1,)), ((), ())), preferred_element_type=jnp.float32
    )
    terms = lax.all_to_all(terms.reshape(-1, heads, rows), "head", 0, 0)
    rate = (rate_base * jax.nn.softplus(jnp.sum(terms, 0))).astype(jnp.bfloat16)
    rate = lax.all_to_all(jnp.repeat(rate, 2, axis=0), "tok", 0, 0, tiled=True).astype(jnp.float32)

    def mixed(first):
        return [part for slot in range(first, first + slots) for part in (same[slot], other[slot])]

    is_first = chip < slots

    def table(first, active, later):
        at = chip ^ jnp.arange(first, first + slots, dtype=jnp.int32)
        place = 2 * (at % slots)[:, None] + (core ^ jnp.arange(2, dtype=jnp.int32))[None]
        opening = 2 * slots * (at[0] // slots)
        flags = [chip, active, opening, (opening > 0) & (core == 0), later, (chip ^ (slots - 1)) % slots]
        return jnp.concatenate([jnp.stack([jnp.asarray(flag, jnp.int32) for flag in flags]), place.reshape(-1)])

    near = functools.partial(stage, blocks=mixed(0), maps=qkv_maps, rate=rate, initial=fast_init)
    *early, weights = near(
        table(0, is_first, False), before=other[:slots], earlier=fast_init, kept=[]
    )
    *far, weights = stage(
        table(slots, True, is_first), mixed(slots), other[:slots], qkv_maps, rate, weights, fast_init, []
    )
    *late, _ = near(
        table(0, ~is_first, True), before=other[slots:], earlier=weights, kept=early
    )
    results = late + far
    results = [results[0]] + [swap(results[slot], 2 * slot) for slot in range(1, chips)]
    combined = jnp.zeros_like(tokens)
    for slot in range(chips):
        combined = lax.dynamic_update_slice_in_dim(combined, results[slot], (chip ^ slot) * width, 1)
    return combined


def body(tokens, qkv_maps, rate_map, fast_init):
    groups = lax.axis_size("tok")
    heads = qkv_maps.shape[0]
    powers = groups & (groups - 1) == 0 and groups > 2
    if powers and groups == 2 * heads and tokens.shape[0] == WINDOW:
        return head_body(tokens, qkv_maps, rate_map, fast_init)
    return general_body(tokens, qkv_maps, rate_map, fast_init)


def solution(mesh):
    in_specs = (
        P("tok", "head"),
        P("head", None, None),
        P("head", None),
        P("head", None, None, None),
    )
    out_specs = P("tok", "head")
    return jax.shard_map(body, mesh=mesh, in_specs=in_specs, out_specs=out_specs, check_vma=False)
```

```python
import functools

import jax
import jax.numpy as jnp
from jax import lax
from jax.experimental import pallas as pl
from jax.experimental.pallas import tpu as pltpu
from jax.sharding import PartitionSpec as P

WINDOW = 512


rate_base = 0.003
epsilon = 1e-06
VMEM_LIMIT = 33 * 1024 * 1024
BEGIN_LIMIT = 33 * 1024 * 1024


def from_behind(block, axis, distance):
    devices = range(lax.axis_size(axis))
    route = [(i - distance, i) for i in devices if i - distance in devices]
    return lax.ppermute(block, axis, route)


def rms_rows(matrix):
    matrix = matrix.astype(jnp.float32)
    return matrix / jnp.sqrt(jnp.mean(matrix * matrix, axis=-1, keepdims=True) + epsilon)


def renorm(updated, initial):
    target = jnp.sqrt(jnp.mean(initial * initial, axis=-1, keepdims=True) + epsilon)
    current = jnp.sqrt(jnp.mean(updated * updated, axis=-1, keepdims=True) + epsilon)
    return (updated * (target / current)).astype(jnp.bfloat16)


def band_attention(queries, key_rows, value_rows, query_pos, key_pos, score_scale):
    scores = (
        jnp.einsum("qhd,khd->hqk", queries, key_rows, preferred_element_type=jnp.float32)
        * score_scale
    )
    key_mask = (
        (key_pos[None, :] <= query_pos[:, None])
        & (key_pos[None, :] > query_pos[:, None] - WINDOW)
        & (key_pos[None, :] >= 0)
    )
    key_mask = key_mask[None]
    row_max = jnp.max(jnp.where(key_mask, scores, -1e30), axis=2, keepdims=True)
    raised = jnp.where(key_mask, jnp.exp(scores - row_max), 0.0)
    probs = (raised / jnp.sum(raised, axis=2, keepdims=True)).astype(jnp.bfloat16)
    return jnp.einsum("hqk,khd->qhd", probs, value_rows, preferred_element_type=jnp.float32)


def fast_gradient(weights, key_part, value_part, rate_part):
    pre_gate = jnp.einsum(
        "rhd,hde->rhe", key_part, weights[:, 0], preferred_element_type=jnp.float32
    )
    pre_up = jnp.einsum("rhd,hde->rhe", key_part, weights[:, 1], preferred_element_type=jnp.float32)
    sigma = jax.nn.sigmoid(pre_gate)
    gated = pre_gate * sigma
    hidden = (gated * pre_up).astype(jnp.bfloat16)
    target = (rate_part.astype(jnp.float32)[:, :, None] * value_part.astype(jnp.float32)).astype(
        jnp.bfloat16
    )
    grad_down = jnp.einsum("rhe,rhd->hed", hidden, target, preferred_element_type=jnp.float32)
    back_hidden = jnp.einsum(
        "rhd,hed->rhe", target, weights[:, 2], preferred_element_type=jnp.float32
    )
    gate_delta = (back_hidden * pre_up * sigma * (1.0 + pre_gate * (1.0 - sigma))).astype(
        jnp.bfloat16
    )
    up_delta = (back_hidden * gated).astype(jnp.bfloat16)
    grad_gate = jnp.einsum("rhd,rhe->hde", key_part, gate_delta, preferred_element_type=jnp.float32)
    grad_up = jnp.einsum("rhd,rhe->hde", key_part, up_delta, preferred_element_type=jnp.float32)
    return jnp.stack([grad_gate, grad_up, grad_down], 1)


def fast_apply(weights, query_part):
    app_gate = jnp.einsum(
        "rhd,hde->rhe", query_part, weights[:, 0], preferred_element_type=jnp.float32
    )
    app_up = jnp.einsum(
        "rhd,hde->rhe", query_part, weights[:, 1], preferred_element_type=jnp.float32
    )
    app_hidden = (app_gate * jax.nn.sigmoid(app_gate) * app_up).astype(jnp.bfloat16)
    result = jnp.einsum(
        "rhe,hed->rhd", app_hidden, weights[:, 2], preferred_element_type=jnp.float32
    )
    return result.astype(jnp.bfloat16)


def update_weights(weights, partial_value, initial):
    total = lax.psum(partial_value.astype(jnp.bfloat16), "tok").astype(jnp.float32)
    return renorm(weights.astype(jnp.float32) + total, initial)


def general_body(tokens, qkv_maps, rate_map, fast_init):
    tok_rows = tokens.shape[0]
    head_count = qkv_maps.shape[0]
    head_width = qkv_maps.shape[1]
    groups = lax.axis_size("tok")
    logit_terms = jnp.dot(tokens, rate_map, preferred_element_type=jnp.float32)
    logits = lax.psum_scatter(
        logit_terms.astype(jnp.bfloat16), "head", scatter_dimension=1, tiled=True
    ).astype(jnp.float32)
    rate = (rate_base * jax.nn.softplus(logits)).astype(jnp.bfloat16)
    inputs = tokens.reshape(tok_rows, head_count, head_width)
    projected = jnp.einsum("rhd,hde->rhe", inputs, qkv_maps, preferred_element_type=jnp.float32)
    queries = projected[:, :, :head_width].astype(jnp.bfloat16)
    key_rows = projected[:, :, head_width : 2 * head_width].astype(jnp.bfloat16)
    value_rows = projected[:, :, 2 * head_width :].astype(jnp.bfloat16)
    tail_rows = min(WINDOW, tok_rows)
    edge = jnp.stack([key_rows, value_rows], 0)
    distance = 0
    received = [from_behind(edge, "tok", distance + 1)]
    anchor = lax.axis_index("tok") * tok_rows
    offsets = jnp.arange(tail_rows, dtype=jnp.int32)
    distance = 1
    arrived = received[distance - 1]
    key_parts = [arrived[0]]
    value_parts = [arrived[1]]
    position_parts = [anchor - distance * tok_rows + tok_rows - tail_rows + offsets]
    local_pos = anchor + jnp.arange(tok_rows, dtype=jnp.int32)
    all_keys = jnp.concatenate(key_parts + [key_rows], 0)
    all_values = jnp.concatenate(value_parts + [value_rows], 0)
    all_pos = jnp.concatenate(position_parts + [local_pos], 0)
    attended = band_attention(
        queries, all_keys, all_values, local_pos, all_pos, head_width ** (-0.5)
    )
    q_norm = rms_rows(queries).astype(jnp.bfloat16)
    k_norm = rms_rows(key_rows).astype(jnp.bfloat16)
    initial = fast_init.astype(jnp.float32)
    weights = fast_init
    own_block = lax.axis_index("tok") // (groups // 2)
    fast_out = jnp.zeros_like(q_norm)
    for half_index in range(2):
        partial_value = fast_gradient(weights, k_norm, value_rows, rate)
        partial_value = jnp.where(own_block == half_index, partial_value, 0.0)
        weights = update_weights(weights, partial_value, initial)
        applied = fast_apply(weights, q_norm)
        fast_out = jnp.where(own_block == half_index, applied, fast_out)
    combined = (attended + fast_out.astype(jnp.float32)).astype(jnp.bfloat16)
    return combined.reshape(tok_rows, head_count * head_width)


def matmul(left, right):
    return jnp.dot(left, right, preferred_element_type=jnp.float32)


def matmul_nt(left, right):
    return lax.dot_general(left, right, (((1,), (1,)), ((), ())), preferred_element_type=jnp.float32)


def matmul_tn(left, right):
    return lax.dot_general(left, right, (((0,), (0,)), ((), ())), preferred_element_type=jnp.float32)


def unit_rows(rows):
    rows = rows.astype(jnp.float32)
    scale = lax.rsqrt(jnp.mean(rows * rows, axis=-1, keepdims=True) + epsilon)
    return (rows * scale).astype(jnp.bfloat16)


def logistic(a):
    return 0.5 * jnp.tanh(0.5 * a) + 0.5


def fetch(source, target, sem, when=None):
    copy = pltpu.make_async_copy(source, target, sem)
    if when is None:
        copy.start()
    else:
        pl.when(when)(copy.start)


def fetched(target, sem):
    pltpu.make_async_copy(target, target, sem).wait()


def learn(at, x, m, rate_row, pool, put_query, put_key_value):
    rows, width = x.shape[1:]
    here = pl.ds(pl.multiple_of(rows * at, rows), rows)
    key_rows = matmul(x[at], m[:, width : 2 * width]).astype(jnp.bfloat16)
    value_rows = matmul(x[at], m[:, 2 * width :]).astype(jnp.bfloat16)
    put_key_value(key_rows, value_rows)
    pool[0, here] = unit_rows(key_rows)
    spread = jnp.broadcast_to(rate_row, (128, rows)).T
    spread = jnp.concatenate([spread] * (width // 128), 1)
    pool[2, here] = (spread * value_rows.astype(jnp.float32)).astype(jnp.bfloat16)

    @pl.when(at % 2 == 0)
    def _():
        put_query(matmul(x[at], m[:, :width]).astype(jnp.bfloat16))


def deltas(at, rows, w, pool):
    here = pl.ds(pl.multiple_of(rows * at, rows), rows)
    gate = matmul(pool[0, here], w[0])
    up = matmul(pool[0, here], w[1])
    back = matmul_nt(pool[2, here], w[2])
    sigma = logistic(gate)
    gated = gate * sigma
    pool[1, here] = (gated * up).astype(jnp.bfloat16)
    pool[3, here] = (back * up * sigma * (1.0 + gate * (1.0 - sigma))).astype(jnp.bfloat16)
    pool[4, here] = (back * gated).astype(jnp.bfloat16)


def gradient(at, pool):
    return matmul_tn(pool[at // 2], pool[jnp.where(at == 2, 2, 3 + at)])


def stage_kernel(counts, table, *refs):
    count, befores, earliers, begun = counts
    slots = count // 2 + begun
    blocks, refs = refs[:count], refs[count:]
    before, refs = refs[:befores], refs[befores:]
    earlier, refs = refs[:earliers], refs[earliers:]
    held, refs = refs[: 2 * begun], refs[2 * begun :]
    (maps, rate, initial), refs = refs[:3], refs[3:]
    results, new, refs = refs[:slots], refs[slots], refs[slots + 1 :]
    x, m, w, start, fresh, k, v, q, attended, pool, out, sems, *grads = refs
    rows, width = x.shape[1:]
    part = rows // 2
    updates, answers, first, there = table[0] > 0, table[1] > 0, table[2], table[3] > 0
    at_maps, at_start, at_weights, at_new, at_held, at_grads = (sems.at[count + 1 + at] for at in range(6))
    send_new = pltpu.make_async_copy(fresh, new, at_new)
    send = [pltpu.make_async_copy(out.at[at], results[at], sems.at[count + 7 + at]) for at in range(slots)]

    def span(at, size=rows):
        return pl.ds(pl.multiple_of(at, part), size)

    def answer():
        row = lax.broadcasted_iota(jnp.int32, (part, rows + part), 0)
        column = lax.broadcasted_iota(jnp.int32, (part, rows + part), 1)
        band = (column > row) & (column <= row + rows)

        @pl.loop(0, slots)
        def _(at):
            @pl.loop(0, 2)
            def _(half):
                own = span(part * half, part)
                base = rows * table[6 + 2 * at] + part * half
                scores = matmul_nt(q[at, own], k[span(base, rows + part)]) * (width ** -0.5)
                floor = jnp.where(first > 0, 0, rows - base)
                scores = jnp.where(band & (column >= floor), scores, -1e30)
                raised = jnp.exp(scores - jnp.max(scores, axis=1, keepdims=True))
                total = jnp.sum(raised, axis=1, keepdims=True)
                values = v[span(base, rows + part)]
                attended[own] = matmul(raised.astype(jnp.bfloat16), values) / total

            queries = unit_rows(q[at])
            gate = matmul(queries, fresh[0])
            up = matmul(queries, fresh[1])
            inner = (gate * logistic(gate) * up).astype(jnp.bfloat16)
            fast = matmul(inner, fresh[2]).astype(jnp.bfloat16).astype(jnp.float32)
            out[at] = (attended[...] + fast).astype(jnp.bfloat16)

        for copy in send:
            copy.start()
        for copy in send:
            copy.wait()

    @pl.when(updates | answers)
    def _():
        fetch(maps, m, at_maps)
        for at in range(count):
            fetch(blocks[at], x.at[at], sems.at[at])
        for at in range(befores):
            fetch(before[at], x.at[count], sems.at[count], there & (table[4] == at))
        for at in range(earliers):
            fetch(earlier[at], w, at_weights, table[5] == at)
        fetch(initial, w, at_weights, table[5] >= earliers)
        fetch(initial, start, at_start)
        if begun:
            for at in range(2):
                to = span(rows * (table[6 + count + at] + 1))
                fetch(held[0].at[1 + at], k.at[to], at_held)
                fetch(held[0].at[3 + at], v.at[to], at_held)
            fetch(held[0].at[0], q.at[slots - 1], at_held)
            fetch(held[1], grads[0], at_grads)
        fetched(m, at_maps)

        @pl.loop(0, count)
        def _(at):
            to = span(rows * (table[6 + at] + 1))

            def put_query(query_rows):
                q[at // 2] = query_rows

            def put_key_value(key_rows, value_rows):
                k[to] = key_rows
                v[to] = value_rows

            fetched(x.at[at], sems.at[at])
            learn(at, x, m, rate[pl.ds(first + table[6 + at], 1)], pool, put_query, put_key_value)

        @pl.when(there)
        def _():
            fetched(x.at[count], sems.at[count])
            k[:rows] = matmul(x[count], m[:, width : 2 * width]).astype(jnp.bfloat16)
            v[:rows] = matmul(x[count], m[:, 2 * width :]).astype(jnp.bfloat16)

        @pl.when(jnp.logical_not(there))
        def _():
            k[:rows] = jnp.zeros((rows, width), jnp.bfloat16)
            v[:rows] = jnp.zeros((rows, width), jnp.bfloat16)

        fetched(w, at_weights)
        fetched(start, at_start)
        if begun:
            fetched(k.at[pl.ds(0, 4 * rows)], at_held)
            fetched(q.at[0], at_held)
            fetched(grads[0], at_grads)

        @pl.when(updates)
        def _():
            pl.loop(0, count)(lambda at: deltas(at, rows, w, pool))

            @pl.loop(0, 3)
            def _(at):
                updated = w[at].astype(jnp.float32) + gradient(at, pool)
                if begun:
                    updated = updated + grads[0][at]
                origin = start[at].astype(jnp.float32)
                wanted = jnp.mean(origin * origin, axis=-1, keepdims=True) + epsilon
                held_now = jnp.mean(updated * updated, axis=-1, keepdims=True) + epsilon
                fresh[at] = (updated * (jnp.sqrt(wanted) * lax.rsqrt(held_now))).astype(jnp.bfloat16)

            send_new.start()

        @pl.when(jnp.logical_not(updates))
        def _():
            fresh[...] = w[...]

        pl.when(answers)(answer)
        pl.when(updates)(send_new.wait)


def stage(table, blocks, before, earlier, maps, rate, initial, held=(), scale=24):
    count, begun = len(blocks), len(held) // 2
    rows, width = blocks[0].shape
    matrices = initial.shape
    bfloat = functools.partial(pltpu.VMEM, dtype=jnp.bfloat16)
    anywhere = pl.BlockSpec(memory_space=pl.ANY)
    slots = count // 2 + begun
    stretch = 2 * slots * rows
    operands = [*blocks, *before, *earlier, *held, maps]
    return pl.pallas_call(
        functools.partial(stage_kernel, (count, len(before), len(earlier), begun)),
        grid_spec=pltpu.PrefetchScalarGridSpec(
            num_scalar_prefetch=1,
            grid=(),
            in_specs=[anywhere] * len(operands) + [pl.BlockSpec(memory_space=pltpu.VMEM), anywhere],
            out_specs=[anywhere] * (slots + 1),
            scratch_shapes=[
                bfloat((count + 1, rows, width)),
                bfloat(maps.shape),
                bfloat(matrices),
                bfloat(matrices),
                bfloat(matrices),
                bfloat((stretch + rows, width)),
                bfloat((stretch + rows, width)),
                bfloat((slots, rows, width)),
                pltpu.VMEM((rows, width), jnp.float32),
                bfloat((5, count * rows, width)),
                bfloat((slots, rows, width)),
                pltpu.SemaphoreType.DMA((count + 7 + slots,)),
            ]
            + [pltpu.VMEM(matrices, jnp.float32)] * begun,
        ),
        out_shape=[jax.ShapeDtypeStruct((rows, width), jnp.bfloat16)] * slots
        + [jax.ShapeDtypeStruct(matrices, jnp.bfloat16)],
        compiler_params=pltpu.CompilerParams(vmem_limit_bytes=VMEM_LIMIT),
        cost_estimate=pl.CostEstimate(flops=scale * stretch * width * width, bytes_accessed=scale * stretch * width, transcendentals=0),
        name="stage",
    )(table, *operands, rate, initial)


def after(array, *others):
    return lax.optimization_barrier((array, *others))[0]


def head_body(tokens, qkv_maps, rate_map, fast_init):
    rows = tokens.shape[0]
    heads, width = qkv_maps.shape[:2]
    groups = lax.axis_size("tok")
    chips = groups // 2
    slots = chips // 2
    last = chips - 1
    me = lax.axis_index("tok")
    chip, core = me // 2, me % 2
    is_first = (chip < slots).astype(jnp.int32)

    def swap(block, bits):
        return lax.ppermute(block, "tok", [(i, i ^ bits) for i in range(groups)])

    def piece(slot, source, index):
        return lax.dynamic_slice_in_dim(source, (index ^ slot) * width, width, 1)

    maps = lax.dynamic_index_in_dim(qkv_maps, chip, 0, False)
    initial = lax.dynamic_index_in_dim(fast_init, chip, 0, False)
    same = {slot: swap(piece(slot, tokens, chip), 2 * slot) for slot in range(1, slots)}
    same[last] = swap(piece(last, tokens, chip), 2 * last)
    terms = lax.dot_general(
        rate_map, tokens, (((0,), (1,)), ((), ())), preferred_element_type=jnp.float32
    )
    terms = lax.all_to_all(jnp.repeat(terms, 2, axis=0), ("head", "tok"), 0, 0, tiled=True)
    logits = jnp.sum(terms.reshape(-1, groups, rows), 0)
    rate = (rate_base * jax.nn.softplus(logits)).astype(jnp.bfloat16).astype(jnp.float32)
    source = tokens
    for slot in range(1, slots):
        source = after(source, same[slot])
    for slot in range(slots, last):
        same[slot] = swap(piece(slot, source, chip), 2 * slot)
    same[0] = piece(0, source, chip)
    other = {slot: swap(same[slot], 1) for slot in range(slots)}

    def integers(entries):
        return jnp.stack([jnp.asarray(entry, jnp.int32) for entry in entries])

    def places(slot):
        return [2 * ((chip ^ slot) % slots) + core, 2 * ((chip ^ slot) % slots) + (1 - core)]

    def opening(slot):
        return 2 * slots * ((chip ^ slot) // slots)

    def table(slots_in, updates, answers, earlier):
        first = opening(slots_in[0])
        before = (chip ^ (slots - 1)) % slots
        flags = [updates, answers, first, (first > 0) & (core == 0), before, earlier]
        return integers(flags + [place for slot in slots_in for place in places(slot)])

    near_slots, far_slots = range(slots), range(slots, chips)
    near_blocks = [block for slot in near_slots for block in (same[slot], other[slot])]
    near_others = [other[slot] for slot in near_slots]
    shared = dict(maps=maps, rate=rate, initial=initial)
    *_, first_new = stage(table(near_slots, is_first, False, 0), near_blocks, near_others[:1], [], scale=0, **shared)
    for slot in far_slots:
        other[slot] = swap(after(same[slot], first_new), 1)
    far_blocks = [block for slot in far_slots for block in (same[slot], other[slot])]
    *far_results, far_new = stage(
        table(far_slots, True, True, 1 - is_first), far_blocks, near_others, [first_new], **shared
    )
    *near_results, _ = stage(
        table(near_slots, 1 - is_first, True, 1 - is_first), near_blocks, [other[slot] for slot in far_slots], [first_new, far_new], **shared
    )
    results = near_results + far_results
    combined = jnp.zeros_like(tokens)
    for slot in (0, *far_slots, *range(1, slots)):
        result = swap(results[slot], 2 * slot) if slot else results[slot]
        combined = lax.dynamic_update_slice_in_dim(combined, result, (chip ^ slot) * width, 1)
    return combined


def body(tokens, qkv_maps, rate_map, fast_init):
    groups = lax.axis_size("tok")
    heads = qkv_maps.shape[0]
    powers = groups & (groups - 1) == 0 and groups > 2
    if powers and groups == 2 * heads and tokens.shape[0] == WINDOW:
        return head_body(tokens, qkv_maps, rate_map, fast_init)
    return general_body(tokens, qkv_maps, rate_map, fast_init)


def solution(mesh):
    in_specs = (
        P("tok", "head"),
        P("head", None, None),
        P("head", None),
        P("head", None, None, None),
    )
    out_specs = P("tok", "head")
    return jax.shard_map(body, mesh=mesh, in_specs=in_specs, out_specs=out_specs, check_vma=False)
```

```python
import functools

import jax
import jax.numpy as jnp
from jax import lax
from jax.experimental import pallas as pl
from jax.experimental.pallas import tpu as pltpu
from jax.sharding import PartitionSpec as P

WINDOW = 512


rate_base = 0.003
epsilon = 1e-06
VMEM_LIMIT = 40 * 1024 * 1024
STATE = 64


def from_behind(block, axis, distance):
    devices = range(lax.axis_size(axis))
    route = [(i - distance, i) for i in devices if i - distance in devices]
    return lax.ppermute(block, axis, route)


def rms_rows(matrix):
    matrix = matrix.astype(jnp.float32)
    return matrix / jnp.sqrt(jnp.mean(matrix * matrix, axis=-1, keepdims=True) + epsilon)


def renorm(updated, initial):
    target = jnp.sqrt(jnp.mean(initial * initial, axis=-1, keepdims=True) + epsilon)
    current = jnp.sqrt(jnp.mean(updated * updated, axis=-1, keepdims=True) + epsilon)
    return (updated * (target / current)).astype(jnp.bfloat16)


def band_attention(queries, key_rows, value_rows, query_pos, key_pos, score_scale):
    scores = (
        jnp.einsum("qhd,khd->hqk", queries, key_rows, preferred_element_type=jnp.float32)
        * score_scale
    )
    key_mask = (
        (key_pos[None, :] <= query_pos[:, None])
        & (key_pos[None, :] > query_pos[:, None] - WINDOW)
        & (key_pos[None, :] >= 0)
    )
    key_mask = key_mask[None]
    row_max = jnp.max(jnp.where(key_mask, scores, -1e30), axis=2, keepdims=True)
    raised = jnp.where(key_mask, jnp.exp(scores - row_max), 0.0)
    probs = (raised / jnp.sum(raised, axis=2, keepdims=True)).astype(jnp.bfloat16)
    return jnp.einsum("hqk,khd->qhd", probs, value_rows, preferred_element_type=jnp.float32)


def fast_gradient(weights, key_part, value_part, rate_part):
    pre_gate = jnp.einsum(
        "rhd,hde->rhe", key_part, weights[:, 0], preferred_element_type=jnp.float32
    )
    pre_up = jnp.einsum("rhd,hde->rhe", key_part, weights[:, 1], preferred_element_type=jnp.float32)
    sigma = jax.nn.sigmoid(pre_gate)
    gated = pre_gate * sigma
    hidden = (gated * pre_up).astype(jnp.bfloat16)
    target = (rate_part.astype(jnp.float32)[:, :, None] * value_part.astype(jnp.float32)).astype(
        jnp.bfloat16
    )
    grad_down = jnp.einsum("rhe,rhd->hed", hidden, target, preferred_element_type=jnp.float32)
    back_hidden = jnp.einsum(
        "rhd,hed->rhe", target, weights[:, 2], preferred_element_type=jnp.float32
    )
    gate_delta = (back_hidden * pre_up * sigma * (1.0 + pre_gate * (1.0 - sigma))).astype(
        jnp.bfloat16
    )
    up_delta = (back_hidden * gated).astype(jnp.bfloat16)
    grad_gate = jnp.einsum("rhd,rhe->hde", key_part, gate_delta, preferred_element_type=jnp.float32)
    grad_up = jnp.einsum("rhd,rhe->hde", key_part, up_delta, preferred_element_type=jnp.float32)
    return jnp.stack([grad_gate, grad_up, grad_down], 1)


def fast_apply(weights, query_part):
    app_gate = jnp.einsum(
        "rhd,hde->rhe", query_part, weights[:, 0], preferred_element_type=jnp.float32
    )
    app_up = jnp.einsum(
        "rhd,hde->rhe", query_part, weights[:, 1], preferred_element_type=jnp.float32
    )
    app_hidden = (app_gate * jax.nn.sigmoid(app_gate) * app_up).astype(jnp.bfloat16)
    result = jnp.einsum(
        "rhe,hed->rhd", app_hidden, weights[:, 2], preferred_element_type=jnp.float32
    )
    return result.astype(jnp.bfloat16)


def update_weights(weights, partial_value, initial):
    total = lax.psum(partial_value.astype(jnp.bfloat16), "tok").astype(jnp.float32)
    return renorm(weights.astype(jnp.float32) + total, initial)


def general_body(tokens, qkv_maps, rate_map, fast_init):
    tok_rows = tokens.shape[0]
    head_count = qkv_maps.shape[0]
    head_width = qkv_maps.shape[1]
    groups = lax.axis_size("tok")
    logit_terms = jnp.dot(tokens, rate_map, preferred_element_type=jnp.float32)
    logits = lax.psum_scatter(
        logit_terms.astype(jnp.bfloat16), "head", scatter_dimension=1, tiled=True
    ).astype(jnp.float32)
    rate = (rate_base * jax.nn.softplus(logits)).astype(jnp.bfloat16)
    inputs = tokens.reshape(tok_rows, head_count, head_width)
    projected = jnp.einsum("rhd,hde->rhe", inputs, qkv_maps, preferred_element_type=jnp.float32)
    queries = projected[:, :, :head_width].astype(jnp.bfloat16)
    key_rows = projected[:, :, head_width : 2 * head_width].astype(jnp.bfloat16)
    value_rows = projected[:, :, 2 * head_width :].astype(jnp.bfloat16)
    tail_rows = min(WINDOW, tok_rows)
    edge = jnp.stack([key_rows, value_rows], 0)
    distance = 0
    received = [from_behind(edge, "tok", distance + 1)]
    anchor = lax.axis_index("tok") * tok_rows
    offsets = jnp.arange(tail_rows, dtype=jnp.int32)
    distance = 1
    arrived = received[distance - 1]
    key_parts = [arrived[0]]
    value_parts = [arrived[1]]
    position_parts = [anchor - distance * tok_rows + tok_rows - tail_rows + offsets]
    local_pos = anchor + jnp.arange(tok_rows, dtype=jnp.int32)
    all_keys = jnp.concatenate(key_parts + [key_rows], 0)
    all_values = jnp.concatenate(value_parts + [value_rows], 0)
    all_pos = jnp.concatenate(position_parts + [local_pos], 0)
    attended = band_attention(
        queries, all_keys, all_values, local_pos, all_pos, head_width ** (-0.5)
    )
    q_norm = rms_rows(queries).astype(jnp.bfloat16)
    k_norm = rms_rows(key_rows).astype(jnp.bfloat16)
    initial = fast_init.astype(jnp.float32)
    weights = fast_init
    own_block = lax.axis_index("tok") // (groups // 2)
    fast_out = jnp.zeros_like(q_norm)
    for half_index in range(2):
        partial_value = fast_gradient(weights, k_norm, value_rows, rate)
        partial_value = jnp.where(own_block == half_index, partial_value, 0.0)
        weights = update_weights(weights, partial_value, initial)
        applied = fast_apply(weights, q_norm)
        fast_out = jnp.where(own_block == half_index, applied, fast_out)
    combined = (attended + fast_out.astype(jnp.float32)).astype(jnp.bfloat16)
    return combined.reshape(tok_rows, head_count * head_width)


def matmul(left, right):
    return jnp.dot(left, right, preferred_element_type=jnp.float32)


def matmul_nt(left, right):
    return lax.dot_general(left, right, (((1,), (1,)), ((), ())), preferred_element_type=jnp.float32)


def matmul_tn(left, right):
    return lax.dot_general(left, right, (((0,), (0,)), ((), ())), preferred_element_type=jnp.float32)


def unit_rows(rows):
    rows = rows.astype(jnp.float32)
    scale = lax.rsqrt(jnp.mean(rows * rows, axis=-1, keepdims=True) + epsilon)
    return (rows * scale).astype(jnp.bfloat16)


def logistic(a):
    return 0.5 * jnp.tanh(0.5 * a) + 0.5


def fetch(source, target, sem, when=None):
    copy = pltpu.make_async_copy(source, target, sem)
    if when is None:
        copy.start()
    else:
        pl.when(when)(copy.start)


def fetched(target, sem):
    pltpu.make_async_copy(target, target, sem).wait()


def learn(at, x, source, m, rate_row, pool, put_query, put_key_value):
    rows, width = x.shape[1:]
    here = pl.ds(pl.multiple_of(rows * at, rows), rows)
    key_rows = matmul(x[source], m[:, width : 2 * width]).astype(jnp.bfloat16)
    value_rows = matmul(x[source], m[:, 2 * width :]).astype(jnp.bfloat16)
    if put_key_value is not None:
        put_key_value(key_rows, value_rows)
    pool[0, here] = unit_rows(key_rows)
    spread = jnp.broadcast_to(rate_row, (128, rows)).T
    spread = jnp.concatenate([spread] * (width // 128), 1)
    pool[2, here] = (spread * value_rows.astype(jnp.float32)).astype(jnp.bfloat16)

    if put_query is not None:

        @pl.when(at % 2 == 0)
        def _():
            put_query(matmul(x[source], m[:, :width]).astype(jnp.bfloat16))


def deltas(at, rows, w, pool):
    here = pl.ds(pl.multiple_of(rows * at, rows), rows)
    gate = matmul(pool[0, here], w[0])
    up = matmul(pool[0, here], w[1])
    back = matmul_nt(pool[2, here], w[2])
    sigma = logistic(gate)
    gated = gate * sigma
    pool[1, here] = (gated * up).astype(jnp.bfloat16)
    pool[3, here] = (back * up * sigma * (1.0 + gate * (1.0 - sigma))).astype(jnp.bfloat16)
    pool[4, here] = (back * gated).astype(jnp.bfloat16)


def gradient(at, pool, rows):
    return matmul_tn(pool[at // 2, :rows], pool[jnp.where(at == 2, 2, 3 + at), :rows])


def renew(updated, initial):
    origin = initial.astype(jnp.float32)
    wanted = jnp.mean(origin * origin, axis=-1, keepdims=True) + epsilon
    held = jnp.mean(updated * updated, axis=-1, keepdims=True) + epsilon
    return (updated * (jnp.sqrt(wanted) * lax.rsqrt(held))).astype(jnp.bfloat16)


def begin_kernel(count, table, *refs):
    near, far, refs = refs[:count], refs[count : count + 2], refs[count + 2 :]
    maps, rate, initial, state, x, m, w, fresh, kept, grads, pool, sems = refs
    rows = x.shape[1]
    updates = table[0] > 0
    fetch(maps, m, sems.at[count + 2])
    for at in range(count):
        fetch(near[at], x.at[at], sems.at[at], updates)
    for at in range(2):
        fetch(far[at], x.at[count + at], sems.at[count + at])
    fetch(initial, w, sems.at[count + 3])
    fetched(m, sems.at[count + 2])

    @pl.when(updates)
    def _():
        @pl.loop(0, count, unroll=True)
        def _(at):
            fetched(x.at[at], sems.at[at])
            learn(at, x, at, m, rate[pl.ds(table[1 + at], 1)], pool, None, None)

        fetched(w, sems.at[count + 3])
        pl.loop(0, count, unroll=True)(lambda at: deltas(at, rows, w, pool))

        @pl.loop(0, 3)
        def _(at):
            fresh[at] = renew(w[at].astype(jnp.float32) + gradient(at, pool, count * rows), w[at])

    @pl.when(jnp.logical_not(updates))
    def _():
        fetched(w, sems.at[count + 3])
        fresh[...] = w[...]

    send = [pltpu.make_async_copy(fresh, state.at[pl.ds(0, 3)], sems.at[0])]
    send[0].start()

    @pl.loop(0, 2, unroll=True)
    def _(at):
        def put_query(query_rows):
            kept[0] = query_rows

        def put_key_value(key_rows, value_rows):
            kept[1 + at] = key_rows
            kept[3 + at] = value_rows

        fetched(x.at[count + at], sems.at[count + at])
        learn(at, x, count + at, m, rate[pl.ds(table[1 + count + at], 1)], pool, put_query, put_key_value)

    send.append(pltpu.make_async_copy(kept, state.at[pl.ds(3, 5)], sems.at[1]))
    send[1].start()
    pl.loop(0, 2, unroll=True)(lambda at: deltas(at, rows, fresh, pool))

    @pl.loop(0, 3)
    def _(at):
        grads[at] = gradient(at, pool, 2 * rows).astype(jnp.bfloat16)

    send.append(pltpu.make_async_copy(grads, state.at[pl.ds(8, 3)], sems.at[2]))
    send[2].start()
    for copy in send:
        copy.wait()


def begin(table, near, far, maps, rate, initial):
    rows, width = near[0].shape
    count = len(near)
    anywhere = pl.BlockSpec(memory_space=pl.ANY)
    bfloat = functools.partial(pltpu.VMEM, dtype=jnp.bfloat16)
    operands = [*near, *far, maps]
    return pl.pallas_call(
        functools.partial(begin_kernel, count),
        grid_spec=pltpu.PrefetchScalarGridSpec(
            num_scalar_prefetch=1,
            grid=(),
            in_specs=[anywhere] * len(operands) + [pl.BlockSpec(memory_space=pltpu.VMEM), anywhere],
            out_specs=anywhere,
            scratch_shapes=[
                bfloat((count + 2, rows, width)),
                bfloat(maps.shape),
                bfloat(initial.shape),
                bfloat(initial.shape),
                bfloat((5, rows, width)),
                bfloat(initial.shape),
                bfloat((5, count * rows, width)),
                pltpu.SemaphoreType.DMA((count + 4,)),
            ],
        ),
        out_shape=jax.ShapeDtypeStruct((STATE, rows, width), jnp.bfloat16),
        compiler_params=pltpu.CompilerParams(vmem_limit_bytes=VMEM_LIMIT),
        cost_estimate=pl.CostEstimate(flops=1, bytes_accessed=1, transcendentals=0),
        name="begin",
    )(table, *operands, rate, initial)


def stage_kernel(counts, table, *refs):
    count, befores, earliers, begun = counts
    slots = count // 2 + begun
    blocks, refs = refs[:count], refs[count:]
    before, refs = refs[:befores], refs[befores:]
    earlier, refs = refs[:earliers], refs[earliers:]
    (maps, rate, initial), refs = refs[:3], refs[3:]
    results, new, refs = refs[:slots], refs[slots], refs[slots + 1 :]
    x, m, w, start, fresh, k, v, q, attended, pool, out, sems, *grads = refs
    rows, width = x.shape[1:]
    part = rows // 2
    updates, answers, first, there = table[0] > 0, table[1] > 0, table[2], table[3] > 0
    at_maps, at_start, at_weights, at_new, at_held, at_grads = (sems.at[count + 1 + at] for at in range(6))
    send_new = pltpu.make_async_copy(fresh, new, at_new)
    send = [pltpu.make_async_copy(out.at[at], results[at], sems.at[count + 7 + at]) for at in range(slots)]

    def span(at, size=rows):
        return pl.ds(pl.multiple_of(at, part), size)

    def answer():
        row = lax.broadcasted_iota(jnp.int32, (part, rows + part), 0)
        column = lax.broadcasted_iota(jnp.int32, (part, rows + part), 1)
        band = (column > row) & (column <= row + rows)

        @pl.loop(0, slots)
        def _(at):
            @pl.loop(0, 2, unroll=True)
            def _(half):
                own = span(part * half, part)
                base = rows * table[6 + 2 * at] + part * half
                scores = matmul_nt(q[at, own], k[span(base, rows + part)]) * (width ** -0.5)
                floor = jnp.where(first > 0, 0, rows - base)
                scores = jnp.where(band & (column >= floor), scores, -1e30)
                raised = jnp.exp(scores - jnp.max(scores, axis=1, keepdims=True))
                total = jnp.sum(raised, axis=1, keepdims=True)
                values = v[span(base, rows + part)]
                attended[own] = matmul(raised.astype(jnp.bfloat16), values) / total

            queries = unit_rows(q[at])
            gate = matmul(queries, fresh[0])
            up = matmul(queries, fresh[1])
            inner = (gate * logistic(gate) * up).astype(jnp.bfloat16)
            fast = matmul(inner, fresh[2]).astype(jnp.bfloat16).astype(jnp.float32)
            out[at] = (attended[...] + fast).astype(jnp.bfloat16)

        for copy in send:
            copy.start()
        for copy in send:
            copy.wait()

    @pl.when(updates | answers)
    def _():
        fetch(maps, m, at_maps)
        for at in range(count):
            fetch(blocks[at], x.at[at], sems.at[at])
        for at in range(befores):
            fetch(before[at], x.at[count], sems.at[count], there & (table[4] == at))
        for at in range(earliers):
            fetch(earlier[at].at[pl.ds(0, 3)], w, at_weights, table[5] == at)
        fetch(initial, start, at_start)
        if begun:
            for at in range(2):
                to = span(rows * (table[6 + count + at] + 1))
                fetch(earlier[0].at[4 + at], k.at[to], at_held)
                fetch(earlier[0].at[6 + at], v.at[to], at_held)
            fetch(earlier[0].at[3], q.at[slots - 1], at_held)
            fetch(earlier[0].at[pl.ds(8, 3)], grads[0], at_grads)
        fetched(m, at_maps)

        @pl.loop(0, count, unroll=True)
        def _(at):
            to = span(rows * (table[6 + at] + 1))

            def put_query(query_rows):
                q[at // 2] = query_rows

            def put_key_value(key_rows, value_rows):
                k[to] = key_rows
                v[to] = value_rows

            fetched(x.at[at], sems.at[at])
            learn(at, x, at, m, rate[pl.ds(first + table[6 + at], 1)], pool, put_query, put_key_value)

        @pl.when(there)
        def _():
            fetched(x.at[count], sems.at[count])
            k[:rows] = matmul(x[count], m[:, width : 2 * width]).astype(jnp.bfloat16)
            v[:rows] = matmul(x[count], m[:, 2 * width :]).astype(jnp.bfloat16)

        @pl.when(jnp.logical_not(there))
        def _():
            k[:rows] = jnp.zeros((rows, width), jnp.bfloat16)
            v[:rows] = jnp.zeros((rows, width), jnp.bfloat16)

        fetched(w, at_weights)
        fetched(start, at_start)
        if begun:
            fetched(k.at[pl.ds(0, 4 * rows)], at_held)
            fetched(q.at[0], at_held)
            fetched(grads[0], at_grads)

        @pl.when(updates)
        def _():
            pl.loop(0, count, unroll=True)(lambda at: deltas(at, rows, w, pool))

            @pl.loop(0, 3)
            def _(at):
                updated = w[at].astype(jnp.float32) + gradient(at, pool, count * rows)
                if begun:
                    updated = updated + grads[0][at].astype(jnp.float32)
                fresh[at] = renew(updated, start[at])

            send_new.start()

        @pl.when(jnp.logical_not(updates))
        def _():
            fresh[...] = w[...]

        pl.when(answers)(answer)
        pl.when(updates)(send_new.wait)


def stage(table, blocks, before, earlier, maps, rate, initial, begun=False, scale=24):
    count, begun = len(blocks), int(begun)
    rows, width = blocks[0].shape
    matrices = initial.shape
    bfloat = functools.partial(pltpu.VMEM, dtype=jnp.bfloat16)
    anywhere = pl.BlockSpec(memory_space=pl.ANY)
    slots = count // 2 + begun
    stretch = 2 * slots * rows
    operands = [*blocks, *before, *earlier, maps]
    return pl.pallas_call(
        functools.partial(stage_kernel, (count, len(before), len(earlier), begun)),
        grid_spec=pltpu.PrefetchScalarGridSpec(
            num_scalar_prefetch=1,
            grid=(),
            in_specs=[anywhere] * len(operands) + [pl.BlockSpec(memory_space=pltpu.VMEM), anywhere],
            out_specs=[anywhere] * (slots + 1),
            scratch_shapes=[
                bfloat((count + 1, rows, width)),
                bfloat(maps.shape),
                bfloat(matrices),
                bfloat(matrices),
                bfloat(matrices),
                bfloat((stretch + rows, width)),
                bfloat((stretch + rows, width)),
                bfloat((slots, rows, width)),
                pltpu.VMEM((rows, width), jnp.float32),
                bfloat((5, count * rows, width)),
                bfloat((slots, rows, width)),
                pltpu.SemaphoreType.DMA((count + 7 + slots,)),
            ]
            + [bfloat(matrices)] * begun,
        ),
        out_shape=[jax.ShapeDtypeStruct((rows, width), jnp.bfloat16)] * slots
        + [jax.ShapeDtypeStruct(matrices, jnp.bfloat16)],
        compiler_params=pltpu.CompilerParams(vmem_limit_bytes=VMEM_LIMIT),
        cost_estimate=pl.CostEstimate(flops=scale * stretch * width * width, bytes_accessed=scale * stretch * width, transcendentals=0),
        name="stage",
    )(table, *operands, rate, initial)


def after(array, *others):
    return lax.optimization_barrier((array, *others))[0]


def head_body(tokens, qkv_maps, rate_map, fast_init):
    rows = tokens.shape[0]
    heads, width = qkv_maps.shape[:2]
    groups = lax.axis_size("tok")
    chips = groups // 2
    slots = chips // 2
    last = chips - 1
    me = lax.axis_index("tok")
    chip, core = me // 2, me % 2
    is_first = (chip < slots).astype(jnp.int32)

    def swap(block, bits):
        return lax.ppermute(block, "tok", [(i, i ^ bits) for i in range(groups)])

    def piece(slot, source, index):
        return lax.dynamic_slice_in_dim(source, (index ^ slot) * width, width, 1)

    maps = lax.dynamic_index_in_dim(qkv_maps, chip, 0, False)
    initial = lax.dynamic_index_in_dim(fast_init, chip, 0, False)
    same = {slot: swap(piece(slot, tokens, chip), 2 * slot) for slot in range(1, slots)}
    same[last] = swap(piece(last, tokens, chip), 2 * last)
    terms = lax.dot_general(
        rate_map, tokens, (((0,), (1,)), ((), ())), preferred_element_type=jnp.float32
    )
    terms = lax.all_to_all(jnp.repeat(terms, 2, axis=0), ("head", "tok"), 0, 0, tiled=True)
    logits = jnp.sum(terms.reshape(-1, groups, rows), 0)
    rate = (rate_base * jax.nn.softplus(logits)).astype(jnp.bfloat16).astype(jnp.float32)
    source = after(tokens, *(same[slot] for slot in range(1, slots)))
    for slot in range(slots, last):
        same[slot] = swap(after(piece(slot, source, chip), same[last]), 2 * slot)
    same[0] = piece(0, source, chip)
    other = {slot: swap(same[slot], 1) for slot in range(slots)}

    def integers(entries):
        return jnp.stack([jnp.asarray(entry, jnp.int32) for entry in entries])

    def places(slot):
        return [2 * ((chip ^ slot) % slots) + core, 2 * ((chip ^ slot) % slots) + (1 - core)]

    def opening(slot):
        return 2 * slots * ((chip ^ slot) // slots)

    def table(slots_in, updates, answers, earlier):
        first = opening(slots_in[0])
        before = (chip ^ (slots - 1)) % slots
        flags = [updates, answers, first, (first > 0) & (core == 0), before, earlier]
        return integers(flags + [place for slot in slots_in for place in places(slot)])

    near_slots, far_slots = range(slots), range(slots, chips)
    near_blocks = [block for slot in near_slots for block in (same[slot], other[slot])]
    near_others = [other[slot] for slot in near_slots]
    shared = dict(maps=maps, rate=rate, initial=initial)
    other[last] = swap(same[last], 1)
    rates_in = [opening(slot) + place for slot in (*near_slots, last) for place in places(slot)]
    state = begin(integers([is_first] + rates_in), near_blocks, [same[last], other[last]], **shared)
    far_blocks = []
    for slot in far_slots[:-1]:
        same[slot] = after(same[slot], state)
        other[slot] = swap(same[slot], 1)
        far_blocks += [same[slot], other[slot]]
    *far_results, far_new = stage(
        table(far_slots, True, True, 0), far_blocks, near_others, [state], begun=True, **shared
    )
    *near_results, _ = stage(
        table(near_slots, 1 - is_first, True, 1 - is_first), near_blocks,
        [other[slot] for slot in far_slots], [state, far_new], **shared
    )
    results = near_results + far_results
    combined = jnp.zeros_like(tokens)
    for slot in (0, *far_slots, *range(1, slots)):
        result = swap(results[slot], 2 * slot) if slot else results[slot]
        combined = lax.dynamic_update_slice_in_dim(combined, result, (chip ^ slot) * width, 1)
    return combined


def body(tokens, qkv_maps, rate_map, fast_init):
    groups = lax.axis_size("tok")
    heads = qkv_maps.shape[0]
    powers = groups & (groups - 1) == 0 and groups > 2
    if powers and groups == 2 * heads and tokens.shape[0] == WINDOW:
        return head_body(tokens, qkv_maps, rate_map, fast_init)
    return general_body(tokens, qkv_maps, rate_map, fast_init)


def solution(mesh):
    in_specs = (
        P("tok", "head"),
        P("head", None, None),
        P("head", None),
        P("head", None, None, None),
    )
    out_specs = P("tok", "head")
    return jax.shard_map(body, mesh=mesh, in_specs=in_specs, out_specs=out_specs, check_vma=False)
```

```python
import functools

import jax
import jax.numpy as jnp
from jax import lax
from jax.experimental import pallas as pl
from jax.experimental.pallas import tpu as pltpu
from jax.sharding import PartitionSpec as P

WINDOW = 512


rate_base = 0.003
epsilon = 1e-06
VMEM_LIMIT = 40 * 1024 * 1024
STATE = 64


def from_behind(block, axis, distance):
    devices = range(lax.axis_size(axis))
    route = [(i - distance, i) for i in devices if i - distance in devices]
    return lax.ppermute(block, axis, route)


def rms_rows(matrix):
    matrix = matrix.astype(jnp.float32)
    return matrix / jnp.sqrt(jnp.mean(matrix * matrix, axis=-1, keepdims=True) + epsilon)


def renorm(updated, initial):
    target = jnp.sqrt(jnp.mean(initial * initial, axis=-1, keepdims=True) + epsilon)
    current = jnp.sqrt(jnp.mean(updated * updated, axis=-1, keepdims=True) + epsilon)
    return (updated * (target / current)).astype(jnp.bfloat16)


def band_attention(queries, key_rows, value_rows, query_pos, key_pos, score_scale):
    scores = (
        jnp.einsum("qhd,khd->hqk", queries, key_rows, preferred_element_type=jnp.float32)
        * score_scale
    )
    key_mask = (
        (key_pos[None, :] <= query_pos[:, None])
        & (key_pos[None, :] > query_pos[:, None] - WINDOW)
        & (key_pos[None, :] >= 0)
    )
    key_mask = key_mask[None]
    row_max = jnp.max(jnp.where(key_mask, scores, -1e30), axis=2, keepdims=True)
    raised = jnp.where(key_mask, jnp.exp(scores - row_max), 0.0)
    probs = (raised / jnp.sum(raised, axis=2, keepdims=True)).astype(jnp.bfloat16)
    return jnp.einsum("hqk,khd->qhd", probs, value_rows, preferred_element_type=jnp.float32)


def fast_gradient(weights, key_part, value_part, rate_part):
    pre_gate = jnp.einsum(
        "rhd,hde->rhe", key_part, weights[:, 0], preferred_element_type=jnp.float32
    )
    pre_up = jnp.einsum("rhd,hde->rhe", key_part, weights[:, 1], preferred_element_type=jnp.float32)
    sigma = jax.nn.sigmoid(pre_gate)
    gated = pre_gate * sigma
    hidden = (gated * pre_up).astype(jnp.bfloat16)
    target = (rate_part.astype(jnp.float32)[:, :, None] * value_part.astype(jnp.float32)).astype(
        jnp.bfloat16
    )
    grad_down = jnp.einsum("rhe,rhd->hed", hidden, target, preferred_element_type=jnp.float32)
    back_hidden = jnp.einsum(
        "rhd,hed->rhe", target, weights[:, 2], preferred_element_type=jnp.float32
    )
    gate_delta = (back_hidden * pre_up * sigma * (1.0 + pre_gate * (1.0 - sigma))).astype(
        jnp.bfloat16
    )
    up_delta = (back_hidden * gated).astype(jnp.bfloat16)
    grad_gate = jnp.einsum("rhd,rhe->hde", key_part, gate_delta, preferred_element_type=jnp.float32)
    grad_up = jnp.einsum("rhd,rhe->hde", key_part, up_delta, preferred_element_type=jnp.float32)
    return jnp.stack([grad_gate, grad_up, grad_down], 1)


def fast_apply(weights, query_part):
    app_gate = jnp.einsum(
        "rhd,hde->rhe", query_part, weights[:, 0], preferred_element_type=jnp.float32
    )
    app_up = jnp.einsum(
        "rhd,hde->rhe", query_part, weights[:, 1], preferred_element_type=jnp.float32
    )
    app_hidden = (app_gate * jax.nn.sigmoid(app_gate) * app_up).astype(jnp.bfloat16)
    result = jnp.einsum(
        "rhe,hed->rhd", app_hidden, weights[:, 2], preferred_element_type=jnp.float32
    )
    return result.astype(jnp.bfloat16)


def update_weights(weights, partial_value, initial):
    total = lax.psum(partial_value.astype(jnp.bfloat16), "tok").astype(jnp.float32)
    return renorm(weights.astype(jnp.float32) + total, initial)


def general_body(tokens, qkv_maps, rate_map, fast_init):
    tok_rows = tokens.shape[0]
    head_count = qkv_maps.shape[0]
    head_width = qkv_maps.shape[1]
    groups = lax.axis_size("tok")
    logit_terms = jnp.dot(tokens, rate_map, preferred_element_type=jnp.float32)
    logits = lax.psum_scatter(
        logit_terms.astype(jnp.bfloat16), "head", scatter_dimension=1, tiled=True
    ).astype(jnp.float32)
    rate = (rate_base * jax.nn.softplus(logits)).astype(jnp.bfloat16)
    inputs = tokens.reshape(tok_rows, head_count, head_width)
    projected = jnp.einsum("rhd,hde->rhe", inputs, qkv_maps, preferred_element_type=jnp.float32)
    queries = projected[:, :, :head_width].astype(jnp.bfloat16)
    key_rows = projected[:, :, head_width : 2 * head_width].astype(jnp.bfloat16)
    value_rows = projected[:, :, 2 * head_width :].astype(jnp.bfloat16)
    tail_rows = min(WINDOW, tok_rows)
    edge = jnp.stack([key_rows, value_rows], 0)
    distance = 0
    received = [from_behind(edge, "tok", distance + 1)]
    anchor = lax.axis_index("tok") * tok_rows
    offsets = jnp.arange(tail_rows, dtype=jnp.int32)
    distance = 1
    arrived = received[distance - 1]
    key_parts = [arrived[0]]
    value_parts = [arrived[1]]
    position_parts = [anchor - distance * tok_rows + tok_rows - tail_rows + offsets]
    local_pos = anchor + jnp.arange(tok_rows, dtype=jnp.int32)
    all_keys = jnp.concatenate(key_parts + [key_rows], 0)
    all_values = jnp.concatenate(value_parts + [value_rows], 0)
    all_pos = jnp.concatenate(position_parts + [local_pos], 0)
    attended = band_attention(
        queries, all_keys, all_values, local_pos, all_pos, head_width ** (-0.5)
    )
    q_norm = rms_rows(queries).astype(jnp.bfloat16)
    k_norm = rms_rows(key_rows).astype(jnp.bfloat16)
    initial = fast_init.astype(jnp.float32)
    weights = fast_init
    own_block = lax.axis_index("tok") // (groups // 2)
    fast_out = jnp.zeros_like(q_norm)
    for half_index in range(2):
        partial_value = fast_gradient(weights, k_norm, value_rows, rate)
        partial_value = jnp.where(own_block == half_index, partial_value, 0.0)
        weights = update_weights(weights, partial_value, initial)
        applied = fast_apply(weights, q_norm)
        fast_out = jnp.where(own_block == half_index, applied, fast_out)
    combined = (attended + fast_out.astype(jnp.float32)).astype(jnp.bfloat16)
    return combined.reshape(tok_rows, head_count * head_width)


def matmul(left, right):
    return jnp.dot(left, right, preferred_element_type=jnp.float32)


def matmul_nt(left, right):
    return lax.dot_general(left, right, (((1,), (1,)), ((), ())), preferred_element_type=jnp.float32)


def matmul_tn(left, right):
    return lax.dot_general(left, right, (((0,), (0,)), ((), ())), preferred_element_type=jnp.float32)


def unit_rows(rows):
    rows = rows.astype(jnp.float32)
    scale = lax.rsqrt(jnp.mean(rows * rows, axis=-1, keepdims=True) + epsilon)
    return (rows * scale).astype(jnp.bfloat16)


def logistic(a):
    return 0.5 * jnp.tanh(0.5 * a) + 0.5


def fetch(source, target, sem, when=None):
    copy = pltpu.make_async_copy(source, target, sem)
    if when is None:
        copy.start()
    else:
        pl.when(when)(copy.start)


def fetched(target, sem):
    pltpu.make_async_copy(target, target, sem).wait()


def learn(at, x, source, m, rate_row, pool, put_query, put_key_value):
    rows, width = x.shape[1:]
    here = pl.ds(pl.multiple_of(rows * at, rows), rows)
    key_rows = matmul(x[source], m[:, width : 2 * width]).astype(jnp.bfloat16)
    value_rows = matmul(x[source], m[:, 2 * width :]).astype(jnp.bfloat16)
    if put_key_value is not None:
        put_key_value(key_rows, value_rows)
    pool[0, here] = unit_rows(key_rows)
    spread = jnp.broadcast_to(rate_row, (128, rows)).T
    spread = jnp.concatenate([spread] * (width // 128), 1)
    pool[2, here] = (spread * value_rows.astype(jnp.float32)).astype(jnp.bfloat16)

    if put_query is not None:

        @pl.when(at % 2 == 0)
        def _():
            put_query(matmul(x[source], m[:, :width]).astype(jnp.bfloat16))


def deltas(at, rows, w, pool, both=None):
    here = pl.ds(pl.multiple_of(rows * at, rows), rows)
    gate = matmul(pool[0, here], w[0])
    up = matmul(pool[0, here], w[1])
    back = matmul_nt(pool[2, here], w[2])
    sigma = logistic(gate)
    gated = gate * sigma
    pool[1, here] = (gated * up).astype(jnp.bfloat16)
    width = gate.shape[1]
    gate_delta = (back * up * sigma * (1.0 + gate * (1.0 - sigma))).astype(jnp.bfloat16)
    up_delta = (back * gated).astype(jnp.bfloat16)
    if both is None:
        pool[3, here] = gate_delta
        pool[4, here] = up_delta
    else:
        both[here, :width] = gate_delta
        both[here, width:] = up_delta


def gradient(at, pool, rows):
    return matmul_tn(pool[at // 2, :rows], pool[jnp.where(at == 2, 2, 3 + at), :rows])


def gradients(rows, pool, both, take):
    width = pool.shape[2]
    grads = matmul_tn(pool[0, :rows], both[:rows])
    take(0, grads[:, :width])
    take(1, grads[:, width:])
    take(2, matmul_tn(pool[1, :rows], pool[2, :rows]))


def renew(updated, initial):
    origin = initial.astype(jnp.float32)
    wanted = jnp.mean(origin * origin, axis=-1, keepdims=True) + epsilon
    held = jnp.mean(updated * updated, axis=-1, keepdims=True) + epsilon
    return (updated * (jnp.sqrt(wanted) * lax.rsqrt(held))).astype(jnp.bfloat16)


def begin_kernel(count, table, *refs):
    near, far, refs = refs[:count], refs[count : count + 2], refs[count + 2 :]
    maps, rate, initial, state, x, m, w, fresh, kept, grads, pool, both, sems = refs
    rows = x.shape[1]
    updates = table[0] > 0
    fetch(maps, m, sems.at[count + 2])
    for at in range(count):
        fetch(near[at], x.at[at], sems.at[at], updates)
    for at in range(2):
        fetch(far[at], x.at[count + at], sems.at[count + at])
    fetch(initial, w, sems.at[count + 3])
    fetched(m, sems.at[count + 2])

    @pl.when(updates)
    def _():
        @pl.loop(0, count, unroll=True)
        def _(at):
            fetched(x.at[at], sems.at[at])
            learn(at, x, at, m, rate[pl.ds(table[1 + at], 1)], pool, None, None)

        fetched(w, sems.at[count + 3])
        pl.loop(0, count, unroll=True)(lambda at: deltas(at, rows, w, pool, both))

        def take(at, grad):
            fresh[at] = renew(w[at].astype(jnp.float32) + grad, w[at])

        gradients(count * rows, pool, both, take)

    @pl.when(jnp.logical_not(updates))
    def _():
        fetched(w, sems.at[count + 3])
        fresh[...] = w[...]

    send = [pltpu.make_async_copy(fresh, state.at[pl.ds(0, 3)], sems.at[0])]
    send[0].start()

    @pl.loop(0, 2, unroll=True)
    def _(at):
        def put_query(query_rows):
            kept[0] = query_rows

        def put_key_value(key_rows, value_rows):
            kept[1 + at] = key_rows
            kept[3 + at] = value_rows

        fetched(x.at[count + at], sems.at[count + at])
        learn(at, x, count + at, m, rate[pl.ds(table[1 + count + at], 1)], pool, put_query, put_key_value)

    send.append(pltpu.make_async_copy(kept, state.at[pl.ds(3, 5)], sems.at[1]))
    send[1].start()
    pl.loop(0, 2, unroll=True)(lambda at: deltas(at, rows, fresh, pool, both))

    def take(at, grad):
        grads[at] = grad.astype(jnp.bfloat16)

    gradients(2 * rows, pool, both, take)

    send.append(pltpu.make_async_copy(grads, state.at[pl.ds(8, 3)], sems.at[2]))
    send[2].start()
    for copy in send:
        copy.wait()


def begin(table, near, far, maps, rate, initial):
    rows, width = near[0].shape
    count = len(near)
    anywhere = pl.BlockSpec(memory_space=pl.ANY)
    bfloat = functools.partial(pltpu.VMEM, dtype=jnp.bfloat16)
    operands = [*near, *far, maps]
    return pl.pallas_call(
        functools.partial(begin_kernel, count),
        grid_spec=pltpu.PrefetchScalarGridSpec(
            num_scalar_prefetch=1,
            grid=(),
            in_specs=[anywhere] * len(operands) + [pl.BlockSpec(memory_space=pltpu.VMEM), anywhere],
            out_specs=anywhere,
            scratch_shapes=[
                bfloat((count + 2, rows, width)),
                bfloat(maps.shape),
                bfloat(initial.shape),
                bfloat(initial.shape),
                bfloat((5, rows, width)),
                bfloat(initial.shape),
                bfloat((3, count * rows, width)),
                bfloat((count * rows, 2 * width)),
                pltpu.SemaphoreType.DMA((count + 4,)),
            ],
        ),
        out_shape=jax.ShapeDtypeStruct((STATE, rows, width), jnp.bfloat16),
        compiler_params=pltpu.CompilerParams(vmem_limit_bytes=VMEM_LIMIT),
        cost_estimate=pl.CostEstimate(flops=1, bytes_accessed=1, transcendentals=0),
        name="begin",
    )(table, *operands, rate, initial)


def stage_kernel(counts, table, *refs):
    count, befores, begun = counts
    slots = count // 2 + begun
    wanted = count // 2
    blocks, refs = refs[:count], refs[count:]
    before, refs = refs[:befores], refs[befores:]
    state, refs = refs[0], refs[1:]
    (maps, rate, initial), refs = refs[:3], refs[3:]
    results, new, refs = refs[:wanted], refs[wanted : wanted + begun], refs[wanted + begun :]
    x, m, w, start, fresh, k, v, q, attended, pool, out, sems, *grads = refs
    rows, width = x.shape[1:]
    part = rows // 2
    updates, answers, first, there = table[0] > 0, table[1] > 0, table[2], table[3] > 0
    at_maps, at_start, at_weights, at_new, at_held, at_grads = (sems.at[count + 1 + at] for at in range(6))
    if begun:
        send_new = pltpu.make_async_copy(fresh, new[0].at[pl.ds(11, 3)], at_new)
    send = [pltpu.make_async_copy(out.at[at], results[at], sems.at[count + 7 + at]) for at in range(wanted)]

    def span(at, size=rows):
        return pl.ds(pl.multiple_of(at, part), size)

    def answer():
        row = lax.broadcasted_iota(jnp.int32, (part, rows + part), 0)
        column = lax.broadcasted_iota(jnp.int32, (part, rows + part), 1)
        band = (column > row) & (column <= row + rows)

        @pl.loop(0, wanted)
        def _(at):
            @pl.loop(0, 2, unroll=begun > 0)
            def _(half):
                own = span(part * half, part)
                base = rows * table[6 + 2 * at] + part * half
                scores = matmul_nt(q[at, own], k[span(base, rows + part)]) * (width ** -0.5)
                floor = jnp.where(first > 0, 0, rows - base)
                scores = jnp.where(band & (column >= floor), scores, -1e30)
                raised = jnp.exp(scores - jnp.max(scores, axis=1, keepdims=True))
                total = jnp.sum(raised, axis=1, keepdims=True)
                values = v[span(base, rows + part)]
                attended[own] = matmul(raised.astype(jnp.bfloat16), values) / total

            queries = unit_rows(q[at])
            gate = matmul(queries, fresh[0])
            up = matmul(queries, fresh[1])
            inner = (gate * logistic(gate) * up).astype(jnp.bfloat16)
            fast = matmul(inner, fresh[2]).astype(jnp.bfloat16).astype(jnp.float32)
            out[at] = (attended[...] + fast).astype(jnp.bfloat16)

        for copy in send:
            copy.start()
        for copy in send:
            copy.wait()

    @pl.when(updates | answers)
    def _():
        fetch(maps, m, at_maps)
        for at in range(count):
            fetch(blocks[at], x.at[at], sems.at[at])
        for at in range(befores):
            fetch(before[at], x.at[count], sems.at[count], there & (table[4] == at))
        fetch(state.at[pl.ds(table[5], 3)], w, at_weights)
        fetch(initial, start, at_start)
        if begun:
            to = span(rows * (table[6 + count + 1] + 1))
            fetch(state.at[5], k.at[to], at_held)
            fetch(state.at[7], v.at[to], at_held)
            fetch(state.at[pl.ds(8, 3)], grads[0], at_grads)
        fetched(m, at_maps)

        @pl.loop(0, count, unroll=begun > 0)
        def _(at):
            to = span(rows * (table[6 + at] + 1))

            def put_query(query_rows):
                q[at // 2] = query_rows

            def put_key_value(key_rows, value_rows):
                k[to] = key_rows
                v[to] = value_rows

            fetched(x.at[at], sems.at[at])
            learn(at, x, at, m, rate[pl.ds(first + table[6 + at], 1)], pool, put_query, put_key_value)

        @pl.when(there)
        def _():
            fetched(x.at[count], sems.at[count])
            k[:rows] = matmul(x[count], m[:, width : 2 * width]).astype(jnp.bfloat16)
            v[:rows] = matmul(x[count], m[:, 2 * width :]).astype(jnp.bfloat16)

        @pl.when(jnp.logical_not(there))
        def _():
            k[:rows] = jnp.zeros((rows, width), jnp.bfloat16)
            v[:rows] = jnp.zeros((rows, width), jnp.bfloat16)

        fetched(w, at_weights)
        fetched(start, at_start)
        if begun:
            fetched(k.at[pl.ds(0, 2 * rows)], at_held)
            fetched(grads[0], at_grads)

        @pl.when(updates)
        def _():
            pl.loop(0, count, unroll=begun > 0)(lambda at: deltas(at, rows, w, pool))

            @pl.loop(0, 3)
            def _(at):
                updated = w[at].astype(jnp.float32) + gradient(at, pool, count * rows)
                if begun:
                    updated = updated + grads[0][at].astype(jnp.float32)
                fresh[at] = renew(updated, start[at])

            if begun:
                send_new.start()

        @pl.when(jnp.logical_not(updates))
        def _():
            fresh[...] = w[...]

        pl.when(answers)(answer)
        if begun:
            send_new.wait()


def stage(table, blocks, before, state, maps, rate, initial, begun=False, scale=24):
    count, begun = len(blocks), int(begun)
    rows, width = blocks[0].shape
    matrices = initial.shape
    bfloat = functools.partial(pltpu.VMEM, dtype=jnp.bfloat16)
    anywhere = pl.BlockSpec(memory_space=pl.ANY)
    slots = count // 2 + begun
    stretch = 2 * slots * rows
    wanted = count // 2
    operands = [*blocks, *before, state, maps]
    return pl.pallas_call(
        functools.partial(stage_kernel, (count, len(before), begun)),
        grid_spec=pltpu.PrefetchScalarGridSpec(
            num_scalar_prefetch=1,
            grid=(),
            in_specs=[anywhere] * len(operands) + [pl.BlockSpec(memory_space=pltpu.VMEM), anywhere],
            out_specs=[anywhere] * (wanted + begun),
            scratch_shapes=[
                bfloat((count + 1, rows, width)),
                bfloat(maps.shape),
                bfloat(matrices),
                bfloat(matrices),
                bfloat(matrices),
                bfloat((stretch + rows, width)),
                bfloat((stretch + rows, width)),
                bfloat((wanted, rows, width)),
                pltpu.VMEM((rows, width), jnp.float32),
                bfloat((5, count * rows, width)),
                bfloat((wanted, rows, width)),
                pltpu.SemaphoreType.DMA((count + 7 + wanted,)),
            ]
            + [bfloat(matrices)] * begun,
        ),
        out_shape=[jax.ShapeDtypeStruct((rows, width), jnp.bfloat16)] * wanted
        + [jax.ShapeDtypeStruct(state.shape, state.dtype)] * begun,
        input_output_aliases={1 + count + len(before): wanted} if begun else {},
        compiler_params=pltpu.CompilerParams(vmem_limit_bytes=VMEM_LIMIT),
        cost_estimate=pl.CostEstimate(flops=scale * stretch * width * width, bytes_accessed=scale * stretch * width, transcendentals=0),
        name="stage",
    )(table, *operands, rate, initial)


def banded(queries, keys, values, floor):
    part, window = queries.shape[0], keys.shape[0]
    row = lax.broadcasted_iota(jnp.int32, (part, window), 0)
    column = lax.broadcasted_iota(jnp.int32, (part, window), 1)
    band = (column > row) & (column <= row + window - part) & (column >= floor)
    scores = matmul_nt(queries, keys) * (queries.shape[1] ** -0.5)
    scores = jnp.where(band, scores, -1e30)
    raised = jnp.exp(scores - jnp.max(scores, axis=1, keepdims=True))
    total = jnp.sum(raised, axis=1, keepdims=True)
    return matmul(raised.astype(jnp.bfloat16), values) / total


def finish_kernel(befores, table, *refs):
    before, refs = refs[:befores], refs[befores:]
    maps, state, result, x, m, w, q, k, v, attended, out, sems = refs
    rows, width = x.shape
    part = rows // 2
    there = table[0] > 0
    for at in range(befores):
        fetch(before[at], x, sems.at[0], there & (table[1] == at))
    fetch(maps, m, sems.at[1], there)
    fetch(state.at[3], q, sems.at[2])
    fetch(state.at[4], k.at[pl.ds(rows, rows)], sems.at[3])
    fetch(state.at[6], v.at[pl.ds(rows, rows)], sems.at[4])
    fetch(state.at[pl.ds(11, 3)], w, sems.at[5])

    @pl.when(there)
    def _():
        fetched(x, sems.at[0])
        fetched(m, sems.at[1])
        k[:rows] = matmul(x[...], m[:, width : 2 * width]).astype(jnp.bfloat16)
        v[:rows] = matmul(x[...], m[:, 2 * width :]).astype(jnp.bfloat16)

    @pl.when(jnp.logical_not(there))
    def _():
        k[:rows] = jnp.zeros((rows, width), jnp.bfloat16)
        v[:rows] = jnp.zeros((rows, width), jnp.bfloat16)

    fetched(q, sems.at[2])
    fetched(q, sems.at[3])
    fetched(q, sems.at[4])

    @pl.loop(0, 2)
    def _(half):
        first = part * half
        window = pl.ds(first, rows + part)
        floor = jnp.where(there, 0, rows - first)
        attended[pl.ds(first, part)] = banded(q[pl.ds(first, part)], k[window], v[window], floor)

    fetched(w, sems.at[5])
    queries = unit_rows(q[...])
    gate = matmul(queries, w[0])
    up = matmul(queries, w[1])
    inner = (gate * logistic(gate) * up).astype(jnp.bfloat16)
    fast = matmul(inner, w[2]).astype(jnp.bfloat16).astype(jnp.float32)
    out[...] = (attended[...] + fast).astype(jnp.bfloat16)
    copy = pltpu.make_async_copy(out, result, sems.at[0])
    copy.start()
    copy.wait()


def finish(table, before, maps, state):
    rows, width = before[0].shape
    anywhere = pl.BlockSpec(memory_space=pl.ANY)
    bfloat = functools.partial(pltpu.VMEM, dtype=jnp.bfloat16)
    return pl.pallas_call(
        functools.partial(finish_kernel, len(before)),
        grid_spec=pltpu.PrefetchScalarGridSpec(
            num_scalar_prefetch=1,
            grid=(),
            in_specs=[anywhere] * (len(before) + 2),
            out_specs=anywhere,
            scratch_shapes=[
                bfloat((rows, width)),
                bfloat(maps.shape),
                bfloat((3,) + state.shape[1:]),
                bfloat((rows, width)),
                bfloat((2 * rows, width)),
                bfloat((2 * rows, width)),
                pltpu.VMEM((rows, width), jnp.float32),
                bfloat((rows, width)),
                pltpu.SemaphoreType.DMA((6,)),
            ],
        ),
        out_shape=jax.ShapeDtypeStruct((rows, width), jnp.bfloat16),
        compiler_params=pltpu.CompilerParams(vmem_limit_bytes=VMEM_LIMIT),
        cost_estimate=pl.CostEstimate(flops=1, bytes_accessed=1, transcendentals=0),
        name="finish",
    )(table, *before, maps, state)


def after(array, *others):
    return lax.optimization_barrier((array, *others))[0]


def head_body(tokens, qkv_maps, rate_map, fast_init):
    rows = tokens.shape[0]
    heads, width = qkv_maps.shape[:2]
    groups = lax.axis_size("tok")
    chips = groups // 2
    slots = chips // 2
    last = chips - 1
    me = lax.axis_index("tok")
    chip, core = me // 2, me % 2
    is_first = (chip < slots).astype(jnp.int32)

    def swap(block, bits):
        return lax.ppermute(block, "tok", [(i, i ^ bits) for i in range(groups)])

    def piece(slot, source, index):
        return lax.dynamic_slice_in_dim(source, (index ^ slot) * width, width, 1)

    maps = lax.dynamic_index_in_dim(qkv_maps, chip, 0, False)
    initial = lax.dynamic_index_in_dim(fast_init, chip, 0, False)
    same = {slot: swap(piece(slot, tokens, chip), 2 * slot) for slot in range(1, slots)}
    same[last] = swap(piece(last, tokens, chip), 2 * last)
    terms = lax.dot_general(
        rate_map, tokens, (((0,), (1,)), ((), ())), preferred_element_type=jnp.float32
    )
    terms = lax.all_to_all(jnp.repeat(terms, 2, axis=0), ("head", "tok"), 0, 0, tiled=True)
    logits = jnp.sum(terms.reshape(-1, groups, rows), 0)
    rate = (rate_base * jax.nn.softplus(logits)).astype(jnp.bfloat16).astype(jnp.float32)
    source = after(tokens, *(same[slot] for slot in range(1, slots)))
    for slot in range(slots, last):
        same[slot] = swap(after(piece(slot, source, chip), same[last]), 2 * slot)
    same[0] = piece(0, source, chip)
    other = {slot: swap(same[slot], 1) for slot in range(slots)}

    def integers(entries):
        return jnp.stack([jnp.asarray(entry, jnp.int32) for entry in entries])

    def places(slot):
        return [2 * ((chip ^ slot) % slots) + core, 2 * ((chip ^ slot) % slots) + (1 - core)]

    def opening(slot):
        return 2 * slots * ((chip ^ slot) // slots)

    def table(slots_in, updates, answers, weights_at):
        first = opening(slots_in[0])
        before = (chip ^ (slots - 1)) % slots
        flags = [updates, answers, first, (first > 0) & (core == 0), before, weights_at]
        return integers(flags + [place for slot in slots_in for place in places(slot)])

    near_slots, far_slots = range(slots), range(slots, chips)
    near_blocks = [block for slot in near_slots for block in (same[slot], other[slot])]
    near_others = [other[slot] for slot in near_slots]
    shared = dict(maps=maps, rate=rate, initial=initial)
    other[last] = swap(same[last], 1)
    rates_in = [opening(slot) + place for slot in (*near_slots, last) for place in places(slot)]
    state = begin(integers([is_first] + rates_in), near_blocks, [same[last], other[last]], **shared)
    far_blocks = []
    for slot in far_slots[:-1]:
        same[slot] = after(same[slot], state)
        other[slot] = swap(same[slot], 1)
        far_blocks += [same[slot], other[slot]]
    *far_results, state = stage(
        table(far_slots, True, True, 0), far_blocks, near_others, state, begun=True, **shared
    )
    near_results = stage(
        table(near_slots, 1 - is_first, True, 11 * (1 - is_first)), near_blocks,
        [other[slot] for slot in far_slots], state, scale=0, **shared
    )
    at = chip ^ last
    place = jnp.where(core == 1, at, at - 1)
    last_result = finish(
        integers([place >= 0, chip ^ jnp.maximum(place, 0)]), [other[slot] for slot in range(chips)], maps, state
    )
    results = [*near_results, *far_results, last_result]
    combined = jnp.zeros_like(tokens)
    for slot in (*far_slots[:-1], 0, last, *range(1, slots)):
        result = swap(results[slot], 2 * slot) if slot else results[slot]
        combined = lax.dynamic_update_slice_in_dim(combined, result, (chip ^ slot) * width, 1)
    return combined


def body(tokens, qkv_maps, rate_map, fast_init):
    groups = lax.axis_size("tok")
    heads = qkv_maps.shape[0]
    powers = groups & (groups - 1) == 0 and groups > 2
    if powers and groups == 2 * heads and tokens.shape[0] == WINDOW:
        return head_body(tokens, qkv_maps, rate_map, fast_init)
    return general_body(tokens, qkv_maps, rate_map, fast_init)


def solution(mesh):
    in_specs = (
        P("tok", "head"),
        P("head", None, None),
        P("head", None),
        P("head", None, None, None),
    )
    out_specs = P("tok", "head")
    return jax.shard_map(body, mesh=mesh, in_specs=in_specs, out_specs=out_specs, check_vma=False)
```

```python
import functools

import jax
import jax.numpy as jnp
from jax import lax
from jax.experimental import pallas as pl
from jax.experimental.pallas import tpu as pltpu
from jax.sharding import PartitionSpec as P

WINDOW = 512


rate_base = 0.003
epsilon = 1e-06
VMEM_LIMIT = 40 * 1024 * 1024
STATE = 64


def from_behind(block, axis, distance):
    devices = range(lax.axis_size(axis))
    route = [(i - distance, i) for i in devices if i - distance in devices]
    return lax.ppermute(block, axis, route)


def rms_rows(matrix):
    matrix = matrix.astype(jnp.float32)
    return matrix / jnp.sqrt(jnp.mean(matrix * matrix, axis=-1, keepdims=True) + epsilon)


def renorm(updated, initial):
    target = jnp.sqrt(jnp.mean(initial * initial, axis=-1, keepdims=True) + epsilon)
    current = jnp.sqrt(jnp.mean(updated * updated, axis=-1, keepdims=True) + epsilon)
    return (updated * (target / current)).astype(jnp.bfloat16)


def band_attention(queries, key_rows, value_rows, query_pos, key_pos, score_scale):
    scores = (
        jnp.einsum("qhd,khd->hqk", queries, key_rows, preferred_element_type=jnp.float32)
        * score_scale
    )
    key_mask = (
        (key_pos[None, :] <= query_pos[:, None])
        & (key_pos[None, :] > query_pos[:, None] - WINDOW)
        & (key_pos[None, :] >= 0)
    )
    key_mask = key_mask[None]
    row_max = jnp.max(jnp.where(key_mask, scores, -1e30), axis=2, keepdims=True)
    raised = jnp.where(key_mask, jnp.exp(scores - row_max), 0.0)
    probs = (raised / jnp.sum(raised, axis=2, keepdims=True)).astype(jnp.bfloat16)
    return jnp.einsum("hqk,khd->qhd", probs, value_rows, preferred_element_type=jnp.float32)


def fast_gradient(weights, key_part, value_part, rate_part):
    pre_gate = jnp.einsum(
        "rhd,hde->rhe", key_part, weights[:, 0], preferred_element_type=jnp.float32
    )
    pre_up = jnp.einsum("rhd,hde->rhe", key_part, weights[:, 1], preferred_element_type=jnp.float32)
    sigma = jax.nn.sigmoid(pre_gate)
    gated = pre_gate * sigma
    hidden = (gated * pre_up).astype(jnp.bfloat16)
    target = (rate_part.astype(jnp.float32)[:, :, None] * value_part.astype(jnp.float32)).astype(
        jnp.bfloat16
    )
    grad_down = jnp.einsum("rhe,rhd->hed", hidden, target, preferred_element_type=jnp.float32)
    back_hidden = jnp.einsum(
        "rhd,hed->rhe", target, weights[:, 2], preferred_element_type=jnp.float32
    )
    gate_delta = (back_hidden * pre_up * sigma * (1.0 + pre_gate * (1.0 - sigma))).astype(
        jnp.bfloat16
    )
    up_delta = (back_hidden * gated).astype(jnp.bfloat16)
    grad_gate = jnp.einsum("rhd,rhe->hde", key_part, gate_delta, preferred_element_type=jnp.float32)
    grad_up = jnp.einsum("rhd,rhe->hde", key_part, up_delta, preferred_element_type=jnp.float32)
    return jnp.stack([grad_gate, grad_up, grad_down], 1)


def fast_apply(weights, query_part):
    app_gate = jnp.einsum(
        "rhd,hde->rhe", query_part, weights[:, 0], preferred_element_type=jnp.float32
    )
    app_up = jnp.einsum(
        "rhd,hde->rhe", query_part, weights[:, 1], preferred_element_type=jnp.float32
    )
    app_hidden = (app_gate * jax.nn.sigmoid(app_gate) * app_up).astype(jnp.bfloat16)
    result = jnp.einsum(
        "rhe,hed->rhd", app_hidden, weights[:, 2], preferred_element_type=jnp.float32
    )
    return result.astype(jnp.bfloat16)


def update_weights(weights, partial_value, initial):
    total = lax.psum(partial_value.astype(jnp.bfloat16), "tok").astype(jnp.float32)
    return renorm(weights.astype(jnp.float32) + total, initial)


def general_body(tokens, qkv_maps, rate_map, fast_init):
    tok_rows = tokens.shape[0]
    head_count = qkv_maps.shape[0]
    head_width = qkv_maps.shape[1]
    groups = lax.axis_size("tok")
    logit_terms = jnp.dot(tokens, rate_map, preferred_element_type=jnp.float32)
    logits = lax.psum_scatter(
        logit_terms.astype(jnp.bfloat16), "head", scatter_dimension=1, tiled=True
    ).astype(jnp.float32)
    rate = (rate_base * jax.nn.softplus(logits)).astype(jnp.bfloat16)
    inputs = tokens.reshape(tok_rows, head_count, head_width)
    projected = jnp.einsum("rhd,hde->rhe", inputs, qkv_maps, preferred_element_type=jnp.float32)
    queries = projected[:, :, :head_width].astype(jnp.bfloat16)
    key_rows = projected[:, :, head_width : 2 * head_width].astype(jnp.bfloat16)
    value_rows = projected[:, :, 2 * head_width :].astype(jnp.bfloat16)
    tail_rows = min(WINDOW, tok_rows)
    edge = jnp.stack([key_rows, value_rows], 0)
    distance = 0
    received = [from_behind(edge, "tok", distance + 1)]
    anchor = lax.axis_index("tok") * tok_rows
    offsets = jnp.arange(tail_rows, dtype=jnp.int32)
    distance = 1
    arrived = received[distance - 1]
    key_parts = [arrived[0]]
    value_parts = [arrived[1]]
    position_parts = [anchor - distance * tok_rows + tok_rows - tail_rows + offsets]
    local_pos = anchor + jnp.arange(tok_rows, dtype=jnp.int32)
    all_keys = jnp.concatenate(key_parts + [key_rows], 0)
    all_values = jnp.concatenate(value_parts + [value_rows], 0)
    all_pos = jnp.concatenate(position_parts + [local_pos], 0)
    attended = band_attention(
        queries, all_keys, all_values, local_pos, all_pos, head_width ** (-0.5)
    )
    q_norm = rms_rows(queries).astype(jnp.bfloat16)
    k_norm = rms_rows(key_rows).astype(jnp.bfloat16)
    initial = fast_init.astype(jnp.float32)
    weights = fast_init
    own_block = lax.axis_index("tok") // (groups // 2)
    fast_out = jnp.zeros_like(q_norm)
    for half_index in range(2):
        partial_value = fast_gradient(weights, k_norm, value_rows, rate)
        partial_value = jnp.where(own_block == half_index, partial_value, 0.0)
        weights = update_weights(weights, partial_value, initial)
        applied = fast_apply(weights, q_norm)
        fast_out = jnp.where(own_block == half_index, applied, fast_out)
    combined = (attended + fast_out.astype(jnp.float32)).astype(jnp.bfloat16)
    return combined.reshape(tok_rows, head_count * head_width)


def matmul(left, right):
    return jnp.dot(left, right, preferred_element_type=jnp.float32)


def matmul_nt(left, right):
    return lax.dot_general(left, right, (((1,), (1,)), ((), ())), preferred_element_type=jnp.float32)


def matmul_tn(left, right):
    return lax.dot_general(left, right, (((0,), (0,)), ((), ())), preferred_element_type=jnp.float32)


def unit_rows(rows):
    rows = rows.astype(jnp.float32)
    scale = lax.rsqrt(jnp.mean(rows * rows, axis=-1, keepdims=True) + epsilon)
    return (rows * scale).astype(jnp.bfloat16)


def logistic(a):
    return 0.5 * jnp.tanh(0.5 * a) + 0.5


def fetch(source, target, sem, when=None):
    copy = pltpu.make_async_copy(source, target, sem)
    if when is None:
        copy.start()
    else:
        pl.when(when)(copy.start)


def fetched(target, sem):
    pltpu.make_async_copy(target, target, sem).wait()


def learn(at, x, source, m, rate_row, pool, put_query, put_key_value):
    rows, width = x.shape[1:]
    here = pl.ds(pl.multiple_of(rows * at, rows), rows)
    key_rows = matmul(x[source], m[:, width : 2 * width]).astype(jnp.bfloat16)
    value_rows = matmul(x[source], m[:, 2 * width :]).astype(jnp.bfloat16)
    if put_key_value is not None:
        put_key_value(key_rows, value_rows)
    pool[0, here] = unit_rows(key_rows)
    spread = jnp.broadcast_to(rate_row, (128, rows)).T
    spread = jnp.concatenate([spread] * (width // 128), 1)
    pool[2, here] = (spread * value_rows.astype(jnp.float32)).astype(jnp.bfloat16)

    if put_query is not None:

        @pl.when(at % 2 == 0)
        def _():
            put_query(matmul(x[source], m[:, :width]).astype(jnp.bfloat16))


def deltas(at, rows, w, pool, both=None):
    here = pl.ds(pl.multiple_of(rows * at, rows), rows)
    gate = matmul(pool[0, here], w[0]).astype(jnp.bfloat16)
    up = matmul(pool[0, here], w[1]).astype(jnp.bfloat16)
    back = matmul_nt(pool[2, here], w[2]).astype(jnp.bfloat16)
    sigma = logistic(gate)
    gated = gate * sigma
    pool[1, here] = gated * up
    width = gate.shape[1]
    gate_delta = back * up * sigma * (1 + gate * (1 - sigma))
    up_delta = back * gated
    if both is None:
        pool[3, here] = gate_delta
        pool[4, here] = up_delta
    else:
        both[here, :width] = gate_delta
        both[here, width:] = up_delta


def gradient(at, pool, rows):
    return matmul_tn(pool[at // 2, :rows], pool[jnp.where(at == 2, 2, 3 + at), :rows])


def gradients(rows, pool, both, take):
    width = pool.shape[2]
    grads = matmul_tn(pool[0, :rows], both[:rows])
    take(0, grads[:, :width])
    take(1, grads[:, width:])
    take(2, matmul_tn(pool[1, :rows], pool[2, :rows]))


def renew(updated, initial):
    origin = initial.astype(jnp.float32)
    wanted = jnp.mean(origin * origin, axis=-1, keepdims=True) + epsilon
    held = jnp.mean(updated * updated, axis=-1, keepdims=True) + epsilon
    return (updated * (jnp.sqrt(wanted) * lax.rsqrt(held))).astype(jnp.bfloat16)


def begin_kernel(count, table, *refs):
    near, far, refs = refs[:count], refs[count : count + 2], refs[count + 2 :]
    maps, rate, initial, state, x, m, w, fresh, kept, grads, pool, both, sems = refs
    rows = x.shape[1]
    updates = table[0] > 0
    fetch(maps, m, sems.at[count + 2])
    for at in range(count):
        fetch(near[at], x.at[at], sems.at[at], updates)
    for at in range(2):
        fetch(far[at], x.at[count + at], sems.at[count + at])
    fetch(initial, w, sems.at[count + 3])
    fetched(m, sems.at[count + 2])

    @pl.when(updates)
    def _():
        @pl.loop(0, count, unroll=True)
        def _(at):
            fetched(x.at[at], sems.at[at])
            learn(at, x, at, m, rate[pl.ds(table[1 + at], 1)], pool, None, None)

        fetched(w, sems.at[count + 3])
        pl.loop(0, count, unroll=True)(lambda at: deltas(at, rows, w, pool, both))

        def take(at, grad):
            fresh[at] = renew(w[at].astype(jnp.float32) + grad, w[at])

        gradients(count * rows, pool, both, take)

    @pl.when(jnp.logical_not(updates))
    def _():
        fetched(w, sems.at[count + 3])
        fresh[...] = w[...]

    send = [pltpu.make_async_copy(fresh, state.at[pl.ds(0, 3)], sems.at[0])]
    send[0].start()

    @pl.loop(0, 2, unroll=True)
    def _(at):
        def put_query(query_rows):
            kept[0] = query_rows

        def put_key_value(key_rows, value_rows):
            kept[1 + at] = key_rows
            kept[3 + at] = value_rows

        fetched(x.at[count + at], sems.at[count + at])
        learn(at, x, count + at, m, rate[pl.ds(table[1 + count + at], 1)], pool, put_query, put_key_value)

    send.append(pltpu.make_async_copy(kept, state.at[pl.ds(3, 5)], sems.at[1]))
    send[1].start()
    pl.loop(0, 2, unroll=True)(lambda at: deltas(at, rows, fresh, pool, both))

    def take(at, grad):
        grads[at] = grad.astype(jnp.bfloat16)

    gradients(2 * rows, pool, both, take)

    send.append(pltpu.make_async_copy(grads, state.at[pl.ds(8, 3)], sems.at[2]))
    send[2].start()
    for copy in send:
        copy.wait()


def begin(table, near, far, maps, rate, initial):
    rows, width = near[0].shape
    count = len(near)
    anywhere = pl.BlockSpec(memory_space=pl.ANY)
    bfloat = functools.partial(pltpu.VMEM, dtype=jnp.bfloat16)
    operands = [*near, *far, maps]
    return pl.pallas_call(
        functools.partial(begin_kernel, count),
        grid_spec=pltpu.PrefetchScalarGridSpec(
            num_scalar_prefetch=1,
            grid=(),
            in_specs=[anywhere] * len(operands) + [pl.BlockSpec(memory_space=pltpu.VMEM), anywhere],
            out_specs=anywhere,
            scratch_shapes=[
                bfloat((count + 2, rows, width)),
                bfloat(maps.shape),
                bfloat(initial.shape),
                bfloat(initial.shape),
                bfloat((5, rows, width)),
                bfloat(initial.shape),
                bfloat((3, count * rows, width)),
                bfloat((count * rows, 2 * width)),
                pltpu.SemaphoreType.DMA((count + 4,)),
            ],
        ),
        out_shape=jax.ShapeDtypeStruct((STATE, rows, width), jnp.bfloat16),
        compiler_params=pltpu.CompilerParams(vmem_limit_bytes=VMEM_LIMIT),
        cost_estimate=pl.CostEstimate(flops=1, bytes_accessed=1, transcendentals=0),
        name="begin",
    )(table, *operands, rate, initial)


def stage_kernel(counts, table, *refs):
    count, befores, begun = counts
    slots = count // 2 + begun
    wanted = count // 2
    blocks, refs = refs[:count], refs[count:]
    before, refs = refs[:befores], refs[befores:]
    state, refs = refs[0], refs[1:]
    (maps, rate, initial), refs = refs[:3], refs[3:]
    results, new, refs = refs[:wanted], refs[wanted : wanted + begun], refs[wanted + begun :]
    x, m, w, start, fresh, k, v, q, attended, pool, out, sems, *grads = refs
    rows, width = x.shape[1:]
    part = rows // 2
    updates, answers, first, there = table[0] > 0, table[1] > 0, table[2], table[3] > 0
    at_maps, at_start, at_weights, at_new, at_held, at_grads = (sems.at[count + 1 + at] for at in range(6))
    if begun:
        send_new = pltpu.make_async_copy(fresh, new[0].at[pl.ds(11, 3)], at_new)
    send = [pltpu.make_async_copy(out.at[at], results[at], sems.at[count + 7 + at]) for at in range(wanted)]

    def span(at, size=rows):
        return pl.ds(pl.multiple_of(at, part), size)

    def answer():
        row = lax.broadcasted_iota(jnp.int32, (part, rows + part), 0)
        column = lax.broadcasted_iota(jnp.int32, (part, rows + part), 1)
        band = (column > row) & (column <= row + rows)

        @pl.loop(0, wanted)
        def _(at):
            @pl.loop(0, 2, unroll=begun > 0)
            def _(half):
                own = span(part * half, part)
                base = rows * table[6 + 2 * at] + part * half
                scores = matmul_nt(q[at, own], k[span(base, rows + part)]) * (width ** -0.5)
                floor = jnp.where(first > 0, 0, rows - base)
                scores = jnp.where(band & (column >= floor), scores, -1e30)
                raised = jnp.exp(scores - jnp.max(scores, axis=1, keepdims=True))
                total = jnp.sum(raised, axis=1, keepdims=True)
                values = v[span(base, rows + part)]
                attended[own] = matmul(raised.astype(jnp.bfloat16), values) / total

            queries = unit_rows(q[at])
            gate = matmul(queries, fresh[0])
            up = matmul(queries, fresh[1])
            inner = (gate * logistic(gate) * up).astype(jnp.bfloat16)
            fast = matmul(inner, fresh[2]).astype(jnp.bfloat16).astype(jnp.float32)
            out[at] = (attended[...] + fast).astype(jnp.bfloat16)

        for copy in send:
            copy.start()
        for copy in send:
            copy.wait()

    @pl.when(updates | answers)
    def _():
        fetch(maps, m, at_maps)
        for at in range(count):
            fetch(blocks[at], x.at[at], sems.at[at])
        for at in range(befores):
            fetch(before[at], x.at[count], sems.at[count], there & (table[4] == at))
        fetch(state.at[pl.ds(table[5], 3)], w, at_weights)
        fetch(initial, start, at_start)
        if begun:
            to = span(rows * (table[6 + count + 1] + 1))
            fetch(state.at[5], k.at[to], at_held)
            fetch(state.at[7], v.at[to], at_held)
            fetch(state.at[pl.ds(8, 3)], grads[0], at_grads)
        fetched(m, at_maps)

        @pl.loop(0, count, unroll=begun > 0)
        def _(at):
            to = span(rows * (table[6 + at] + 1))

            def put_query(query_rows):
                q[at // 2] = query_rows

            def put_key_value(key_rows, value_rows):
                k[to] = key_rows
                v[to] = value_rows

            fetched(x.at[at], sems.at[at])
            learn(at, x, at, m, rate[pl.ds(first + table[6 + at], 1)], pool, put_query, put_key_value)

        @pl.when(there)
        def _():
            fetched(x.at[count], sems.at[count])
            k[:rows] = matmul(x[count], m[:, width : 2 * width]).astype(jnp.bfloat16)
            v[:rows] = matmul(x[count], m[:, 2 * width :]).astype(jnp.bfloat16)

        @pl.when(jnp.logical_not(there))
        def _():
            k[:rows] = jnp.zeros((rows, width), jnp.bfloat16)
            v[:rows] = jnp.zeros((rows, width), jnp.bfloat16)

        fetched(w, at_weights)
        fetched(start, at_start)
        if begun:
            fetched(k.at[pl.ds(0, 2 * rows)], at_held)
            fetched(grads[0], at_grads)

        @pl.when(updates)
        def _():
            pl.loop(0, count, unroll=begun > 0)(lambda at: deltas(at, rows, w, pool))

            @pl.loop(0, 3)
            def _(at):
                updated = w[at].astype(jnp.float32) + gradient(at, pool, count * rows)
                if begun:
                    updated = updated + grads[0][at].astype(jnp.float32)
                fresh[at] = renew(updated, start[at])

            if begun:
                send_new.start()

        @pl.when(jnp.logical_not(updates))
        def _():
            fresh[...] = w[...]

        pl.when(answers)(answer)
        if begun:
            send_new.wait()


def stage(table, blocks, before, state, maps, rate, initial, begun=False, scale=24):
    count, begun = len(blocks), int(begun)
    rows, width = blocks[0].shape
    matrices = initial.shape
    bfloat = functools.partial(pltpu.VMEM, dtype=jnp.bfloat16)
    anywhere = pl.BlockSpec(memory_space=pl.ANY)
    slots = count // 2 + begun
    stretch = 2 * slots * rows
    wanted = count // 2
    operands = [*blocks, *before, state, maps]
    return pl.pallas_call(
        functools.partial(stage_kernel, (count, len(before), begun)),
        grid_spec=pltpu.PrefetchScalarGridSpec(
            num_scalar_prefetch=1,
            grid=(),
            in_specs=[anywhere] * len(operands) + [pl.BlockSpec(memory_space=pltpu.VMEM), anywhere],
            out_specs=[anywhere] * (wanted + begun),
            scratch_shapes=[
                bfloat((count + 1, rows, width)),
                bfloat(maps.shape),
                bfloat(matrices),
                bfloat(matrices),
                bfloat(matrices),
                bfloat((stretch + rows, width)),
                bfloat((stretch + rows, width)),
                bfloat((wanted, rows, width)),
                pltpu.VMEM((rows, width), jnp.float32),
                bfloat((5, count * rows, width)),
                bfloat((wanted, rows, width)),
                pltpu.SemaphoreType.DMA((count + 7 + wanted,)),
            ]
            + [bfloat(matrices)] * begun,
        ),
        out_shape=[jax.ShapeDtypeStruct((rows, width), jnp.bfloat16)] * wanted
        + [jax.ShapeDtypeStruct(state.shape, state.dtype)] * begun,
        input_output_aliases={1 + count + len(before): wanted} if begun else {},
        compiler_params=pltpu.CompilerParams(vmem_limit_bytes=VMEM_LIMIT),
        cost_estimate=pl.CostEstimate(flops=scale * stretch * width * width, bytes_accessed=scale * stretch * width, transcendentals=0),
        name="stage",
    )(table, *operands, rate, initial)


def banded(queries, keys, values, floor):
    part, window = queries.shape[0], keys.shape[0]
    row = lax.broadcasted_iota(jnp.int32, (part, window), 0)
    column = lax.broadcasted_iota(jnp.int32, (part, window), 1)
    band = (column > row) & (column <= row + window - part) & (column >= floor)
    scores = matmul_nt(queries, keys) * (queries.shape[1] ** -0.5)
    scores = jnp.where(band, scores, -1e30)
    raised = jnp.exp(scores - jnp.max(scores, axis=1, keepdims=True))
    total = jnp.sum(raised, axis=1, keepdims=True)
    return matmul(raised.astype(jnp.bfloat16), values) / total


def finish_kernel(befores, table, *refs):
    before, refs = refs[:befores], refs[befores:]
    maps, state, result, x, m, w, q, k, v, attended, out, sems = refs
    rows, width = x.shape
    part = rows // 2
    there = table[0] > 0
    for at in range(befores):
        fetch(before[at], x, sems.at[0], there & (table[1] == at))
    fetch(maps, m, sems.at[1], there)
    fetch(state.at[3], q, sems.at[2])
    fetch(state.at[4], k.at[pl.ds(rows, rows)], sems.at[3])
    fetch(state.at[6], v.at[pl.ds(rows, rows)], sems.at[4])
    fetch(state.at[pl.ds(11, 3)], w, sems.at[5])

    @pl.when(there)
    def _():
        fetched(x, sems.at[0])
        fetched(m, sems.at[1])
        k[:rows] = matmul(x[...], m[:, width : 2 * width]).astype(jnp.bfloat16)
        v[:rows] = matmul(x[...], m[:, 2 * width :]).astype(jnp.bfloat16)

    @pl.when(jnp.logical_not(there))
    def _():
        k[:rows] = jnp.zeros((rows, width), jnp.bfloat16)
        v[:rows] = jnp.zeros((rows, width), jnp.bfloat16)

    fetched(q, sems.at[2])
    fetched(q, sems.at[3])
    fetched(q, sems.at[4])

    @pl.loop(0, 2)
    def _(half):
        first = part * half
        window = pl.ds(first, rows + part)
        floor = jnp.where(there, 0, rows - first)
        attended[pl.ds(first, part)] = banded(q[pl.ds(first, part)], k[window], v[window], floor)

    fetched(w, sems.at[5])
    queries = unit_rows(q[...])
    gate = matmul(queries, w[0])
    up = matmul(queries, w[1])
    inner = (gate * logistic(gate) * up).astype(jnp.bfloat16)
    fast = matmul(inner, w[2]).astype(jnp.bfloat16).astype(jnp.float32)
    out[...] = (attended[...] + fast).astype(jnp.bfloat16)
    copy = pltpu.make_async_copy(out, result, sems.at[0])
    copy.start()
    copy.wait()


def finish(table, before, maps, state):
    rows, width = before[0].shape
    anywhere = pl.BlockSpec(memory_space=pl.ANY)
    bfloat = functools.partial(pltpu.VMEM, dtype=jnp.bfloat16)
    return pl.pallas_call(
        functools.partial(finish_kernel, len(before)),
        grid_spec=pltpu.PrefetchScalarGridSpec(
            num_scalar_prefetch=1,
            grid=(),
            in_specs=[anywhere] * (len(before) + 2),
            out_specs=anywhere,
            scratch_shapes=[
                bfloat((rows, width)),
                bfloat(maps.shape),
                bfloat((3,) + state.shape[1:]),
                bfloat((rows, width)),
                bfloat((2 * rows, width)),
                bfloat((2 * rows, width)),
                pltpu.VMEM((rows, width), jnp.float32),
                bfloat((rows, width)),
                pltpu.SemaphoreType.DMA((6,)),
            ],
        ),
        out_shape=jax.ShapeDtypeStruct((rows, width), jnp.bfloat16),
        compiler_params=pltpu.CompilerParams(vmem_limit_bytes=VMEM_LIMIT),
        cost_estimate=pl.CostEstimate(flops=1, bytes_accessed=1, transcendentals=0),
        name="finish",
    )(table, *before, maps, state)


def after(array, *others):
    return lax.optimization_barrier((array, *others))[0]


def head_body(tokens, qkv_maps, rate_map, fast_init):
    rows = tokens.shape[0]
    heads, width = qkv_maps.shape[:2]
    groups = lax.axis_size("tok")
    chips = groups // 2
    slots = chips // 2
    last = chips - 1
    me = lax.axis_index("tok")
    chip, core = me // 2, me % 2
    is_first = (chip < slots).astype(jnp.int32)

    def swap(block, bits):
        return lax.ppermute(block, "tok", [(i, i ^ bits) for i in range(groups)])

    def piece(slot, source, index):
        return lax.dynamic_slice_in_dim(source, (index ^ slot) * width, width, 1)

    maps = lax.dynamic_index_in_dim(qkv_maps, chip, 0, False)
    initial = lax.dynamic_index_in_dim(fast_init, chip, 0, False)
    same = {slot: swap(piece(slot, tokens, chip), 2 * slot) for slot in range(1, slots)}
    same[last] = swap(piece(last, tokens, chip), 2 * last)
    terms = lax.dot_general(
        rate_map, tokens, (((0,), (1,)), ((), ())), preferred_element_type=jnp.float32
    )
    terms = lax.all_to_all(jnp.repeat(terms, 2, axis=0), ("head", "tok"), 0, 0, tiled=True)
    logits = jnp.sum(terms.reshape(-1, groups, rows), 0)
    rate = (rate_base * jax.nn.softplus(logits)).astype(jnp.bfloat16).astype(jnp.float32)
    source = after(tokens, *(same[slot] for slot in range(1, slots)))
    for slot in range(slots, last):
        same[slot] = swap(piece(slot, source, chip), 2 * slot)
    same[0] = piece(0, source, chip)
    other = {slot: swap(same[slot], 1) for slot in range(slots)}

    def integers(entries):
        return jnp.stack([jnp.asarray(entry, jnp.int32) for entry in entries])

    def places(slot):
        return [2 * ((chip ^ slot) % slots) + core, 2 * ((chip ^ slot) % slots) + (1 - core)]

    def opening(slot):
        return 2 * slots * ((chip ^ slot) // slots)

    def table(slots_in, updates, answers, weights_at):
        first = opening(slots_in[0])
        before = (chip ^ (slots - 1)) % slots
        flags = [updates, answers, first, (first > 0) & (core == 0), before, weights_at]
        return integers(flags + [place for slot in slots_in for place in places(slot)])

    near_slots, far_slots = range(slots), range(slots, chips)
    near_blocks = [block for slot in near_slots for block in (same[slot], other[slot])]
    near_others = [other[slot] for slot in near_slots]
    shared = dict(maps=maps, rate=rate, initial=initial)
    other[last] = swap(same[last], 1)
    rates_in = [opening(slot) + place for slot in (*near_slots, last) for place in places(slot)]
    state = begin(integers([is_first] + rates_in), near_blocks, [same[last], other[last]], **shared)
    far_blocks = []
    for slot in far_slots[:-1]:
        same[slot] = after(same[slot], state)
        other[slot] = swap(same[slot], 1)
        far_blocks += [same[slot], other[slot]]
    *far_results, state = stage(
        table(far_slots, True, True, 0), far_blocks, near_others, state, begun=True, **shared
    )
    near_results = stage(
        table(near_slots, 1 - is_first, True, 11 * (1 - is_first)), near_blocks,
        [other[slot] for slot in far_slots], state, scale=0, **shared
    )
    at = chip ^ last
    place = jnp.where(core == 1, at, at - 1)
    last_result = finish(
        integers([place >= 0, chip ^ jnp.maximum(place, 0)]), [other[slot] for slot in range(chips)], maps, state
    )
    results = [*near_results, *far_results, last_result]
    combined = jnp.zeros_like(tokens)
    for slot in (*far_slots[:-1], 0, last, *range(1, slots)):
        result = swap(results[slot], 2 * slot) if slot else results[slot]
        combined = lax.dynamic_update_slice_in_dim(combined, result, (chip ^ slot) * width, 1)
    return combined


def body(tokens, qkv_maps, rate_map, fast_init):
    groups = lax.axis_size("tok")
    heads = qkv_maps.shape[0]
    powers = groups & (groups - 1) == 0 and groups > 2
    if powers and groups == 2 * heads and tokens.shape[0] == WINDOW:
        return head_body(tokens, qkv_maps, rate_map, fast_init)
    return general_body(tokens, qkv_maps, rate_map, fast_init)


def solution(mesh):
    in_specs = (
        P("tok", "head"),
        P("head", None, None),
        P("head", None),
        P("head", None, None, None),
    )
    out_specs = P("tok", "head")
    return jax.shard_map(body, mesh=mesh, in_specs=in_specs, out_specs=out_specs, check_vma=False)
```

```python
import functools

import jax
import jax.numpy as jnp
from jax import lax
from jax.experimental import pallas as pl
from jax.experimental.pallas import tpu as pltpu
from jax.sharding import PartitionSpec as P

WINDOW = 512


rate_base = 0.003
epsilon = 1e-06
VMEM_LIMIT = 40 * 1024 * 1024
STATE = 64


def from_behind(block, axis, distance):
    devices = range(lax.axis_size(axis))
    route = [(i - distance, i) for i in devices if i - distance in devices]
    return lax.ppermute(block, axis, route)


def rms_rows(matrix):
    matrix = matrix.astype(jnp.float32)
    return matrix / jnp.sqrt(jnp.mean(matrix * matrix, axis=-1, keepdims=True) + epsilon)


def renorm(updated, initial):
    target = jnp.sqrt(jnp.mean(initial * initial, axis=-1, keepdims=True) + epsilon)
    current = jnp.sqrt(jnp.mean(updated * updated, axis=-1, keepdims=True) + epsilon)
    return (updated * (target / current)).astype(jnp.bfloat16)


def band_attention(queries, key_rows, value_rows, query_pos, key_pos, score_scale):
    scores = (
        jnp.einsum("qhd,khd->hqk", queries, key_rows, preferred_element_type=jnp.float32)
        * score_scale
    )
    key_mask = (
        (key_pos[None, :] <= query_pos[:, None])
        & (key_pos[None, :] > query_pos[:, None] - WINDOW)
        & (key_pos[None, :] >= 0)
    )
    key_mask = key_mask[None]
    row_max = jnp.max(jnp.where(key_mask, scores, -1e30), axis=2, keepdims=True)
    raised = jnp.where(key_mask, jnp.exp(scores - row_max), 0.0)
    probs = (raised / jnp.sum(raised, axis=2, keepdims=True)).astype(jnp.bfloat16)
    return jnp.einsum("hqk,khd->qhd", probs, value_rows, preferred_element_type=jnp.float32)


def fast_gradient(weights, key_part, value_part, rate_part):
    pre_gate = jnp.einsum(
        "rhd,hde->rhe", key_part, weights[:, 0], preferred_element_type=jnp.float32
    )
    pre_up = jnp.einsum("rhd,hde->rhe", key_part, weights[:, 1], preferred_element_type=jnp.float32)
    sigma = jax.nn.sigmoid(pre_gate)
    gated = pre_gate * sigma
    hidden = (gated * pre_up).astype(jnp.bfloat16)
    target = (rate_part.astype(jnp.float32)[:, :, None] * value_part.astype(jnp.float32)).astype(
        jnp.bfloat16
    )
    grad_down = jnp.einsum("rhe,rhd->hed", hidden, target, preferred_element_type=jnp.float32)
    back_hidden = jnp.einsum(
        "rhd,hed->rhe", target, weights[:, 2], preferred_element_type=jnp.float32
    )
    gate_delta = (back_hidden * pre_up * sigma * (1.0 + pre_gate * (1.0 - sigma))).astype(
        jnp.bfloat16
    )
    up_delta = (back_hidden * gated).astype(jnp.bfloat16)
    grad_gate = jnp.einsum("rhd,rhe->hde", key_part, gate_delta, preferred_element_type=jnp.float32)
    grad_up = jnp.einsum("rhd,rhe->hde", key_part, up_delta, preferred_element_type=jnp.float32)
    return jnp.stack([grad_gate, grad_up, grad_down], 1)


def fast_apply(weights, query_part):
    app_gate = jnp.einsum(
        "rhd,hde->rhe", query_part, weights[:, 0], preferred_element_type=jnp.float32
    )
    app_up = jnp.einsum(
        "rhd,hde->rhe", query_part, weights[:, 1], preferred_element_type=jnp.float32
    )
    app_hidden = (app_gate * jax.nn.sigmoid(app_gate) * app_up).astype(jnp.bfloat16)
    result = jnp.einsum(
        "rhe,hed->rhd", app_hidden, weights[:, 2], preferred_element_type=jnp.float32
    )
    return result.astype(jnp.bfloat16)


def update_weights(weights, partial_value, initial):
    total = lax.psum(partial_value.astype(jnp.bfloat16), "tok").astype(jnp.float32)
    return renorm(weights.astype(jnp.float32) + total, initial)


def general_body(tokens, qkv_maps, rate_map, fast_init):
    tok_rows = tokens.shape[0]
    head_count = qkv_maps.shape[0]
    head_width = qkv_maps.shape[1]
    groups = lax.axis_size("tok")
    logit_terms = jnp.dot(tokens, rate_map, preferred_element_type=jnp.float32)
    logits = lax.psum_scatter(
        logit_terms.astype(jnp.bfloat16), "head", scatter_dimension=1, tiled=True
    ).astype(jnp.float32)
    rate = (rate_base * jax.nn.softplus(logits)).astype(jnp.bfloat16)
    inputs = tokens.reshape(tok_rows, head_count, head_width)
    projected = jnp.einsum("rhd,hde->rhe", inputs, qkv_maps, preferred_element_type=jnp.float32)
    queries = projected[:, :, :head_width].astype(jnp.bfloat16)
    key_rows = projected[:, :, head_width : 2 * head_width].astype(jnp.bfloat16)
    value_rows = projected[:, :, 2 * head_width :].astype(jnp.bfloat16)
    tail_rows = min(WINDOW, tok_rows)
    edge = jnp.stack([key_rows, value_rows], 0)
    distance = 0
    received = [from_behind(edge, "tok", distance + 1)]
    anchor = lax.axis_index("tok") * tok_rows
    offsets = jnp.arange(tail_rows, dtype=jnp.int32)
    distance = 1
    arrived = received[distance - 1]
    key_parts = [arrived[0]]
    value_parts = [arrived[1]]
    position_parts = [anchor - distance * tok_rows + tok_rows - tail_rows + offsets]
    local_pos = anchor + jnp.arange(tok_rows, dtype=jnp.int32)
    all_keys = jnp.concatenate(key_parts + [key_rows], 0)
    all_values = jnp.concatenate(value_parts + [value_rows], 0)
    all_pos = jnp.concatenate(position_parts + [local_pos], 0)
    attended = band_attention(
        queries, all_keys, all_values, local_pos, all_pos, head_width ** (-0.5)
    )
    q_norm = rms_rows(queries).astype(jnp.bfloat16)
    k_norm = rms_rows(key_rows).astype(jnp.bfloat16)
    initial = fast_init.astype(jnp.float32)
    weights = fast_init
    own_block = lax.axis_index("tok") // (groups // 2)
    fast_out = jnp.zeros_like(q_norm)
    for half_index in range(2):
        partial_value = fast_gradient(weights, k_norm, value_rows, rate)
        partial_value = jnp.where(own_block == half_index, partial_value, 0.0)
        weights = update_weights(weights, partial_value, initial)
        applied = fast_apply(weights, q_norm)
        fast_out = jnp.where(own_block == half_index, applied, fast_out)
    combined = (attended + fast_out.astype(jnp.float32)).astype(jnp.bfloat16)
    return combined.reshape(tok_rows, head_count * head_width)


def matmul(left, right):
    return jnp.dot(left, right, preferred_element_type=jnp.float32)


def matmul_nt(left, right):
    return lax.dot_general(left, right, (((1,), (1,)), ((), ())), preferred_element_type=jnp.float32)


def matmul_tn(left, right):
    return lax.dot_general(left, right, (((0,), (0,)), ((), ())), preferred_element_type=jnp.float32)


def unit_rows(rows):
    rows = rows.astype(jnp.float32)
    scale = lax.rsqrt(jnp.mean(rows * rows, axis=-1, keepdims=True) + epsilon)
    return (rows * scale).astype(jnp.bfloat16)


def logistic(a):
    return 0.5 * jnp.tanh(0.5 * a) + 0.5


def fetch(source, target, sem, when=None):
    copy = pltpu.make_async_copy(source, target, sem)
    if when is None:
        copy.start()
    else:
        pl.when(when)(copy.start)


def fetched(target, sem):
    pltpu.make_async_copy(target, target, sem).wait()


def learn(at, x, source, m, rate_row, pool, put_query, put_key_value):
    rows, width = x.shape[1:]
    here = pl.ds(pl.multiple_of(rows * at, rows), rows)
    key_rows = matmul(x[source], m[:, width : 2 * width]).astype(jnp.bfloat16)
    value_rows = matmul(x[source], m[:, 2 * width :]).astype(jnp.bfloat16)
    if put_key_value is not None:
        put_key_value(key_rows, value_rows)
    pool[0, here] = unit_rows(key_rows)
    spread = jnp.broadcast_to(rate_row, (128, rows)).T
    spread = jnp.concatenate([spread] * (width // 128), 1)
    pool[2, here] = (spread * value_rows.astype(jnp.float32)).astype(jnp.bfloat16)

    if put_query is not None:

        @pl.when(at % 2 == 0)
        def _():
            put_query(matmul(x[source], m[:, :width]).astype(jnp.bfloat16))


def deltas(at, rows, w, pool, both=None):
    here = pl.ds(pl.multiple_of(rows * at, rows), rows)
    gate = matmul(pool[0, here], w[0])
    sigma = logistic(gate)
    slope = (1.0 + gate * (1.0 - sigma)).astype(jnp.bfloat16)
    gated = (gate * sigma).astype(jnp.bfloat16)
    up = matmul(pool[0, here], w[1]).astype(jnp.bfloat16)
    back = matmul_nt(pool[2, here], w[2]).astype(jnp.bfloat16)
    pool[1, here] = gated * up
    width = gate.shape[1]
    gate_delta = back * up * (sigma.astype(jnp.bfloat16) * slope)
    up_delta = back * gated
    if both is None:
        pool[3, here] = gate_delta
        pool[4, here] = up_delta
    else:
        both[here, :width] = gate_delta
        both[here, width:] = up_delta


def gradient(at, pool, rows):
    return matmul_tn(pool[at // 2, :rows], pool[jnp.where(at == 2, 2, 3 + at), :rows])


def gradients(rows, pool, both, take):
    width = pool.shape[2]
    grads = matmul_tn(pool[0, :rows], both[:rows])
    take(0, grads[:, :width])
    take(1, grads[:, width:])
    take(2, matmul_tn(pool[1, :rows], pool[2, :rows]))


def renew(updated, initial):
    origin = initial.astype(jnp.float32)
    wanted = jnp.mean(origin * origin, axis=-1, keepdims=True) + epsilon
    held = jnp.mean(updated * updated, axis=-1, keepdims=True) + epsilon
    return (updated * (jnp.sqrt(wanted) * lax.rsqrt(held))).astype(jnp.bfloat16)


def begin_kernel(count, table, *refs):
    near, far, refs = refs[:count], refs[count : count + 2], refs[count + 2 :]
    maps, rate, initial, state, x, m, w, fresh, kept, grads, pool, both, sems = refs
    rows = x.shape[1]
    updates = table[0] > 0
    fetch(maps, m, sems.at[count + 2])
    for at in range(count):
        fetch(near[at], x.at[at], sems.at[at], updates)
    for at in range(2):
        fetch(far[at], x.at[count + at], sems.at[count + at])
    fetch(initial, w, sems.at[count + 3])
    fetched(m, sems.at[count + 2])

    @pl.when(updates)
    def _():
        @pl.loop(0, count, unroll=True)
        def _(at):
            fetched(x.at[at], sems.at[at])
            learn(at, x, at, m, rate[pl.ds(table[1 + at], 1)], pool, None, None)

        fetched(w, sems.at[count + 3])
        pl.loop(0, count, unroll=True)(lambda at: deltas(at, rows, w, pool, both))

        def take(at, grad):
            fresh[at] = renew(w[at].astype(jnp.float32) + grad, w[at])

        gradients(count * rows, pool, both, take)

    @pl.when(jnp.logical_not(updates))
    def _():
        fetched(w, sems.at[count + 3])
        fresh[...] = w[...]

    send = [pltpu.make_async_copy(fresh, state.at[pl.ds(0, 3)], sems.at[0])]
    send[0].start()

    @pl.loop(0, 2, unroll=True)
    def _(at):
        def put_query(query_rows):
            kept[0] = query_rows

        def put_key_value(key_rows, value_rows):
            kept[1 + at] = key_rows
            kept[3 + at] = value_rows

        fetched(x.at[count + at], sems.at[count + at])
        learn(at, x, count + at, m, rate[pl.ds(table[1 + count + at], 1)], pool, put_query, put_key_value)

    send.append(pltpu.make_async_copy(kept, state.at[pl.ds(3, 5)], sems.at[1]))
    send[1].start()
    pl.loop(0, 2, unroll=True)(lambda at: deltas(at, rows, fresh, pool, both))

    def take(at, grad):
        grads[at] = grad.astype(jnp.bfloat16)

    gradients(2 * rows, pool, both, take)

    send.append(pltpu.make_async_copy(grads, state.at[pl.ds(8, 3)], sems.at[2]))
    send[2].start()
    for copy in send:
        copy.wait()


def begin(table, near, far, maps, rate, initial):
    rows, width = near[0].shape
    count = len(near)
    anywhere = pl.BlockSpec(memory_space=pl.ANY)
    bfloat = functools.partial(pltpu.VMEM, dtype=jnp.bfloat16)
    operands = [*near, *far, maps]
    return pl.pallas_call(
        functools.partial(begin_kernel, count),
        grid_spec=pltpu.PrefetchScalarGridSpec(
            num_scalar_prefetch=1,
            grid=(),
            in_specs=[anywhere] * len(operands) + [pl.BlockSpec(memory_space=pltpu.VMEM), anywhere],
            out_specs=anywhere,
            scratch_shapes=[
                bfloat((count + 2, rows, width)),
                bfloat(maps.shape),
                bfloat(initial.shape),
                bfloat(initial.shape),
                bfloat((5, rows, width)),
                bfloat(initial.shape),
                bfloat((3, count * rows, width)),
                bfloat((count * rows, 2 * width)),
                pltpu.SemaphoreType.DMA((count + 4,)),
            ],
        ),
        out_shape=jax.ShapeDtypeStruct((STATE, rows, width), jnp.bfloat16),
        compiler_params=pltpu.CompilerParams(vmem_limit_bytes=VMEM_LIMIT),
        cost_estimate=pl.CostEstimate(flops=1, bytes_accessed=1, transcendentals=0),
        name="begin",
    )(table, *operands, rate, initial)


def stage_kernel(counts, table, *refs):
    count, befores, begun = counts
    slots = count // 2 + begun
    wanted = count // 2
    blocks, refs = refs[:count], refs[count:]
    before, refs = refs[:befores], refs[befores:]
    state, refs = refs[0], refs[1:]
    (maps, rate, initial), refs = refs[:3], refs[3:]
    results, new, refs = refs[:wanted], refs[wanted : wanted + begun], refs[wanted + begun :]
    x, m, w, start, fresh, k, v, q, attended, pool, out, sems, *grads = refs
    rows, width = x.shape[1:]
    part = rows // 2
    updates, answers, first, there = table[0] > 0, table[1] > 0, table[2], table[3] > 0
    at_maps, at_start, at_weights, at_new, at_held, at_grads = (sems.at[count + 1 + at] for at in range(6))
    if begun:
        send_new = pltpu.make_async_copy(fresh, new[0].at[pl.ds(11, 3)], at_new)
    send = [pltpu.make_async_copy(out.at[at], results[at], sems.at[count + 7 + at]) for at in range(wanted)]

    def span(at, size=rows):
        return pl.ds(pl.multiple_of(at, part), size)

    def answer():
        row = lax.broadcasted_iota(jnp.int32, (part, rows + part), 0)
        column = lax.broadcasted_iota(jnp.int32, (part, rows + part), 1)
        band = (column > row) & (column <= row + rows)

        @pl.loop(0, wanted)
        def _(at):
            @pl.loop(0, 2, unroll=begun > 0)
            def _(half):
                own = span(part * half, part)
                base = rows * table[6 + 2 * at] + part * half
                scores = matmul_nt(q[at, own], k[span(base, rows + part)]) * (width ** -0.5)
                floor = jnp.where(first > 0, 0, rows - base)
                scores = jnp.where(band & (column >= floor), scores, -1e30)
                raised = jnp.exp(scores - jnp.max(scores, axis=1, keepdims=True))
                total = jnp.sum(raised, axis=1, keepdims=True)
                values = v[span(base, rows + part)]
                attended[own] = matmul(raised.astype(jnp.bfloat16), values) / total

            queries = unit_rows(q[at])
            gate = matmul(queries, fresh[0])
            up = matmul(queries, fresh[1])
            inner = (gate * logistic(gate) * up).astype(jnp.bfloat16)
            fast = matmul(inner, fresh[2]).astype(jnp.bfloat16).astype(jnp.float32)
            out[at] = (attended[...] + fast).astype(jnp.bfloat16)

        for copy in send:
            copy.start()
        for copy in send:
            copy.wait()

    @pl.when(updates | answers)
    def _():
        fetch(maps, m, at_maps)
        for at in range(count):
            fetch(blocks[at], x.at[at], sems.at[at])
        for at in range(befores):
            fetch(before[at], x.at[count], sems.at[count], there & (table[4] == at))
        fetch(state.at[pl.ds(table[5], 3)], w, at_weights)
        fetch(initial, start, at_start)
        if begun:
            to = span(rows * (table[6 + count + 1] + 1))
            fetch(state.at[5], k.at[to], at_held)
            fetch(state.at[7], v.at[to], at_held)
            fetch(state.at[pl.ds(8, 3)], grads[0], at_grads)
        fetched(m, at_maps)

        @pl.loop(0, count, unroll=begun > 0)
        def _(at):
            to = span(rows * (table[6 + at] + 1))

            def put_query(query_rows):
                q[at // 2] = query_rows

            def put_key_value(key_rows, value_rows):
                k[to] = key_rows
                v[to] = value_rows

            fetched(x.at[at], sems.at[at])
            learn(at, x, at, m, rate[pl.ds(first + table[6 + at], 1)], pool, put_query, put_key_value)

        @pl.when(there)
        def _():
            fetched(x.at[count], sems.at[count])
            k[:rows] = matmul(x[count], m[:, width : 2 * width]).astype(jnp.bfloat16)
            v[:rows] = matmul(x[count], m[:, 2 * width :]).astype(jnp.bfloat16)

        @pl.when(jnp.logical_not(there))
        def _():
            k[:rows] = jnp.zeros((rows, width), jnp.bfloat16)
            v[:rows] = jnp.zeros((rows, width), jnp.bfloat16)

        fetched(w, at_weights)
        fetched(start, at_start)
        if begun:
            fetched(k.at[pl.ds(0, 2 * rows)], at_held)
            fetched(grads[0], at_grads)

        @pl.when(updates)
        def _():
            pl.loop(0, count, unroll=begun > 0)(lambda at: deltas(at, rows, w, pool))

            @pl.loop(0, 3)
            def _(at):
                updated = w[at].astype(jnp.float32) + gradient(at, pool, count * rows)
                if begun:
                    updated = updated + grads[0][at].astype(jnp.float32)
                fresh[at] = renew(updated, start[at])

            if begun:
                send_new.start()

        @pl.when(jnp.logical_not(updates))
        def _():
            fresh[...] = w[...]

        pl.when(answers)(answer)
        if begun:
            send_new.wait()


def stage(table, blocks, before, state, maps, rate, initial, begun=False, scale=24):
    count, begun = len(blocks), int(begun)
    rows, width = blocks[0].shape
    matrices = initial.shape
    bfloat = functools.partial(pltpu.VMEM, dtype=jnp.bfloat16)
    anywhere = pl.BlockSpec(memory_space=pl.ANY)
    slots = count // 2 + begun
    stretch = 2 * slots * rows
    wanted = count // 2
    operands = [*blocks, *before, state, maps]
    return pl.pallas_call(
        functools.partial(stage_kernel, (count, len(before), begun)),
        grid_spec=pltpu.PrefetchScalarGridSpec(
            num_scalar_prefetch=1,
            grid=(),
            in_specs=[anywhere] * len(operands) + [pl.BlockSpec(memory_space=pltpu.VMEM), anywhere],
            out_specs=[anywhere] * (wanted + begun),
            scratch_shapes=[
                bfloat((count + 1, rows, width)),
                bfloat(maps.shape),
                bfloat(matrices),
                bfloat(matrices),
                bfloat(matrices),
                bfloat((stretch + rows, width)),
                bfloat((stretch + rows, width)),
                bfloat((wanted, rows, width)),
                pltpu.VMEM((rows, width), jnp.float32),
                bfloat((5, count * rows, width)),
                bfloat((wanted, rows, width)),
                pltpu.SemaphoreType.DMA((count + 7 + wanted,)),
            ]
            + [bfloat(matrices)] * begun,
        ),
        out_shape=[jax.ShapeDtypeStruct((rows, width), jnp.bfloat16)] * wanted
        + [jax.ShapeDtypeStruct(state.shape, state.dtype)] * begun,
        input_output_aliases={1 + count + len(before): wanted} if begun else {},
        compiler_params=pltpu.CompilerParams(vmem_limit_bytes=VMEM_LIMIT),
        cost_estimate=pl.CostEstimate(flops=scale * stretch * width * width, bytes_accessed=scale * stretch * width, transcendentals=0),
        name="stage",
    )(table, *operands, rate, initial)


def banded(queries, keys, values, floor):
    part, window = queries.shape[0], keys.shape[0]
    row = lax.broadcasted_iota(jnp.int32, (part, window), 0)
    column = lax.broadcasted_iota(jnp.int32, (part, window), 1)
    band = (column > row) & (column <= row + window - part) & (column >= floor)
    scores = matmul_nt(queries, keys) * (queries.shape[1] ** -0.5)
    scores = jnp.where(band, scores, -1e30)
    raised = jnp.exp(scores - jnp.max(scores, axis=1, keepdims=True))
    total = jnp.sum(raised, axis=1, keepdims=True)
    return matmul(raised.astype(jnp.bfloat16), values) / total


def finish_kernel(befores, table, *refs):
    before, refs = refs[:befores], refs[befores:]
    maps, state, result, x, m, w, q, k, v, attended, out, sems = refs
    rows, width = x.shape
    part = rows // 2
    there = table[0] > 0
    for at in range(befores):
        fetch(before[at], x, sems.at[0], there & (table[1] == at))
    fetch(maps, m, sems.at[1], there)
    fetch(state.at[3], q, sems.at[2])
    fetch(state.at[4], k.at[pl.ds(rows, rows)], sems.at[3])
    fetch(state.at[6], v.at[pl.ds(rows, rows)], sems.at[4])
    fetch(state.at[pl.ds(11, 3)], w, sems.at[5])

    @pl.when(there)
    def _():
        fetched(x, sems.at[0])
        fetched(m, sems.at[1])
        k[:rows] = matmul(x[...], m[:, width : 2 * width]).astype(jnp.bfloat16)
        v[:rows] = matmul(x[...], m[:, 2 * width :]).astype(jnp.bfloat16)

    @pl.when(jnp.logical_not(there))
    def _():
        k[:rows] = jnp.zeros((rows, width), jnp.bfloat16)
        v[:rows] = jnp.zeros((rows, width), jnp.bfloat16)

    fetched(q, sems.at[2])
    fetched(q, sems.at[3])
    fetched(q, sems.at[4])

    @pl.loop(0, 2)
    def _(half):
        first = part * half
        window = pl.ds(first, rows + part)
        floor = jnp.where(there, 0, rows - first)
        attended[pl.ds(first, part)] = banded(q[pl.ds(first, part)], k[window], v[window], floor)

    fetched(w, sems.at[5])
    queries = unit_rows(q[...])
    gate = matmul(queries, w[0])
    up = matmul(queries, w[1])
    inner = (gate * logistic(gate) * up).astype(jnp.bfloat16)
    fast = matmul(inner, w[2]).astype(jnp.bfloat16).astype(jnp.float32)
    out[...] = (attended[...] + fast).astype(jnp.bfloat16)
    copy = pltpu.make_async_copy(out, result, sems.at[0])
    copy.start()
    copy.wait()


def finish(table, before, maps, state):
    rows, width = before[0].shape
    anywhere = pl.BlockSpec(memory_space=pl.ANY)
    bfloat = functools.partial(pltpu.VMEM, dtype=jnp.bfloat16)
    return pl.pallas_call(
        functools.partial(finish_kernel, len(before)),
        grid_spec=pltpu.PrefetchScalarGridSpec(
            num_scalar_prefetch=1,
            grid=(),
            in_specs=[anywhere] * (len(before) + 2),
            out_specs=anywhere,
            scratch_shapes=[
                bfloat((rows, width)),
                bfloat(maps.shape),
                bfloat((3,) + state.shape[1:]),
                bfloat((rows, width)),
                bfloat((2 * rows, width)),
                bfloat((2 * rows, width)),
                pltpu.VMEM((rows, width), jnp.float32),
                bfloat((rows, width)),
                pltpu.SemaphoreType.DMA((6,)),
            ],
        ),
        out_shape=jax.ShapeDtypeStruct((rows, width), jnp.bfloat16),
        compiler_params=pltpu.CompilerParams(vmem_limit_bytes=VMEM_LIMIT),
        cost_estimate=pl.CostEstimate(flops=1, bytes_accessed=1, transcendentals=0),
        name="finish",
    )(table, *before, maps, state)


def after(array, *others):
    return lax.optimization_barrier((array, *others))[0]


def head_body(tokens, qkv_maps, rate_map, fast_init):
    rows = tokens.shape[0]
    heads, width = qkv_maps.shape[:2]
    groups = lax.axis_size("tok")
    chips = groups // 2
    slots = chips // 2
    last = chips - 1
    me = lax.axis_index("tok")
    chip, core = me // 2, me % 2
    is_first = (chip < slots).astype(jnp.int32)

    def swap(block, bits):
        return lax.ppermute(block, "tok", [(i, i ^ bits) for i in range(groups)])

    def piece(slot, source, index):
        return lax.dynamic_slice_in_dim(source, (index ^ slot) * width, width, 1)

    maps = lax.dynamic_index_in_dim(qkv_maps, chip, 0, False)
    initial = lax.dynamic_index_in_dim(fast_init, chip, 0, False)
    same = {slot: swap(piece(slot, tokens, chip), 2 * slot) for slot in range(1, slots)}
    same[last] = swap(piece(last, tokens, chip), 2 * last)
    terms = lax.dot_general(
        rate_map, tokens, (((0,), (1,)), ((), ())), preferred_element_type=jnp.float32
    )
    terms = lax.all_to_all(jnp.repeat(terms, 2, axis=0), ("head", "tok"), 0, 0, tiled=True)
    logits = jnp.sum(terms.reshape(-1, groups, rows), 0)
    rate = (rate_base * jax.nn.softplus(logits)).astype(jnp.bfloat16).astype(jnp.float32)
    source = after(tokens, *(same[slot] for slot in range(1, slots)))
    for slot in range(slots, last):
        same[slot] = swap(piece(slot, source, chip), 2 * slot)
    same[0] = piece(0, source, chip)
    other = {slot: swap(same[slot], 1) for slot in range(slots)}

    def integers(entries):
        return jnp.stack([jnp.asarray(entry, jnp.int32) for entry in entries])

    def places(slot):
        return [2 * ((chip ^ slot) % slots) + core, 2 * ((chip ^ slot) % slots) + (1 - core)]

    def opening(slot):
        return 2 * slots * ((chip ^ slot) // slots)

    def table(slots_in, updates, answers, weights_at):
        first = opening(slots_in[0])
        before = (chip ^ (slots - 1)) % slots
        flags = [updates, answers, first, (first > 0) & (core == 0), before, weights_at]
        return integers(flags + [place for slot in slots_in for place in places(slot)])

    near_slots, far_slots = range(slots), range(slots, chips)
    near_blocks = [block for slot in near_slots for block in (same[slot], other[slot])]
    near_others = [other[slot] for slot in near_slots]
    shared = dict(maps=maps, rate=rate, initial=initial)
    other[last] = swap(same[last], 1)
    rates_in = [opening(slot) + place for slot in (*near_slots, last) for place in places(slot)]
    state = begin(integers([is_first] + rates_in), near_blocks, [same[last], other[last]], **shared)
    far_blocks = []
    for slot in far_slots[:-1]:
        same[slot] = after(same[slot], state)
        other[slot] = swap(same[slot], 1)
        far_blocks += [same[slot], other[slot]]
    *far_results, state = stage(
        table(far_slots, True, True, 0), far_blocks, near_others, state, begun=True, **shared
    )
    near_results = stage(
        table(near_slots, 1 - is_first, True, 11 * (1 - is_first)), near_blocks,
        [other[slot] for slot in far_slots], state, scale=0, **shared
    )
    at = chip ^ last
    place = jnp.where(core == 1, at, at - 1)
    last_result = finish(
        integers([place >= 0, chip ^ jnp.maximum(place, 0)]), [other[slot] for slot in range(chips)], maps, state
    )
    results = [*near_results, *far_results, last_result]
    combined = jnp.zeros_like(tokens)
    for slot in (*far_slots[:-1], 0, last, *range(1, slots)):
        result = swap(results[slot], 2 * slot) if slot else results[slot]
        combined = lax.dynamic_update_slice_in_dim(combined, result, (chip ^ slot) * width, 1)
    return combined


def body(tokens, qkv_maps, rate_map, fast_init):
    groups = lax.axis_size("tok")
    heads = qkv_maps.shape[0]
    powers = groups & (groups - 1) == 0 and groups > 2
    if powers and groups == 2 * heads and tokens.shape[0] == WINDOW:
        return head_body(tokens, qkv_maps, rate_map, fast_init)
    return general_body(tokens, qkv_maps, rate_map, fast_init)


def solution(mesh):
    in_specs = (
        P("tok", "head"),
        P("head", None, None),
        P("head", None),
        P("head", None, None, None),
    )
    out_specs = P("tok", "head")
    return jax.shard_map(body, mesh=mesh, in_specs=in_specs, out_specs=out_specs, check_vma=False)
```

```python
import functools

import jax
import jax.numpy as jnp
from jax import lax
from jax.experimental import pallas as pl
from jax.experimental.pallas import tpu as pltpu
from jax.sharding import PartitionSpec as P

WINDOW = 512


rate_base = 0.003
epsilon = 1e-06
VMEM_LIMIT = 40 * 1024 * 1024
STATE = 64


def from_behind(block, axis, distance):
    devices = range(lax.axis_size(axis))
    route = [(i - distance, i) for i in devices if i - distance in devices]
    return lax.ppermute(block, axis, route)


def rms_rows(matrix):
    matrix = matrix.astype(jnp.float32)
    return matrix / jnp.sqrt(jnp.mean(matrix * matrix, axis=-1, keepdims=True) + epsilon)


def renorm(updated, initial):
    target = jnp.sqrt(jnp.mean(initial * initial, axis=-1, keepdims=True) + epsilon)
    current = jnp.sqrt(jnp.mean(updated * updated, axis=-1, keepdims=True) + epsilon)
    return (updated * (target / current)).astype(jnp.bfloat16)


def band_attention(queries, key_rows, value_rows, query_pos, key_pos, score_scale):
    scores = (
        jnp.einsum("qhd,khd->hqk", queries, key_rows, preferred_element_type=jnp.float32)
        * score_scale
    )
    key_mask = (
        (key_pos[None, :] <= query_pos[:, None])
        & (key_pos[None, :] > query_pos[:, None] - WINDOW)
        & (key_pos[None, :] >= 0)
    )
    key_mask = key_mask[None]
    row_max = jnp.max(jnp.where(key_mask, scores, -1e30), axis=2, keepdims=True)
    raised = jnp.where(key_mask, jnp.exp(scores - row_max), 0.0)
    probs = (raised / jnp.sum(raised, axis=2, keepdims=True)).astype(jnp.bfloat16)
    return jnp.einsum("hqk,khd->qhd", probs, value_rows, preferred_element_type=jnp.float32)


def fast_gradient(weights, key_part, value_part, rate_part):
    pre_gate = jnp.einsum(
        "rhd,hde->rhe", key_part, weights[:, 0], preferred_element_type=jnp.float32
    )
    pre_up = jnp.einsum("rhd,hde->rhe", key_part, weights[:, 1], preferred_element_type=jnp.float32)
    sigma = jax.nn.sigmoid(pre_gate)
    gated = pre_gate * sigma
    hidden = (gated * pre_up).astype(jnp.bfloat16)
    target = (rate_part.astype(jnp.float32)[:, :, None] * value_part.astype(jnp.float32)).astype(
        jnp.bfloat16
    )
    grad_down = jnp.einsum("rhe,rhd->hed", hidden, target, preferred_element_type=jnp.float32)
    back_hidden = jnp.einsum(
        "rhd,hed->rhe", target, weights[:, 2], preferred_element_type=jnp.float32
    )
    gate_delta = (back_hidden * pre_up * sigma * (1.0 + pre_gate * (1.0 - sigma))).astype(
        jnp.bfloat16
    )
    up_delta = (back_hidden * gated).astype(jnp.bfloat16)
    grad_gate = jnp.einsum("rhd,rhe->hde", key_part, gate_delta, preferred_element_type=jnp.float32)
    grad_up = jnp.einsum("rhd,rhe->hde", key_part, up_delta, preferred_element_type=jnp.float32)
    return jnp.stack([grad_gate, grad_up, grad_down], 1)


def fast_apply(weights, query_part):
    app_gate = jnp.einsum(
        "rhd,hde->rhe", query_part, weights[:, 0], preferred_element_type=jnp.float32
    )
    app_up = jnp.einsum(
        "rhd,hde->rhe", query_part, weights[:, 1], preferred_element_type=jnp.float32
    )
    app_hidden = (app_gate * jax.nn.sigmoid(app_gate) * app_up).astype(jnp.bfloat16)
    result = jnp.einsum(
        "rhe,hed->rhd", app_hidden, weights[:, 2], preferred_element_type=jnp.float32
    )
    return result.astype(jnp.bfloat16)


def update_weights(weights, partial_value, initial):
    total = lax.psum(partial_value.astype(jnp.bfloat16), "tok").astype(jnp.float32)
    return renorm(weights.astype(jnp.float32) + total, initial)


def general_body(tokens, qkv_maps, rate_map, fast_init):
    tok_rows = tokens.shape[0]
    head_count = qkv_maps.shape[0]
    head_width = qkv_maps.shape[1]
    groups = lax.axis_size("tok")
    logit_terms = jnp.dot(tokens, rate_map, preferred_element_type=jnp.float32)
    logits = lax.psum_scatter(
        logit_terms.astype(jnp.bfloat16), "head", scatter_dimension=1, tiled=True
    ).astype(jnp.float32)
    rate = (rate_base * jax.nn.softplus(logits)).astype(jnp.bfloat16)
    inputs = tokens.reshape(tok_rows, head_count, head_width)
    projected = jnp.einsum("rhd,hde->rhe", inputs, qkv_maps, preferred_element_type=jnp.float32)
    queries = projected[:, :, :head_width].astype(jnp.bfloat16)
    key_rows = projected[:, :, head_width : 2 * head_width].astype(jnp.bfloat16)
    value_rows = projected[:, :, 2 * head_width :].astype(jnp.bfloat16)
    tail_rows = min(WINDOW, tok_rows)
    edge = jnp.stack([key_rows, value_rows], 0)
    distance = 0
    received = [from_behind(edge, "tok", distance + 1)]
    anchor = lax.axis_index("tok") * tok_rows
    offsets = jnp.arange(tail_rows, dtype=jnp.int32)
    distance = 1
    arrived = received[distance - 1]
    key_parts = [arrived[0]]
    value_parts = [arrived[1]]
    position_parts = [anchor - distance * tok_rows + tok_rows - tail_rows + offsets]
    local_pos = anchor + jnp.arange(tok_rows, dtype=jnp.int32)
    all_keys = jnp.concatenate(key_parts + [key_rows], 0)
    all_values = jnp.concatenate(value_parts + [value_rows], 0)
    all_pos = jnp.concatenate(position_parts + [local_pos], 0)
    attended = band_attention(
        queries, all_keys, all_values, local_pos, all_pos, head_width ** (-0.5)
    )
    q_norm = rms_rows(queries).astype(jnp.bfloat16)
    k_norm = rms_rows(key_rows).astype(jnp.bfloat16)
    initial = fast_init.astype(jnp.float32)
    weights = fast_init
    own_block = lax.axis_index("tok") // (groups // 2)
    fast_out = jnp.zeros_like(q_norm)
    for half_index in range(2):
        partial_value = fast_gradient(weights, k_norm, value_rows, rate)
        partial_value = jnp.where(own_block == half_index, partial_value, 0.0)
        weights = update_weights(weights, partial_value, initial)
        applied = fast_apply(weights, q_norm)
        fast_out = jnp.where(own_block == half_index, applied, fast_out)
    combined = (attended + fast_out.astype(jnp.float32)).astype(jnp.bfloat16)
    return combined.reshape(tok_rows, head_count * head_width)


def matmul(left, right):
    return jnp.dot(left, right, preferred_element_type=jnp.float32)


def matmul_nt(left, right):
    return lax.dot_general(left, right, (((1,), (1,)), ((), ())), preferred_element_type=jnp.float32)


def matmul_tn(left, right):
    return lax.dot_general(left, right, (((0,), (0,)), ((), ())), preferred_element_type=jnp.float32)


def unit_rows(rows):
    rows = rows.astype(jnp.float32)
    scale = lax.rsqrt(jnp.mean(rows * rows, axis=-1, keepdims=True) + epsilon)
    return (rows * scale).astype(jnp.bfloat16)


def logistic(a):
    return 0.5 * jnp.tanh(0.5 * a) + 0.5


def fetch(source, target, sem, when=None):
    copy = pltpu.make_async_copy(source, target, sem)
    if when is None:
        copy.start()
    else:
        pl.when(when)(copy.start)


def fetched(target, sem):
    pltpu.make_async_copy(target, target, sem).wait()


def learn(at, x, source, m, rate_row, pool, put_query, put_key_value):
    rows, width = x.shape[1:]
    here = pl.ds(pl.multiple_of(rows * at, rows), rows)
    key_rows = matmul(x[source], m[:, width : 2 * width]).astype(jnp.bfloat16)
    value_rows = matmul(x[source], m[:, 2 * width :]).astype(jnp.bfloat16)
    if put_key_value is not None:
        put_key_value(key_rows, value_rows)
    pool[0, here] = unit_rows(key_rows)
    spread = jnp.broadcast_to(rate_row, (128, rows)).T
    spread = jnp.concatenate([spread] * (width // 128), 1)
    pool[2, here] = (spread * value_rows.astype(jnp.float32)).astype(jnp.bfloat16)

    if put_query is not None:

        @pl.when(at % 2 == 0)
        def _():
            put_query(matmul(x[source], m[:, :width]).astype(jnp.bfloat16))


def deltas(at, rows, w, pool, both=None):
    here = pl.ds(pl.multiple_of(rows * at, rows), rows)
    gate = matmul(pool[0, here], w[0]).astype(jnp.bfloat16)
    up = matmul(pool[0, here], w[1]).astype(jnp.bfloat16)
    back = matmul_nt(pool[2, here], w[2]).astype(jnp.bfloat16)
    sigma = logistic(gate)
    gated = gate * sigma
    pool[1, here] = gated * up
    width = gate.shape[1]
    gate_delta = back * up * sigma * (1 + gate * (1 - sigma))
    up_delta = back * gated
    if both is None:
        pool[3, here] = gate_delta
        pool[4, here] = up_delta
    else:
        both[here, :width] = gate_delta
        both[here, width:] = up_delta


def gradient(at, pool, rows):
    return matmul_tn(pool[at // 2, :rows], pool[jnp.where(at == 2, 2, 3 + at), :rows])


def gradients(rows, pool, both, take):
    width = pool.shape[2]
    grads = matmul_tn(pool[0, :rows], both[:rows])
    take(0, grads[:, :width])
    take(1, grads[:, width:])
    take(2, matmul_tn(pool[1, :rows], pool[2, :rows]))


def renew(updated, initial):
    origin = initial.astype(jnp.float32)
    wanted = jnp.mean(origin * origin, axis=-1, keepdims=True) + epsilon
    held = jnp.mean(updated * updated, axis=-1, keepdims=True) + epsilon
    return (updated * (jnp.sqrt(wanted) * lax.rsqrt(held))).astype(jnp.bfloat16)


def begin_kernel(count, table, *refs):
    near, far, refs = refs[:count], refs[count : count + 2], refs[count + 2 :]
    maps, rate, initial, state, x, m, w, fresh, kept, grads, pool, both, sems = refs
    rows = x.shape[1]
    updates = table[0] > 0
    fetch(maps, m, sems.at[count + 2])
    for at in range(count):
        fetch(near[at], x.at[at], sems.at[at], updates)
    for at in range(2):
        fetch(far[at], x.at[count + at], sems.at[count + at])
    fetch(initial, w, sems.at[count + 3])
    fetched(m, sems.at[count + 2])

    @pl.when(updates)
    def _():
        @pl.loop(0, count, unroll=True)
        def _(at):
            fetched(x.at[at], sems.at[at])
            learn(at, x, at, m, rate[pl.ds(table[1 + at], 1)], pool, None, None)

        fetched(w, sems.at[count + 3])
        pl.loop(0, count, unroll=True)(lambda at: deltas(at, rows, w, pool, both))

        def take(at, grad):
            fresh[at] = renew(w[at].astype(jnp.float32) + grad, w[at])

        gradients(count * rows, pool, both, take)

    @pl.when(jnp.logical_not(updates))
    def _():
        fetched(w, sems.at[count + 3])
        fresh[...] = w[...]

    send = [pltpu.make_async_copy(fresh, state.at[pl.ds(0, 3)], sems.at[0])]
    send[0].start()

    @pl.loop(0, 2, unroll=True)
    def _(at):
        def put_query(query_rows):
            kept[0] = query_rows

        def put_key_value(key_rows, value_rows):
            kept[1 + at] = key_rows
            kept[3 + at] = value_rows

        fetched(x.at[count + at], sems.at[count + at])
        learn(at, x, count + at, m, rate[pl.ds(table[1 + count + at], 1)], pool, put_query, put_key_value)

    send.append(pltpu.make_async_copy(kept, state.at[pl.ds(3, 5)], sems.at[1]))
    send[1].start()
    pl.loop(0, 2, unroll=True)(lambda at: deltas(at, rows, fresh, pool, both))

    def take(at, grad):
        grads[at] = grad.astype(jnp.bfloat16)

    gradients(2 * rows, pool, both, take)

    send.append(pltpu.make_async_copy(grads, state.at[pl.ds(8, 3)], sems.at[2]))
    send[2].start()
    for copy in send:
        copy.wait()


def begin(table, near, far, maps, rate, initial):
    rows, width = near[0].shape
    count = len(near)
    anywhere = pl.BlockSpec(memory_space=pl.ANY)
    bfloat = functools.partial(pltpu.VMEM, dtype=jnp.bfloat16)
    operands = [*near, *far, maps]
    return pl.pallas_call(
        functools.partial(begin_kernel, count),
        grid_spec=pltpu.PrefetchScalarGridSpec(
            num_scalar_prefetch=1,
            grid=(),
            in_specs=[anywhere] * len(operands) + [pl.BlockSpec(memory_space=pltpu.VMEM), anywhere],
            out_specs=anywhere,
            scratch_shapes=[
                bfloat((count + 2, rows, width)),
                bfloat(maps.shape),
                bfloat(initial.shape),
                bfloat(initial.shape),
                bfloat((5, rows, width)),
                bfloat(initial.shape),
                bfloat((3, count * rows, width)),
                bfloat((count * rows, 2 * width)),
                pltpu.SemaphoreType.DMA((count + 4,)),
            ],
        ),
        out_shape=jax.ShapeDtypeStruct((STATE, rows, width), jnp.bfloat16),
        compiler_params=pltpu.CompilerParams(vmem_limit_bytes=VMEM_LIMIT),
        cost_estimate=pl.CostEstimate(flops=1, bytes_accessed=1, transcendentals=0),
        name="begin",
    )(table, *operands, rate, initial)


def stage_kernel(counts, table, *refs):
    count, befores, begun = counts
    slots = count // 2 + begun
    wanted = count // 2
    blocks, refs = refs[:count], refs[count:]
    before, refs = refs[:befores], refs[befores:]
    state, refs = refs[0], refs[1:]
    (maps, rate, initial), refs = refs[:3], refs[3:]
    results, new, refs = refs[:wanted], refs[wanted : wanted + begun], refs[wanted + begun :]
    x, m, w, start, fresh, k, v, q, attended, pool, out, sems, *grads = refs
    rows, width = x.shape[1:]
    part = rows // 2
    updates, answers, first, there = table[0] > 0, table[1] > 0, table[2], table[3] > 0
    at_maps, at_start, at_weights, at_new, at_held, at_grads = (sems.at[count + 1 + at] for at in range(6))
    if begun:
        send_new = pltpu.make_async_copy(fresh, new[0].at[pl.ds(11, 3)], at_new)
    send = [pltpu.make_async_copy(out.at[at], results[at], sems.at[count + 7 + at]) for at in range(wanted)]

    def span(at, size=rows):
        return pl.ds(pl.multiple_of(at, part), size)

    def answer():
        row = lax.broadcasted_iota(jnp.int32, (part, rows + part), 0)
        column = lax.broadcasted_iota(jnp.int32, (part, rows + part), 1)
        band = (column > row) & (column <= row + rows)

        @pl.loop(0, wanted)
        def _(at):
            @pl.loop(0, 2, unroll=begun > 0)
            def _(half):
                own = span(part * half, part)
                base = rows * table[6 + 2 * at] + part * half
                scores = matmul_nt(q[at, own], k[span(base, rows + part)]) * (width ** -0.5)
                floor = jnp.where(first > 0, 0, rows - base)
                scores = jnp.where(band & (column >= floor), scores, -1e30)
                raised = jnp.exp(scores - jnp.max(scores, axis=1, keepdims=True))
                total = jnp.sum(raised, axis=1, keepdims=True)
                values = v[span(base, rows + part)]
                attended[own] = matmul(raised.astype(jnp.bfloat16), values) * (1.0 / total)

            queries = unit_rows(q[at])
            gate = matmul(queries, fresh[0])
            up = matmul(queries, fresh[1])
            inner = (gate * logistic(gate) * up).astype(jnp.bfloat16)
            fast = matmul(inner, fresh[2]).astype(jnp.bfloat16).astype(jnp.float32)
            out[at] = (attended[...] + fast).astype(jnp.bfloat16)

        for copy in send:
            copy.start()
        for copy in send:
            copy.wait()

    @pl.when(updates | answers)
    def _():
        fetch(maps, m, at_maps)
        for at in range(count):
            fetch(blocks[at], x.at[at], sems.at[at])
        for at in range(befores):
            fetch(before[at], x.at[count], sems.at[count], there & (table[4] == at))
        fetch(state.at[pl.ds(table[5], 3)], w, at_weights)
        fetch(initial, start, at_start)
        if begun:
            to = span(rows * (table[6 + count + 1] + 1))
            fetch(state.at[5], k.at[to], at_held)
            fetch(state.at[7], v.at[to], at_held)
            fetch(state.at[pl.ds(8, 3)], grads[0], at_grads)
        fetched(m, at_maps)

        @pl.loop(0, count, unroll=begun > 0)
        def _(at):
            to = span(rows * (table[6 + at] + 1))

            def put_query(query_rows):
                q[at // 2] = query_rows

            def put_key_value(key_rows, value_rows):
                k[to] = key_rows
                v[to] = value_rows

            fetched(x.at[at], sems.at[at])
            learn(at, x, at, m, rate[pl.ds(first + table[6 + at], 1)], pool, put_query, put_key_value)

        @pl.when(there)
        def _():
            fetched(x.at[count], sems.at[count])
            k[:rows] = matmul(x[count], m[:, width : 2 * width]).astype(jnp.bfloat16)
            v[:rows] = matmul(x[count], m[:, 2 * width :]).astype(jnp.bfloat16)

        @pl.when(jnp.logical_not(there))
        def _():
            k[:rows] = jnp.zeros((rows, width), jnp.bfloat16)
            v[:rows] = jnp.zeros((rows, width), jnp.bfloat16)

        fetched(w, at_weights)
        fetched(start, at_start)
        if begun:
            fetched(k.at[pl.ds(0, 2 * rows)], at_held)
            fetched(grads[0], at_grads)

        @pl.when(updates)
        def _():
            pl.loop(0, count, unroll=begun > 0)(lambda at: deltas(at, rows, w, pool))

            @pl.loop(0, 3)
            def _(at):
                updated = w[at].astype(jnp.float32) + gradient(at, pool, count * rows)
                if begun:
                    updated = updated + grads[0][at].astype(jnp.float32)
                fresh[at] = renew(updated, start[at])

            if begun:
                send_new.start()

        @pl.when(jnp.logical_not(updates))
        def _():
            fresh[...] = w[...]

        pl.when(answers)(answer)
        if begun:
            send_new.wait()


def stage(table, blocks, before, state, maps, rate, initial, begun=False, scale=24):
    count, begun = len(blocks), int(begun)
    rows, width = blocks[0].shape
    matrices = initial.shape
    bfloat = functools.partial(pltpu.VMEM, dtype=jnp.bfloat16)
    anywhere = pl.BlockSpec(memory_space=pl.ANY)
    slots = count // 2 + begun
    stretch = 2 * slots * rows
    wanted = count // 2
    operands = [*blocks, *before, state, maps]
    return pl.pallas_call(
        functools.partial(stage_kernel, (count, len(before), begun)),
        grid_spec=pltpu.PrefetchScalarGridSpec(
            num_scalar_prefetch=1,
            grid=(),
            in_specs=[anywhere] * len(operands) + [pl.BlockSpec(memory_space=pltpu.VMEM), anywhere],
            out_specs=[anywhere] * (wanted + begun),
            scratch_shapes=[
                bfloat((count + 1, rows, width)),
                bfloat(maps.shape),
                bfloat(matrices),
                bfloat(matrices),
                bfloat(matrices),
                bfloat((stretch + rows, width)),
                bfloat((stretch + rows, width)),
                bfloat((wanted, rows, width)),
                pltpu.VMEM((rows, width), jnp.float32),
                bfloat((5, count * rows, width)),
                bfloat((wanted, rows, width)),
                pltpu.SemaphoreType.DMA((count + 7 + wanted,)),
            ]
            + [bfloat(matrices)] * begun,
        ),
        out_shape=[jax.ShapeDtypeStruct((rows, width), jnp.bfloat16)] * wanted
        + [jax.ShapeDtypeStruct(state.shape, state.dtype)] * begun,
        input_output_aliases={1 + count + len(before): wanted} if begun else {},
        compiler_params=pltpu.CompilerParams(vmem_limit_bytes=VMEM_LIMIT),
        cost_estimate=pl.CostEstimate(flops=scale * stretch * width * width, bytes_accessed=scale * stretch * width, transcendentals=0),
        name="stage",
    )(table, *operands, rate, initial)


def banded(queries, keys, values, floor):
    part, window = queries.shape[0], keys.shape[0]
    row = lax.broadcasted_iota(jnp.int32, (part, window), 0)
    column = lax.broadcasted_iota(jnp.int32, (part, window), 1)
    band = (column > row) & (column <= row + window - part) & (column >= floor)
    scores = matmul_nt(queries, keys) * (queries.shape[1] ** -0.5)
    scores = jnp.where(band, scores, -1e30)
    raised = jnp.exp(scores - jnp.max(scores, axis=1, keepdims=True))
    total = jnp.sum(raised, axis=1, keepdims=True)
    return matmul(raised.astype(jnp.bfloat16), values) * (1.0 / total)


def finish_kernel(befores, table, *refs):
    before, refs = refs[:befores], refs[befores:]
    maps, state, result, x, m, w, q, k, v, attended, out, sems = refs
    rows, width = x.shape
    part = rows // 2
    there = table[0] > 0
    for at in range(befores):
        fetch(before[at], x, sems.at[0], there & (table[1] == at))
    fetch(maps, m, sems.at[1], there)
    fetch(state.at[3], q, sems.at[2])
    fetch(state.at[4], k.at[pl.ds(rows, rows)], sems.at[3])
    fetch(state.at[6], v.at[pl.ds(rows, rows)], sems.at[4])
    fetch(state.at[pl.ds(11, 3)], w, sems.at[5])

    @pl.when(there)
    def _():
        fetched(x, sems.at[0])
        fetched(m, sems.at[1])
        k[:rows] = matmul(x[...], m[:, width : 2 * width]).astype(jnp.bfloat16)
        v[:rows] = matmul(x[...], m[:, 2 * width :]).astype(jnp.bfloat16)

    @pl.when(jnp.logical_not(there))
    def _():
        k[:rows] = jnp.zeros((rows, width), jnp.bfloat16)
        v[:rows] = jnp.zeros((rows, width), jnp.bfloat16)

    fetched(q, sems.at[2])
    fetched(q, sems.at[3])
    fetched(q, sems.at[4])

    @pl.loop(0, 2)
    def _(half):
        first = part * half
        window = pl.ds(first, rows + part)
        floor = jnp.where(there, 0, rows - first)
        attended[pl.ds(first, part)] = banded(q[pl.ds(first, part)], k[window], v[window], floor)

    fetched(w, sems.at[5])
    queries = unit_rows(q[...])
    gate = matmul(queries, w[0])
    up = matmul(queries, w[1])
    inner = (gate * logistic(gate) * up).astype(jnp.bfloat16)
    fast = matmul(inner, w[2]).astype(jnp.bfloat16).astype(jnp.float32)
    out[...] = (attended[...] + fast).astype(jnp.bfloat16)
    copy = pltpu.make_async_copy(out, result, sems.at[0])
    copy.start()
    copy.wait()


def finish(table, before, maps, state):
    rows, width = before[0].shape
    anywhere = pl.BlockSpec(memory_space=pl.ANY)
    bfloat = functools.partial(pltpu.VMEM, dtype=jnp.bfloat16)
    return pl.pallas_call(
        functools.partial(finish_kernel, len(before)),
        grid_spec=pltpu.PrefetchScalarGridSpec(
            num_scalar_prefetch=1,
            grid=(),
            in_specs=[anywhere] * (len(before) + 2),
            out_specs=anywhere,
            scratch_shapes=[
                bfloat((rows, width)),
                bfloat(maps.shape),
                bfloat((3,) + state.shape[1:]),
                bfloat((rows, width)),
                bfloat((2 * rows, width)),
                bfloat((2 * rows, width)),
                pltpu.VMEM((rows, width), jnp.float32),
                bfloat((rows, width)),
                pltpu.SemaphoreType.DMA((6,)),
            ],
        ),
        out_shape=jax.ShapeDtypeStruct((rows, width), jnp.bfloat16),
        compiler_params=pltpu.CompilerParams(vmem_limit_bytes=VMEM_LIMIT),
        cost_estimate=pl.CostEstimate(flops=1, bytes_accessed=1, transcendentals=0),
        name="finish",
    )(table, *before, maps, state)


def after(array, *others):
    return lax.optimization_barrier((array, *others))[0]


def head_body(tokens, qkv_maps, rate_map, fast_init):
    rows = tokens.shape[0]
    heads, width = qkv_maps.shape[:2]
    groups = lax.axis_size("tok")
    chips = groups // 2
    slots = chips // 2
    last = chips - 1
    me = lax.axis_index("tok")
    chip, core = me // 2, me % 2
    is_first = (chip < slots).astype(jnp.int32)

    def swap(block, bits):
        return lax.ppermute(block, "tok", [(i, i ^ bits) for i in range(groups)])

    def piece(slot, source, index):
        return lax.dynamic_slice_in_dim(source, (index ^ slot) * width, width, 1)

    maps = lax.dynamic_index_in_dim(qkv_maps, chip, 0, False)
    initial = lax.dynamic_index_in_dim(fast_init, chip, 0, False)
    same = {slot: swap(piece(slot, tokens, chip), 2 * slot) for slot in range(1, slots)}
    same[last] = swap(piece(last, tokens, chip), 2 * last)
    terms = lax.dot_general(
        rate_map, tokens, (((0,), (1,)), ((), ())), preferred_element_type=jnp.float32
    )
    terms = lax.all_to_all(jnp.repeat(terms, 2, axis=0), ("head", "tok"), 0, 0, tiled=True)
    logits = jnp.sum(terms.reshape(-1, groups, rows), 0)
    rate = (rate_base * jax.nn.softplus(logits)).astype(jnp.bfloat16).astype(jnp.float32)
    source = after(tokens, *(same[slot] for slot in range(1, slots)))
    for slot in range(slots, last):
        same[slot] = swap(piece(slot, source, chip), 2 * slot)
    same[0] = piece(0, source, chip)
    other = {slot: swap(same[slot], 1) for slot in range(slots)}

    def integers(entries):
        return jnp.stack([jnp.asarray(entry, jnp.int32) for entry in entries])

    def places(slot):
        return [2 * ((chip ^ slot) % slots) + core, 2 * ((chip ^ slot) % slots) + (1 - core)]

    def opening(slot):
        return 2 * slots * ((chip ^ slot) // slots)

    def table(slots_in, updates, answers, weights_at):
        first = opening(slots_in[0])
        before = (chip ^ (slots - 1)) % slots
        flags = [updates, answers, first, (first > 0) & (core == 0), before, weights_at]
        return integers(flags + [place for slot in slots_in for place in places(slot)])

    near_slots, far_slots = range(slots), range(slots, chips)
    near_blocks = [block for slot in near_slots for block in (same[slot], other[slot])]
    near_others = [other[slot] for slot in near_slots]
    shared = dict(maps=maps, rate=rate, initial=initial)
    other[last] = swap(same[last], 1)
    rates_in = [opening(slot) + place for slot in (*near_slots, last) for place in places(slot)]
    state = begin(integers([is_first] + rates_in), near_blocks, [same[last], other[last]], **shared)
    far_blocks = []
    for slot in far_slots[:-1]:
        same[slot] = after(same[slot], state)
        other[slot] = swap(same[slot], 1)
        far_blocks += [same[slot], other[slot]]
    *far_results, state = stage(
        table(far_slots, True, True, 0), far_blocks, near_others, state, begun=True, **shared
    )
    near_results = stage(
        table(near_slots, 1 - is_first, True, 11 * (1 - is_first)), near_blocks,
        [other[slot] for slot in far_slots], state, scale=0, **shared
    )
    at = chip ^ last
    place = jnp.where(core == 1, at, at - 1)
    last_result = finish(
        integers([place >= 0, chip ^ jnp.maximum(place, 0)]), [other[slot] for slot in range(chips)], maps, state
    )
    results = [*near_results, *far_results, last_result]
    combined = jnp.zeros_like(tokens)
    for slot in (*far_slots[:-1], 0, last, *range(1, slots)):
        result = swap(results[slot], 2 * slot) if slot else results[slot]
        combined = lax.dynamic_update_slice_in_dim(combined, result, (chip ^ slot) * width, 1)
    return combined


def body(tokens, qkv_maps, rate_map, fast_init):
    groups = lax.axis_size("tok")
    heads = qkv_maps.shape[0]
    powers = groups & (groups - 1) == 0 and groups > 2
    if powers and groups == 2 * heads and tokens.shape[0] == WINDOW:
        return head_body(tokens, qkv_maps, rate_map, fast_init)
    return general_body(tokens, qkv_maps, rate_map, fast_init)


def solution(mesh):
    in_specs = (
        P("tok", "head"),
        P("head", None, None),
        P("head", None),
        P("head", None, None, None),
    )
    out_specs = P("tok", "head")
    return jax.shard_map(body, mesh=mesh, in_specs=in_specs, out_specs=out_specs, check_vma=False)
```

```python
import functools

import jax
import jax.numpy as jnp
from jax import lax
from jax.experimental import pallas as pl
from jax.experimental.pallas import tpu as pltpu
from jax.sharding import PartitionSpec as P

WINDOW = 512


rate_base = 0.003
epsilon = 1e-06
VMEM_LIMIT = 36 * 1024 * 1024
STATE = 64


def from_behind(block, axis, distance):
    devices = range(lax.axis_size(axis))
    route = [(i - distance, i) for i in devices if i - distance in devices]
    return lax.ppermute(block, axis, route)


def rms_rows(matrix):
    matrix = matrix.astype(jnp.float32)
    return matrix / jnp.sqrt(jnp.mean(matrix * matrix, axis=-1, keepdims=True) + epsilon)


def renorm(updated, initial):
    target = jnp.sqrt(jnp.mean(initial * initial, axis=-1, keepdims=True) + epsilon)
    current = jnp.sqrt(jnp.mean(updated * updated, axis=-1, keepdims=True) + epsilon)
    return (updated * (target / current)).astype(jnp.bfloat16)


def band_attention(queries, key_rows, value_rows, query_pos, key_pos, score_scale):
    scores = (
        jnp.einsum("qhd,khd->hqk", queries, key_rows, preferred_element_type=jnp.float32)
        * score_scale
    )
    key_mask = (
        (key_pos[None, :] <= query_pos[:, None])
        & (key_pos[None, :] > query_pos[:, None] - WINDOW)
        & (key_pos[None, :] >= 0)
    )
    key_mask = key_mask[None]
    row_max = jnp.max(jnp.where(key_mask, scores, -1e30), axis=2, keepdims=True)
    raised = jnp.where(key_mask, jnp.exp(scores - row_max), 0.0)
    probs = (raised / jnp.sum(raised, axis=2, keepdims=True)).astype(jnp.bfloat16)
    return jnp.einsum("hqk,khd->qhd", probs, value_rows, preferred_element_type=jnp.float32)


def fast_gradient(weights, key_part, value_part, rate_part):
    pre_gate = jnp.einsum(
        "rhd,hde->rhe", key_part, weights[:, 0], preferred_element_type=jnp.float32
    )
    pre_up = jnp.einsum("rhd,hde->rhe", key_part, weights[:, 1], preferred_element_type=jnp.float32)
    sigma = jax.nn.sigmoid(pre_gate)
    gated = pre_gate * sigma
    hidden = (gated * pre_up).astype(jnp.bfloat16)
    target = (rate_part.astype(jnp.float32)[:, :, None] * value_part.astype(jnp.float32)).astype(
        jnp.bfloat16
    )
    grad_down = jnp.einsum("rhe,rhd->hed", hidden, target, preferred_element_type=jnp.float32)
    back_hidden = jnp.einsum(
        "rhd,hed->rhe", target, weights[:, 2], preferred_element_type=jnp.float32
    )
    gate_delta = (back_hidden * pre_up * sigma * (1.0 + pre_gate * (1.0 - sigma))).astype(
        jnp.bfloat16
    )
    up_delta = (back_hidden * gated).astype(jnp.bfloat16)
    grad_gate = jnp.einsum("rhd,rhe->hde", key_part, gate_delta, preferred_element_type=jnp.float32)
    grad_up = jnp.einsum("rhd,rhe->hde", key_part, up_delta, preferred_element_type=jnp.float32)
    return jnp.stack([grad_gate, grad_up, grad_down], 1)


def fast_apply(weights, query_part):
    app_gate = jnp.einsum(
        "rhd,hde->rhe", query_part, weights[:, 0], preferred_element_type=jnp.float32
    )
    app_up = jnp.einsum(
        "rhd,hde->rhe", query_part, weights[:, 1], preferred_element_type=jnp.float32
    )
    app_hidden = (app_gate * jax.nn.sigmoid(app_gate) * app_up).astype(jnp.bfloat16)
    result = jnp.einsum(
        "rhe,hed->rhd", app_hidden, weights[:, 2], preferred_element_type=jnp.float32
    )
    return result.astype(jnp.bfloat16)


def update_weights(weights, partial_value, initial):
    total = lax.psum(partial_value.astype(jnp.bfloat16), "tok").astype(jnp.float32)
    return renorm(weights.astype(jnp.float32) + total, initial)


def general_body(tokens, qkv_maps, rate_map, fast_init):
    tok_rows = tokens.shape[0]
    head_count = qkv_maps.shape[0]
    head_width = qkv_maps.shape[1]
    groups = lax.axis_size("tok")
    logit_terms = jnp.dot(tokens, rate_map, preferred_element_type=jnp.float32)
    logits = lax.psum_scatter(
        logit_terms.astype(jnp.bfloat16), "head", scatter_dimension=1, tiled=True
    ).astype(jnp.float32)
    rate = (rate_base * jax.nn.softplus(logits)).astype(jnp.bfloat16)
    inputs = tokens.reshape(tok_rows, head_count, head_width)
    projected = jnp.einsum("rhd,hde->rhe", inputs, qkv_maps, preferred_element_type=jnp.float32)
    queries = projected[:, :, :head_width].astype(jnp.bfloat16)
    key_rows = projected[:, :, head_width : 2 * head_width].astype(jnp.bfloat16)
    value_rows = projected[:, :, 2 * head_width :].astype(jnp.bfloat16)
    tail_rows = min(WINDOW, tok_rows)
    edge = jnp.stack([key_rows, value_rows], 0)
    distance = 0
    received = [from_behind(edge, "tok", distance + 1)]
    anchor = lax.axis_index("tok") * tok_rows
    offsets = jnp.arange(tail_rows, dtype=jnp.int32)
    distance = 1
    arrived = received[distance - 1]
    key_parts = [arrived[0]]
    value_parts = [arrived[1]]
    position_parts = [anchor - distance * tok_rows + tok_rows - tail_rows + offsets]
    local_pos = anchor + jnp.arange(tok_rows, dtype=jnp.int32)
    all_keys = jnp.concatenate(key_parts + [key_rows], 0)
    all_values = jnp.concatenate(value_parts + [value_rows], 0)
    all_pos = jnp.concatenate(position_parts + [local_pos], 0)
    attended = band_attention(
        queries, all_keys, all_values, local_pos, all_pos, head_width ** (-0.5)
    )
    q_norm = rms_rows(queries).astype(jnp.bfloat16)
    k_norm = rms_rows(key_rows).astype(jnp.bfloat16)
    initial = fast_init.astype(jnp.float32)
    weights = fast_init
    own_block = lax.axis_index("tok") // (groups // 2)
    fast_out = jnp.zeros_like(q_norm)
    for half_index in range(2):
        partial_value = fast_gradient(weights, k_norm, value_rows, rate)
        partial_value = jnp.where(own_block == half_index, partial_value, 0.0)
        weights = update_weights(weights, partial_value, initial)
        applied = fast_apply(weights, q_norm)
        fast_out = jnp.where(own_block == half_index, applied, fast_out)
    combined = (attended + fast_out.astype(jnp.float32)).astype(jnp.bfloat16)
    return combined.reshape(tok_rows, head_count * head_width)


def matmul(left, right):
    return jnp.dot(left, right, preferred_element_type=jnp.float32)


def matmul_nt(left, right):
    return lax.dot_general(left, right, (((1,), (1,)), ((), ())), preferred_element_type=jnp.float32)


def matmul_tn(left, right):
    return lax.dot_general(left, right, (((0,), (0,)), ((), ())), preferred_element_type=jnp.float32)


def unit_rows(rows):
    rows = rows.astype(jnp.float32)
    scale = lax.rsqrt(jnp.mean(rows * rows, axis=-1, keepdims=True) + epsilon)
    return (rows * scale).astype(jnp.bfloat16)


def logistic(a):
    return 0.5 * jnp.tanh(0.5 * a) + 0.5


def fetch(source, target, sem, when=None):
    copy = pltpu.make_async_copy(source, target, sem)
    if when is None:
        copy.start()
    else:
        pl.when(when)(copy.start)


def fetched(target, sem):
    pltpu.make_async_copy(target, target, sem).wait()


def learn(at, x, source, m, rate_row, pool, put_query, put_key_value):
    rows, width = x.shape[1:]
    here = pl.ds(pl.multiple_of(rows * at, rows), rows)
    key_rows = matmul(x[source], m[:, width : 2 * width]).astype(jnp.bfloat16)
    value_rows = matmul(x[source], m[:, 2 * width :]).astype(jnp.bfloat16)
    if put_key_value is not None:
        put_key_value(key_rows, value_rows)
    pool[0, here] = unit_rows(key_rows)
    spread = jnp.broadcast_to(rate_row, (128, rows)).T
    spread = jnp.concatenate([spread] * (width // 128), 1)
    pool[2, here] = (spread * value_rows.astype(jnp.float32)).astype(jnp.bfloat16)

    if put_query is not None:

        @pl.when(at % 2 == 0)
        def _():
            put_query(matmul(x[source], m[:, :width]).astype(jnp.bfloat16))


def deltas(at, rows, w, pool, both=None):
    here = pl.ds(pl.multiple_of(rows * at, rows), rows)
    gate = matmul(pool[0, here], w[0]).astype(jnp.bfloat16)
    up = matmul(pool[0, here], w[1]).astype(jnp.bfloat16)
    back = matmul_nt(pool[2, here], w[2]).astype(jnp.bfloat16)
    sigma = logistic(gate)
    gated = gate * sigma
    pool[1, here] = gated * up
    width = gate.shape[1]
    gate_delta = back * up * sigma * (1 + gate * (1 - sigma))
    up_delta = back * gated
    if both is None:
        pool[3, here] = gate_delta
        pool[4, here] = up_delta
    else:
        both[here, :width] = gate_delta
        both[here, width:] = up_delta


def gradient(at, pool, rows):
    return matmul_tn(pool[at // 2, :rows], pool[jnp.where(at == 2, 2, 3 + at), :rows])


def gradients(rows, pool, both, take):
    width = pool.shape[2]
    grads = matmul_tn(pool[0, :rows], both[:rows])
    take(0, grads[:, :width])
    take(1, grads[:, width:])
    take(2, matmul_tn(pool[1, :rows], pool[2, :rows]))


def renew(updated, initial):
    origin = initial.astype(jnp.float32)
    wanted = jnp.mean(origin * origin, axis=-1, keepdims=True) + epsilon
    held = jnp.mean(updated * updated, axis=-1, keepdims=True) + epsilon
    return (updated * (jnp.sqrt(wanted) * lax.rsqrt(held))).astype(jnp.bfloat16)


def begin_kernel(count, table, *refs):
    near, far, refs = refs[:count], refs[count : count + 2], refs[count + 2 :]
    maps, rate, initial, state, x, m, w, fresh, kept, grads, pool, both, sems = refs
    rows = x.shape[1]
    updates = table[0] > 0
    fetch(maps, m, sems.at[count + 2])
    for at in range(count):
        fetch(near[at], x.at[at], sems.at[at], updates)
    for at in range(2):
        fetch(far[at], x.at[count + at], sems.at[count + at])
    fetch(initial, w, sems.at[count + 3])
    fetched(m, sems.at[count + 2])

    @pl.when(updates)
    def _():
        @pl.loop(0, count, unroll=True)
        def _(at):
            fetched(x.at[at], sems.at[at])
            learn(at, x, at, m, rate[pl.ds(table[1 + at], 1)], pool, None, None)

        fetched(w, sems.at[count + 3])
        pl.loop(0, count, unroll=True)(lambda at: deltas(at, rows, w, pool, both))

        def take(at, grad):
            fresh[at] = renew(w[at].astype(jnp.float32) + grad, w[at])

        gradients(count * rows, pool, both, take)

    @pl.when(jnp.logical_not(updates))
    def _():
        fetched(w, sems.at[count + 3])
        fresh[...] = w[...]

    send = [pltpu.make_async_copy(fresh, state.at[pl.ds(0, 3)], sems.at[0])]
    send[0].start()

    @pl.loop(0, 2, unroll=True)
    def _(at):
        def put_query(query_rows):
            kept[0] = query_rows

        def put_key_value(key_rows, value_rows):
            kept[1 + at] = key_rows
            kept[3 + at] = value_rows

        fetched(x.at[count + at], sems.at[count + at])
        learn(at, x, count + at, m, rate[pl.ds(table[1 + count + at], 1)], pool, put_query, put_key_value)

    send.append(pltpu.make_async_copy(kept, state.at[pl.ds(3, 5)], sems.at[1]))
    send[1].start()
    pl.loop(0, 2, unroll=True)(lambda at: deltas(at, rows, fresh, pool, both))

    def take(at, grad):
        grads[at] = grad.astype(jnp.bfloat16)

    gradients(2 * rows, pool, both, take)

    send.append(pltpu.make_async_copy(grads, state.at[pl.ds(8, 3)], sems.at[2]))
    send[2].start()
    for copy in send:
        copy.wait()


def begin(table, near, far, maps, rate, initial):
    rows, width = near[0].shape
    count = len(near)
    anywhere = pl.BlockSpec(memory_space=pl.ANY)
    bfloat = functools.partial(pltpu.VMEM, dtype=jnp.bfloat16)
    operands = [*near, *far, maps]
    return pl.pallas_call(
        functools.partial(begin_kernel, count),
        grid_spec=pltpu.PrefetchScalarGridSpec(
            num_scalar_prefetch=1,
            grid=(),
            in_specs=[anywhere] * len(operands) + [pl.BlockSpec(memory_space=pltpu.VMEM), anywhere],
            out_specs=anywhere,
            scratch_shapes=[
                bfloat((count + 2, rows, width)),
                bfloat(maps.shape),
                bfloat(initial.shape),
                bfloat(initial.shape),
                bfloat((5, rows, width)),
                bfloat(initial.shape),
                bfloat((3, count * rows, width)),
                bfloat((count * rows, 2 * width)),
                pltpu.SemaphoreType.DMA((count + 4,)),
            ],
        ),
        out_shape=jax.ShapeDtypeStruct((STATE, rows, width), jnp.bfloat16),
        compiler_params=pltpu.CompilerParams(vmem_limit_bytes=VMEM_LIMIT),
        cost_estimate=pl.CostEstimate(flops=1, bytes_accessed=1, transcendentals=0),
        name="begin",
    )(table, *operands, rate, initial)


def stage_kernel(counts, table, *refs):
    count, befores, begun = counts
    slots = count // 2 + begun
    wanted = count // 2
    blocks, refs = refs[:count], refs[count:]
    before, refs = refs[:befores], refs[befores:]
    state, refs = refs[0], refs[1:]
    (maps, rate, initial), refs = refs[:3], refs[3:]
    results, new, refs = refs[:wanted], refs[wanted : wanted + begun], refs[wanted + begun :]
    x, m, w, start, fresh, k, v, q, attended, pool, out, sems, *grads = refs
    rows, width = x.shape[1:]
    part = rows // 2
    updates, answers, first, there = table[0] > 0, table[1] > 0, table[2], table[3] > 0
    at_maps, at_start, at_weights, at_new, at_held, at_grads = (sems.at[count + 1 + at] for at in range(6))
    if begun:
        send_new = pltpu.make_async_copy(fresh, new[0].at[pl.ds(11, 3)], at_new)
    send = [pltpu.make_async_copy(out.at[at], results[at], sems.at[count + 7 + at]) for at in range(wanted)]

    def span(at, size=rows):
        return pl.ds(pl.multiple_of(at, part), size)

    def answer():
        row = lax.broadcasted_iota(jnp.int32, (part, rows + part), 0)
        column = lax.broadcasted_iota(jnp.int32, (part, rows + part), 1)
        band = (column > row) & (column <= row + rows)

        @pl.loop(0, wanted)
        def _(at):
            @pl.loop(0, 2, unroll=begun > 0)
            def _(half):
                own = span(part * half, part)
                base = rows * table[6 + 2 * at] + part * half
                scores = matmul_nt(q[at, own], k[span(base, rows + part)]) * (width ** -0.5)
                floor = jnp.where(first > 0, 0, rows - base)
                scores = jnp.where(band & (column >= floor), scores, -1e30)
                raised = jnp.exp(scores - jnp.max(scores, axis=1, keepdims=True))
                total = jnp.sum(raised, axis=1, keepdims=True)
                values = v[span(base, rows + part)]
                attended[own] = matmul(raised.astype(jnp.bfloat16), values) / total

            queries = unit_rows(q[at])
            gate = matmul(queries, fresh[0])
            up = matmul(queries, fresh[1])
            inner = (gate * logistic(gate) * up).astype(jnp.bfloat16)
            fast = matmul(inner, fresh[2]).astype(jnp.bfloat16).astype(jnp.float32)
            out[at] = (attended[...] + fast).astype(jnp.bfloat16)

        for copy in send:
            copy.start()
        for copy in send:
            copy.wait()

    @pl.when(updates | answers)
    def _():
        fetch(maps, m, at_maps)
        for at in range(count):
            fetch(blocks[at], x.at[at], sems.at[at])
        for at in range(befores):
            fetch(before[at], x.at[count], sems.at[count], there & (table[4] == at))
        fetch(state.at[pl.ds(table[5], 3)], w, at_weights)
        fetch(initial, start, at_start)
        if begun:
            to = span(rows * (table[6 + count + 1] + 1))
            fetch(state.at[5], k.at[to], at_held)
            fetch(state.at[7], v.at[to], at_held)
            fetch(state.at[pl.ds(8, 3)], grads[0], at_grads)
        fetched(m, at_maps)

        @pl.loop(0, count, unroll=begun > 0)
        def _(at):
            to = span(rows * (table[6 + at] + 1))

            def put_query(query_rows):
                q[at // 2] = query_rows

            def put_key_value(key_rows, value_rows):
                k[to] = key_rows
                v[to] = value_rows

            fetched(x.at[at], sems.at[at])
            learn(at, x, at, m, rate[pl.ds(first + table[6 + at], 1)], pool, put_query, put_key_value)

        @pl.when(there)
        def _():
            fetched(x.at[count], sems.at[count])
            k[:rows] = matmul(x[count], m[:, width : 2 * width]).astype(jnp.bfloat16)
            v[:rows] = matmul(x[count], m[:, 2 * width :]).astype(jnp.bfloat16)

        @pl.when(jnp.logical_not(there))
        def _():
            k[:rows] = jnp.zeros((rows, width), jnp.bfloat16)
            v[:rows] = jnp.zeros((rows, width), jnp.bfloat16)

        fetched(w, at_weights)
        fetched(start, at_start)
        if begun:
            fetched(k.at[pl.ds(0, 2 * rows)], at_held)
            fetched(grads[0], at_grads)

        @pl.when(updates)
        def _():
            pl.loop(0, count, unroll=begun > 0)(lambda at: deltas(at, rows, w, pool))

            @pl.loop(0, 3)
            def _(at):
                updated = w[at].astype(jnp.float32) + gradient(at, pool, count * rows)
                if begun:
                    updated = updated + grads[0][at].astype(jnp.float32)
                fresh[at] = renew(updated, start[at])

            if begun:
                send_new.start()

        @pl.when(jnp.logical_not(updates))
        def _():
            fresh[...] = w[...]

        pl.when(answers)(answer)
        if begun:
            send_new.wait()


def stage(table, blocks, before, state, maps, rate, initial, begun=False, scale=24):
    count, begun = len(blocks), int(begun)
    rows, width = blocks[0].shape
    matrices = initial.shape
    bfloat = functools.partial(pltpu.VMEM, dtype=jnp.bfloat16)
    anywhere = pl.BlockSpec(memory_space=pl.ANY)
    slots = count // 2 + begun
    stretch = 2 * slots * rows
    wanted = count // 2
    operands = [*blocks, *before, state, maps]
    return pl.pallas_call(
        functools.partial(stage_kernel, (count, len(before), begun)),
        grid_spec=pltpu.PrefetchScalarGridSpec(
            num_scalar_prefetch=1,
            grid=(),
            in_specs=[anywhere] * len(operands) + [pl.BlockSpec(memory_space=pltpu.VMEM), anywhere],
            out_specs=[anywhere] * (wanted + begun),
            scratch_shapes=[
                bfloat((count + 1, rows, width)),
                bfloat(maps.shape),
                bfloat(matrices),
                bfloat(matrices),
                bfloat(matrices),
                bfloat((stretch + rows, width)),
                bfloat((stretch + rows, width)),
                bfloat((wanted, rows, width)),
                pltpu.VMEM((rows, width), jnp.float32),
                bfloat((5, count * rows, width)),
                bfloat((wanted, rows, width)),
                pltpu.SemaphoreType.DMA((count + 7 + wanted,)),
            ]
            + [bfloat(matrices)] * begun,
        ),
        out_shape=[jax.ShapeDtypeStruct((rows, width), jnp.bfloat16)] * wanted
        + [jax.ShapeDtypeStruct(state.shape, state.dtype)] * begun,
        input_output_aliases={1 + count + len(before): wanted} if begun else {},
        compiler_params=pltpu.CompilerParams(vmem_limit_bytes=VMEM_LIMIT),
        cost_estimate=pl.CostEstimate(flops=scale * stretch * width * width, bytes_accessed=scale * stretch * width, transcendentals=0),
        name="stage",
    )(table, *operands, rate, initial)


def banded(queries, keys, values, floor):
    part, window = queries.shape[0], keys.shape[0]
    row = lax.broadcasted_iota(jnp.int32, (part, window), 0)
    column = lax.broadcasted_iota(jnp.int32, (part, window), 1)
    band = (column > row) & (column <= row + window - part) & (column >= floor)
    scores = matmul_nt(queries, keys) * (queries.shape[1] ** -0.5)
    scores = jnp.where(band, scores, -1e30)
    raised = jnp.exp(scores - jnp.max(scores, axis=1, keepdims=True))
    total = jnp.sum(raised, axis=1, keepdims=True)
    return matmul(raised.astype(jnp.bfloat16), values) / total


def finish_kernel(befores, table, *refs):
    before, refs = refs[:befores], refs[befores:]
    maps, state, result, x, m, w, q, k, v, attended, out, sems = refs
    rows, width = x.shape
    part = rows // 2
    there = table[0] > 0
    for at in range(befores):
        fetch(before[at], x, sems.at[0], there & (table[1] == at))
    fetch(maps, m, sems.at[1], there)
    fetch(state.at[3], q, sems.at[2])
    fetch(state.at[4], k.at[pl.ds(rows, rows)], sems.at[3])
    fetch(state.at[6], v.at[pl.ds(rows, rows)], sems.at[4])
    fetch(state.at[pl.ds(11, 3)], w, sems.at[5])

    @pl.when(there)
    def _():
        fetched(x, sems.at[0])
        fetched(m, sems.at[1])
        k[:rows] = matmul(x[...], m[:, width : 2 * width]).astype(jnp.bfloat16)
        v[:rows] = matmul(x[...], m[:, 2 * width :]).astype(jnp.bfloat16)

    @pl.when(jnp.logical_not(there))
    def _():
        k[:rows] = jnp.zeros((rows, width), jnp.bfloat16)
        v[:rows] = jnp.zeros((rows, width), jnp.bfloat16)

    fetched(q, sems.at[2])
    fetched(q, sems.at[3])
    fetched(q, sems.at[4])

    @pl.loop(0, 2)
    def _(half):
        first = part * half
        window = pl.ds(first, rows + part)
        floor = jnp.where(there, 0, rows - first)
        attended[pl.ds(first, part)] = banded(q[pl.ds(first, part)], k[window], v[window], floor)

    fetched(w, sems.at[5])
    queries = unit_rows(q[...])
    gate = matmul(queries, w[0])
    up = matmul(queries, w[1])
    inner = (gate * logistic(gate) * up).astype(jnp.bfloat16)
    fast = matmul(inner, w[2]).astype(jnp.bfloat16).astype(jnp.float32)
    out[...] = (attended[...] + fast).astype(jnp.bfloat16)
    copy = pltpu.make_async_copy(out, result, sems.at[0])
    copy.start()
    copy.wait()


def finish(table, before, maps, state):
    rows, width = before[0].shape
    anywhere = pl.BlockSpec(memory_space=pl.ANY)
    bfloat = functools.partial(pltpu.VMEM, dtype=jnp.bfloat16)
    return pl.pallas_call(
        functools.partial(finish_kernel, len(before)),
        grid_spec=pltpu.PrefetchScalarGridSpec(
            num_scalar_prefetch=1,
            grid=(),
            in_specs=[anywhere] * (len(before) + 2),
            out_specs=anywhere,
            scratch_shapes=[
                bfloat((rows, width)),
                bfloat(maps.shape),
                bfloat((3,) + state.shape[1:]),
                bfloat((rows, width)),
                bfloat((2 * rows, width)),
                bfloat((2 * rows, width)),
                pltpu.VMEM((rows, width), jnp.float32),
                bfloat((rows, width)),
                pltpu.SemaphoreType.DMA((6,)),
            ],
        ),
        out_shape=jax.ShapeDtypeStruct((rows, width), jnp.bfloat16),
        compiler_params=pltpu.CompilerParams(vmem_limit_bytes=VMEM_LIMIT),
        cost_estimate=pl.CostEstimate(flops=1, bytes_accessed=1, transcendentals=0),
        name="finish",
    )(table, *before, maps, state)


def after(array, *others):
    return lax.optimization_barrier((array, *others))[0]


def head_body(tokens, qkv_maps, rate_map, fast_init):
    rows = tokens.shape[0]
    heads, width = qkv_maps.shape[:2]
    groups = lax.axis_size("tok")
    chips = groups // 2
    slots = chips // 2
    last = chips - 1
    me = lax.axis_index("tok")
    chip, core = me // 2, me % 2
    is_first = (chip < slots).astype(jnp.int32)

    def swap(block, bits):
        return lax.ppermute(block, "tok", [(i, i ^ bits) for i in range(groups)])

    def piece(slot, source, index):
        return lax.dynamic_slice_in_dim(source, (index ^ slot) * width, width, 1)

    maps = lax.dynamic_index_in_dim(qkv_maps, chip, 0, False)
    initial = lax.dynamic_index_in_dim(fast_init, chip, 0, False)
    same = {slot: swap(piece(slot, tokens, chip), 2 * slot) for slot in range(1, slots)}
    same[last] = swap(piece(last, tokens, chip), 2 * last)
    terms = lax.dot_general(
        rate_map, tokens, (((0,), (1,)), ((), ())), preferred_element_type=jnp.float32
    )
    terms = lax.all_to_all(jnp.repeat(terms, 2, axis=0), ("head", "tok"), 0, 0, tiled=True)
    logits = jnp.sum(terms.reshape(-1, groups, rows), 0)
    rate = (rate_base * jax.nn.softplus(logits)).astype(jnp.bfloat16).astype(jnp.float32)
    source = after(tokens, *(same[slot] for slot in range(1, slots)))
    for slot in range(slots, last):
        same[slot] = swap(piece(slot, source, chip), 2 * slot)
    same[0] = piece(0, source, chip)
    other = {slot: swap(same[slot], 1) for slot in range(slots)}

    def integers(entries):
        return jnp.stack([jnp.asarray(entry, jnp.int32) for entry in entries])

    def places(slot):
        return [2 * ((chip ^ slot) % slots) + core, 2 * ((chip ^ slot) % slots) + (1 - core)]

    def opening(slot):
        return 2 * slots * ((chip ^ slot) // slots)

    def table(slots_in, updates, answers, weights_at):
        first = opening(slots_in[0])
        before = (chip ^ (slots - 1)) % slots
        flags = [updates, answers, first, (first > 0) & (core == 0), before, weights_at]
        return integers(flags + [place for slot in slots_in for place in places(slot)])

    near_slots, far_slots = range(slots), range(slots, chips)
    near_blocks = [block for slot in near_slots for block in (same[slot], other[slot])]
    near_others = [other[slot] for slot in near_slots]
    shared = dict(maps=maps, rate=rate, initial=initial)
    other[last] = swap(same[last], 1)
    rates_in = [opening(slot) + place for slot in (*near_slots, last) for place in places(slot)]
    state = begin(integers([is_first] + rates_in), near_blocks, [same[last], other[last]], **shared)
    far_blocks = []
    for slot in far_slots[:-1]:
        same[slot] = after(same[slot], state)
        other[slot] = swap(same[slot], 1)
        far_blocks += [same[slot], other[slot]]
    *far_results, state = stage(
        table(far_slots, True, True, 0), far_blocks, near_others, state, begun=True, **shared
    )
    near_results = stage(
        table(near_slots, 1 - is_first, True, 11 * (1 - is_first)), near_blocks,
        [other[slot] for slot in far_slots], state, scale=0, **shared
    )
    at = chip ^ last
    place = jnp.where(core == 1, at, at - 1)
    last_result = finish(
        integers([place >= 0, chip ^ jnp.maximum(place, 0)]), [other[slot] for slot in range(chips)], maps, state
    )
    results = [*near_results, *far_results, last_result]
    combined = jnp.zeros_like(tokens)
    for slot in (*far_slots[:-1], 0, last, *range(1, slots)):
        result = swap(results[slot], 2 * slot) if slot else results[slot]
        combined = lax.dynamic_update_slice_in_dim(combined, result, (chip ^ slot) * width, 1)
    return combined


def body(tokens, qkv_maps, rate_map, fast_init):
    groups = lax.axis_size("tok")
    heads = qkv_maps.shape[0]
    powers = groups & (groups - 1) == 0 and groups > 2
    if powers and groups == 2 * heads and tokens.shape[0] == WINDOW:
        return head_body(tokens, qkv_maps, rate_map, fast_init)
    return general_body(tokens, qkv_maps, rate_map, fast_init)


def solution(mesh):
    in_specs = (
        P("tok", "head"),
        P("head", None, None),
        P("head", None),
        P("head", None, None, None),
    )
    out_specs = P("tok", "head")
    return jax.shard_map(body, mesh=mesh, in_specs=in_specs, out_specs=out_specs, check_vma=False)
```
